32 devices in a mesh: exp: 2 (over x), tx: 4 (over z), ty: 4 (over y, core).
Axes of the slice: x: 2, y: 2, z: 4, core: 2. Of those that a mesh axis runs over, the one named last changes fastest.
Arguments:
- exposures: bfloat16 [4, 512, 128, 128], P('ty', ('exp', 'tx')), may hold values from -8 to 8
- block_tile: int32 [4, 512, 1], P('ty', ('exp', 'tx')), may hold values from 0 to 3, as said below
- affine: int32 [4, 512, 2, 4], P('ty', ('exp', 'tx')), may hold values from -512 to 512
- col_mask: int32 [4, 512, 128], P('ty', ('exp', 'tx')), may hold values 0 or 1
- block_weight: float32 [4, 512], P('ty', ('exp', 'tx')), may hold values from 0.5 to 4
- psf: float32 [2, 2, 9], replicated, may hold values from 0.05 to 0.6
Outputs:
- gradients: float32 [4, 512, 2, 4], P('ty', ('exp', 'tx'))
- coadd: float32 [512, 512], P('tx', 'ty')
The draws below stay inside these ranges and needn't reach their ends.
Inputs may be any that keep to these rules, and one draw needn't show every extreme that they name: `block_tile`: each device's 64 blocks name any tile row at most 32 times, and some tile row exactly 32 times.
All inputs are finite; a program needn't handle non-finite values. No bound on the sum of `col_mask` on one device may be relied on, other than what follows from the above.
Results may differ from the reference program's by a relative error of at most 0.0026.
Values may be sent and summed in bfloat16 or wider, within the bound.
No kernel may reach another device: no remote copies, remote signals or barrier semaphores. Data moves between devices by JAX's collectives and lax.ppermute only.
A program may use at most 128 MiB of HBM per device.

```python
import math
import jax
import jax.numpy as jnp
from jax import lax

P_SIZE = 128
RAD = 4
ITERS = 2
E_DEV = 64
CAP = 32
BL = 512
NX = 512
NY = 512
N_EXP = 2
N_TX = 4
N_TY = 4


def assign_tiles(key):
    device_count = N_TY * N_EXP * N_TX
    device_keys = jax.random.split(jax.random.fold_in(key, 101), device_count)

    def device_rows(device_key):
        shuffle_key, order_key = jax.random.split(device_key)
        slot_total = N_TX * CAP
        shuffled = jax.random.permutation(shuffle_key, slot_total)
        placing = jnp.argsort(shuffled)
        forced_tile = shuffled[0] // CAP
        slot_ids = jnp.arange(slot_total, dtype=jnp.int32)
        priority = jnp.where(slot_ids // CAP == forced_tile, slot_ids - slot_total, placing)
        picked = jnp.argsort(priority, stable=True)[:E_DEV]
        picked = jax.random.permutation(order_key, picked)
        return (picked // CAP).astype(jnp.int32)
    tile_rows = jax.vmap(device_rows)(device_keys)
    return tile_rows.reshape(N_TY, N_EXP * N_TX * E_DEV)


def draw_block_tile(key, part):
    tile_rows = assign_tiles(key)
    return tile_rows[:, :, None]


def draw_exposures(key, part):
    tile_rows = assign_tiles(key)
    key = jax.random.fold_in(key, 7)
    sky_key, noise_key = jax.random.split(key)
    noise = jax.random.normal(noise_key, (N_TY, BL, P_SIZE, P_SIZE), jnp.float32)
    sky_field = jax.random.normal(sky_key, (N_TY, N_TX, P_SIZE, P_SIZE), jnp.float32)
    column_ids = jnp.arange(N_TY, dtype=jnp.int32)[:, None]
    placed = sky_field[column_ids, tile_rows]
    values = 0.8 * placed + 0.6 * noise
    return jnp.clip(values, -8.0, 8.0).astype(jnp.bfloat16)


def with_ends(entries, rng, smallest, high):
    shape = entries.shape
    spot = [jax.random.randint(jax.random.fold_in(rng, axis), (), 0, shape[axis]) for axis in range(len(shape))]
    entries = entries.at[tuple(spot)].set(smallest)
    longest = shape.index(max(shape))
    spot[longest] = (spot[longest] + 1) % shape[longest]
    return entries.at[tuple(spot)].set(high)


def levels(rng, extent, cuts, smallest, high):
    factor_of, own = 1.0, jax.random.fold_in(rng, 6)
    for axis_at, shards_of in cuts:
        steps = jnp.exp(jax.random.uniform(jax.random.fold_in(own, axis_at), (shards_of,), jnp.float32, smallest / len(cuts), high / len(cuts)))
        factor_of = factor_of * jnp.repeat(steps, extent[axis_at] // shards_of).reshape([-1 if axis == axis_at else 1 for axis in range(len(extent))])
    return factor_of


def setup_inputs(seed: int = 0) -> dict:
    streams_of = jax.random.split(jax.random.key(seed), 7)
    return {
        "exposures": draw_exposures(jax.random.fold_in(streams_of[6], 71), 0),
        "block_tile": draw_block_tile(jax.random.fold_in(streams_of[6], 71), 0),
        "affine": with_ends(jax.random.randint(streams_of[2], (N_TY, BL, ITERS, 4), -512, 513), jax.random.fold_in(streams_of[2], 1), -512, 512).astype(jnp.int32),
        "col_mask": with_ends((jax.random.randint(streams_of[3], (N_TY, BL, P_SIZE), 0, 8) < 7).astype(jnp.int32), jax.random.fold_in(streams_of[3], 1), 0, 1),
        "block_weight": jnp.clip(jnp.exp(math.log(4.0) - 2.0794415 * jax.random.uniform(streams_of[4], (N_TY, BL), jnp.float32) ** levels(streams_of[4], (N_TY, BL), ((0, 4), (1, 8)), -0.2, 0.2)), 0.5, 4.0),
        "psf": jnp.clip(jnp.exp(jax.random.uniform(streams_of[5], (ITERS, 2, 2 * RAD + 1), jnp.float32, math.log(0.05), math.log(0.6))), 0.05, 0.6),
    }


def lanczos(offsets):
    inside = jnp.abs(offsets) < 3.0
    return jnp.where(inside, jnp.sinc(offsets) * jnp.sinc(offsets / 3.0), 0.0)


def band_pair(shift, stretch, block_side):
    positions = jnp.arange(block_side, dtype=jnp.float32)
    centre = (block_side - 1) / 2.0
    source = centre + (1.0 + stretch) * (positions - centre) + shift
    offsets = source[:, None] - positions[None, :]
    values, slopes = jax.jvp(lanczos, (offsets,), (jnp.ones_like(offsets),))
    return values.astype(jnp.bfloat16), slopes.astype(jnp.bfloat16)


def warp_block(block, column_mask, affine_terms, weight):
    block_side = block.shape[0]
    scaled = affine_terms.astype(jnp.float32)
    row_band, row_slope = band_pair(scaled[1] / 256.0, scaled[3] / 51200.0, block_side)
    col_band, col_slope = band_pair(scaled[0] / 256.0, scaled[2] / 51200.0, block_side)
    mask_row = column_mask.astype(jnp.bfloat16)
    masked = block * mask_row[None, :]
    row_pass = jnp.dot(row_band, masked, preferred_element_type=jnp.float32).astype(jnp.bfloat16)
    col_pass = jnp.dot(masked, col_band.T, preferred_element_type=jnp.float32).astype(jnp.bfloat16)
    warped = jnp.dot(row_pass, col_band.T, preferred_element_type=jnp.float32)
    slope_x = jnp.dot(row_pass, col_slope.T, preferred_element_type=jnp.float32)
    slope_y = jnp.dot(row_slope, col_pass, preferred_element_type=jnp.float32)
    rows_sum = jnp.sum(row_band.astype(jnp.float32), axis=1)
    cols_sum = jnp.dot(col_band, mask_row, preferred_element_type=jnp.float32)
    sent = (weight * warped).astype(jnp.bfloat16)
    profile = jnp.stack([(weight * rows_sum).astype(jnp.bfloat16), cols_sum.astype(jnp.bfloat16)])
    return sent, profile, warped, slope_x, slope_y, rows_sum, cols_sum


def gradient_terms(warped, slope_x, slope_y, rows_sum, cols_sum, cutout):
    block_side = warped.shape[0]
    centre = (block_side - 1) / 2.0
    coords = (jnp.arange(block_side, dtype=jnp.float32) - centre) / block_side
    residual = (warped - cutout.astype(jnp.float32)) * jax.nn.relu(rows_sum[:, None] * cols_sum[None, :])
    first = jnp.sum(residual * slope_x) / block_side
    second = jnp.sum(residual * slope_y) / block_side
    third = jnp.sum(residual * slope_x * coords[None, :]) / block_side
    fourth = jnp.sum(residual * slope_y * coords[:, None]) / block_side
    return jnp.stack([first, second, third, fourth])


def convolve(padded, psf_taps, rows_out, cols_out):
    row_smoothed = psf_taps[0, 0] * padded[0:rows_out, :]
    for offset_index in range(1, psf_taps.shape[1]):
        row_smoothed = row_smoothed + psf_taps[0, offset_index] * padded[offset_index:offset_index + rows_out, :]
    smoothed = psf_taps[1, 0] * row_smoothed[:, 0:cols_out]
    for offset_index in range(1, psf_taps.shape[1]):
        smoothed = smoothed + psf_taps[1, offset_index] * row_smoothed[:, offset_index:offset_index + cols_out]
    return smoothed


def to_sky(tile_stack):
    return tile_stack.reshape(N_TY, N_TX, P_SIZE, P_SIZE).transpose(1, 2, 0, 3).reshape(N_TX * P_SIZE, N_TY * P_SIZE)


def from_sky(sky_field):
    return sky_field.reshape(N_TX, P_SIZE, N_TY, P_SIZE).transpose(2, 0, 1, 3).reshape(N_TY * N_TX, P_SIZE, P_SIZE)


def reference(exposures, block_tile, affine, col_mask, block_weight, psf):
    batches = N_TY * BL // E_DEV
    block_batches = exposures.reshape(batches, E_DEV, P_SIZE, P_SIZE)
    column_ids = jnp.arange(N_TY, dtype=jnp.int32)[:, None] * N_TX
    tile_ids = (column_ids + block_tile[:, :, 0]).astype(jnp.int32).reshape(batches, E_DEV)
    pixel_masks = col_mask.reshape(batches, E_DEV, P_SIZE)
    weights = block_weight.reshape(batches, E_DEV)
    all_terms = affine.reshape(batches, E_DEV, ITERS, 4)
    tile_total = N_TY * N_TX
    coadd_tiles = jnp.zeros((tile_total, P_SIZE, P_SIZE), jnp.float32)
    gradient_list = []
    for iteration in range(ITERS):
        affine_terms = all_terms[:, :, iteration, :]

        def accumulate(totals, batch_items):
            numerator, denominator = totals
            blocks, masks_now, terms_now, weights_now, tiles_now = batch_items
            outputs = jax.vmap(warp_block)(blocks, masks_now, terms_now, weights_now)
            sent, profile = outputs[0], outputs[1]
            rows_part = profile[:, 0, :].astype(jnp.float32)
            cols_part = profile[:, 1, :].astype(jnp.float32)
            weight_map = jax.nn.relu(rows_part[:, :, None] * cols_part[:, None, :])
            numerator = numerator.at[tiles_now].add(sent.astype(jnp.float32))
            denominator = denominator.at[tiles_now].add(weight_map)
            return (numerator, denominator), None

        empty = jnp.zeros((tile_total, P_SIZE, P_SIZE), jnp.float32)
        (numerator, denominator), _ = lax.scan(accumulate, (empty, empty), (block_batches, pixel_masks, affine_terms, weights, tile_ids))
        coadd_tiles = (numerator + coadd_tiles) / (1.0 + denominator)
        padded = jnp.pad(to_sky(coadd_tiles), RAD)
        model_tiles = from_sky(convolve(padded, psf[iteration], NX, NY)).astype(jnp.bfloat16)

        def compare(totals, batch_items):
            blocks, masks_now, terms_now, weights_now, tiles_now = batch_items
            outputs = jax.vmap(warp_block)(blocks, masks_now, terms_now, weights_now)
            cutouts = model_tiles[tiles_now]
            found = jax.vmap(gradient_terms)(outputs[2], outputs[3], outputs[4], outputs[5], outputs[6], cutouts)
            return totals, found

        _, found = lax.scan(compare, jnp.zeros((), jnp.float32), (block_batches, pixel_masks, affine_terms, weights, tile_ids))
        gradient_list.append(found.reshape(N_TY, BL, 4))
    gradients = jnp.stack(gradient_list, axis=2)
    return gradients, to_sky(coadd_tiles)
```

```python
import functools

import jax
import jax.numpy as jnp
import numpy as np
from jax import lax
from jax.experimental import pallas as pl
from jax.experimental.pallas import tpu as pltpu
from jax.sharding import PartitionSpec as P

RAD = 4
TAPS = 2 * RAD + 1
DEGREE = 10
F32 = jnp.float32
BF16 = jnp.bfloat16
VMEM_BYTES = 40 * 1024 * 1024


def series():
    count = 64
    nodes = np.cos(np.pi * (np.arange(count) + 0.5) / count)
    table = np.zeros((2, DEGREE + 1, 8), np.float64)
    for row in range(1, 7):
        d = nodes * 0.5 + 0.5 - (row - 3)
        a, b = np.sinc(d), np.sinc(d / 3.0)
        da = (np.cos(np.pi * d) - a) / d
        db = (np.cos(np.pi * d / 3.0) - b) / d
        for which, values in enumerate((a * b, da * b + a * db)):
            fit = np.polynomial.chebyshev.Chebyshev.fit(nodes * 0.5, values, DEGREE, domain=[-0.5, 0.5])
            table[which, :, row] = fit.convert(kind=np.polynomial.Polynomial).coef
    return np.repeat(table.reshape(2 * (DEGREE + 1), 8, 1), 128, axis=2).astype(np.float32)


def taps_of(shift_code, stretch_code, coef_ref, slopes):
    side = 128
    centre = (side - 1) / 2.0
    lane = lax.broadcasted_iota(jnp.int32, (8, side), 1).astype(F32)
    shift = jnp.full((8, side), shift_code, jnp.int32).astype(F32) * (1.0 / 256.0)
    stretch = jnp.full((8, side), stretch_code, jnp.int32).astype(F32) * (1.0 / 51200.0)
    source = centre + (1.0 + stretch) * (lane - centre) + shift
    whole = jnp.floor(source)
    v = (source - whole) - 0.5
    found = []
    for which in range(2 if slopes else 1):
        base = which * (DEGREE + 1)
        total = coef_ref[base + DEGREE]
        for power in range(DEGREE - 1, -1, -1):
            total = total * v + coef_ref[base + power]
        found.append(total)
    return found, whole.astype(jnp.int32)


def spread(tap_list, whole):
    side = 128
    base = lax.broadcasted_iota(jnp.int32, (8, side), 0) + 3 - whole
    indices = [jnp.clip(base + 8 * v, 0, 7) for v in range(side // 8)]
    return [
        jnp.concatenate([jnp.take_along_axis(taps, index, axis=0) for index in indices], axis=0).astype(BF16)
        for taps in tap_list
    ]


def dot(a, b):
    return jnp.dot(a, b, preferred_element_type=F32)


def dot_t(a, b):
    return lax.dot_general(a, b, (((0,), (0,)), ((), ())), preferred_element_type=F32)


def mask_rows(mask_row):
    side = mask_row.shape[1]
    first = lax.broadcasted_iota(jnp.int32, (16, side), 0) == 0
    return jnp.where(first, jnp.broadcast_to(mask_row, (16, side)), 0.0).astype(BF16)


def sums_kernel(tiles, halves, step_blocks, place_ref, tile_ref, affine_ref, weight_ref, coef_ref, mask_ref, block_ref, *rest):
    outs = rest[: tiles * halves]
    acc, rows_sc, cols_sc, den_sc = rest[tiles * halves :]
    step = pl.program_id(0)
    side = 128

    @pl.when(step == 0)
    def _():
        acc[...] = jnp.zeros_like(acc)
        rows_sc[...] = jnp.zeros_like(rows_sc)

    def body(j, carry):
        b = step * step_blocks + j
        tile = tile_ref[0, b]
        weight = weight_ref[0, b]
        mask_row = mask_ref[pl.ds(b, 1), :].astype(F32)
        masked = block_ref[j] * mask_row.astype(BF16)
        extra = mask_rows(mask_row)
        for k in range(2):
            (tap_y,), whole_y = taps_of(affine_ref[b, 4 * k + 1], affine_ref[b, 4 * k + 3], coef_ref, False)
            (tap_x,), whole_x = taps_of(affine_ref[b, 4 * k], affine_ref[b, 4 * k + 2], coef_ref, False)
            (ly_t,) = spread([tap_y], whole_y)
            (lx_t,) = spread([tap_x], whole_x)
            row_pass = dot_t(ly_t, masked).astype(BF16)
            both = dot(jnp.concatenate([row_pass, extra], axis=0), lx_t)
            sent = (weight * both[:side]).astype(BF16).astype(F32)
            acc[k, tile] = acc[k, tile] + sent
            at = whole_y + lax.broadcasted_iota(jnp.int32, (8, side), 0) - 3
            used = jnp.where((at >= 0) & (at < side), tap_y.astype(BF16).astype(F32), 0.0)
            rows_sum = jnp.sum(used, axis=0, keepdims=True)
            rows_sc[k, tile, pl.ds(b, 1), :] = (weight * rows_sum).astype(BF16).astype(F32)
            cols_sc[k, pl.ds(b, 1), :] = both[side : side + 1].astype(BF16).astype(F32)
        return carry

    lax.fori_loop(0, step_blocks, body, 0)

    @pl.when(step == pl.num_programs(0) - 1)
    def _():
        for k in range(2):
            cols = cols_sc[k]
            cols = jnp.concatenate([jnp.maximum(cols, 0.0), jnp.maximum(-cols, 0.0)], axis=0).astype(BF16)

            def one(t, carry, k=k, cols=cols):
                rows = rows_sc[k, t]
                rows = jnp.concatenate([jnp.maximum(rows, 0.0), jnp.maximum(-rows, 0.0)], axis=0).astype(BF16)
                den_sc[k, t] = dot_t(rows, cols)
                return carry

            lax.fori_loop(0, tiles, one, 0)
        height = side // halves
        for de in range(halves):
            for dz in range(tiles):
                half = lax.rem(place_ref[0] + de, halves)
                tile = lax.rem(place_ref[1] + dz, tiles)
                out = outs[de * tiles + dz]
                rows = pl.ds(pl.multiple_of(half * height, height), height)
                for k in range(2):
                    out[k] = acc[k, tile, rows, :].astype(BF16)
                    out[2 + k] = den_sc[k, tile, rows, :].astype(BF16)


def vmem():
    return pl.BlockSpec(memory_space=pltpu.VMEM)


def smem():
    return pl.BlockSpec(memory_space=pltpu.SMEM)


def tile_sums(place, target, affine, weights, coef, masks, blocks, tiles, halves):
    count, side = blocks.shape[0], blocks.shape[1]
    step_blocks = 8
    height = side // halves
    pieces = tiles * halves
    return pl.pallas_call(
        functools.partial(sums_kernel, tiles, halves, step_blocks),
        grid=(count // step_blocks,),
        out_shape=[jax.ShapeDtypeStruct((4, height, side), BF16)] * pieces,
        in_specs=[
            smem(), smem(), smem(), smem(), vmem(), vmem(),
            pl.BlockSpec((step_blocks, side, side), lambda i: (i, 0, 0)),
        ],
        out_specs=[pl.BlockSpec((4, height, side), lambda i: (0, 0, 0))] * pieces,
        scratch_shapes=[
            pltpu.VMEM((2, tiles, side, side), F32),
            pltpu.VMEM((2, tiles, count, side), F32),
            pltpu.VMEM((2, count, side), F32),
            pltpu.VMEM((2, tiles, side, side), F32),
        ],
        compiler_params=pltpu.CompilerParams(vmem_limit_bytes=VMEM_BYTES),
        cost_estimate=pl.CostEstimate(flops=int(2e9), bytes_accessed=int(3e6), transcendentals=0),
        name="tile_sums",
    )(place, target, affine, weights, coef, masks, blocks)


def moments(product_x, product_y):
    side = product_x.shape[0]
    centre = (side - 1) / 2.0
    sum_x = product_x[side - 8 : side]
    sum_y = product_y[side - 8 : side]
    later = sum_y
    for v in range(side // 8 - 2, -1, -1):
        sum_x = sum_x + product_x[8 * v : 8 * v + 8]
        sum_y = sum_y + product_y[8 * v : 8 * v + 8]
        if v:
            later = later + sum_y
    sub = lax.broadcasted_iota(jnp.int32, (8, side), 0).astype(F32) - centre
    lane = lax.broadcasted_iota(jnp.int32, (1, side), 1).astype(F32) - centre
    tilted_y = 8.0 * later + sub * sum_y
    first = jnp.sum(sum_x, axis=0, keepdims=True)
    second = jnp.sum(sum_y, axis=0, keepdims=True)
    fourth = jnp.sum(tilted_y, axis=0, keepdims=True)
    return [first, second, first * lane * (1.0 / side), fourth * (1.0 / side)]


def slopes_kernel(step_blocks, affine_ref, coef_ref, mask_ref, block_ref, slope_ref, part_ref):
    step = pl.program_id(0)
    side = 128

    def body(j, carry):
        b = step * step_blocks + j
        mask_row = mask_ref[pl.ds(b, 1), :].astype(F32)
        masked = block_ref[j] * mask_row.astype(BF16)
        extra = mask_rows(mask_row)
        with_ones = jnp.concatenate([masked, jnp.ones((side, side), BF16)], axis=1)
        bands = []
        for k in range(2):
            taps_y, whole_y = taps_of(affine_ref[b, 4 * k + 1], affine_ref[b, 4 * k + 3], coef_ref, True)
            taps_x, whole_x = taps_of(affine_ref[b, 4 * k], affine_ref[b, 4 * k + 2], coef_ref, True)
            bands.append(spread(taps_y, whole_y) + spread(taps_x, whole_x))
        col_both = dot(jnp.concatenate([masked, extra], axis=0), jnp.concatenate([bands[0][2], bands[1][2]], axis=1))
        for k in range(2):
            ly_t, dy_t, lx_t, dx_t = bands[k]
            row_both = dot_t(ly_t, with_ones)
            row_pass = row_both[:, :side].astype(BF16)
            rows_sum = row_both[:, side:]
            col_pass = col_both[:side, k * side : (k + 1) * side].astype(BF16)
            cols_sum = col_both[side : side + 1, k * side : (k + 1) * side]
            both = dot(row_pass, jnp.concatenate([lx_t, dx_t], axis=1))
            warped = both[:, :side]
            slope_y = dot_t(dy_t, col_pass)
            weight_map = jnp.maximum(rows_sum * cols_sum, 0.0)
            value_x = weight_map * both[:, side:]
            value_y = weight_map * slope_y
            slope_ref[j, 2 * k] = value_x
            slope_ref[j, 2 * k + 1] = value_y
            for m, row in enumerate(moments(warped * value_x, warped * value_y)):
                part_ref[j, 4 * k + m : 4 * k + m + 1, :] = row
        return carry

    lax.fori_loop(0, step_blocks, body, 0)


def slopes_of(affine, coef, masks, blocks):
    count, side = blocks.shape[0], blocks.shape[1]
    step_blocks = 4
    return pl.pallas_call(
        functools.partial(slopes_kernel, step_blocks),
        grid=(count // step_blocks,),
        out_shape=[
            jax.ShapeDtypeStruct((count, 4, side, side), F32),
            jax.ShapeDtypeStruct((count, 8, side), F32),
        ],
        in_specs=[smem(), vmem(), vmem(), pl.BlockSpec((step_blocks, side, side), lambda i: (i, 0, 0))],
        out_specs=[
            pl.BlockSpec((step_blocks, 4, side, side), lambda i: (i, 0, 0, 0)),
            pl.BlockSpec((step_blocks, 8, side), lambda i: (i, 0, 0)),
        ],
        compiler_params=pltpu.CompilerParams(vmem_limit_bytes=VMEM_BYTES),
        cost_estimate=pl.CostEstimate(flops=int(8e9), bytes_accessed=int(20e6), transcendentals=0),
        name="slopes",
    )(affine, coef, masks, blocks)


def coadd_kernel(count, *refs):
    parts, (piece_ref, first_ref, last_ref) = refs[:count], refs[count:]
    total = parts[0][...].astype(F32)
    for part in parts[1:]:
        total = total + part[...].astype(F32)
    one = total[0] / (1.0 + total[2])
    two = (total[1] + one) / (1.0 + total[3])
    piece_ref[0] = one
    piece_ref[1] = two
    side = one.shape[1]
    flipped = [jnp.transpose(one), jnp.transpose(two)]
    first_ref[...] = jnp.concatenate([f[0:8] for f in flipped], axis=0).astype(BF16)
    last_ref[...] = jnp.concatenate([f[side - 8 : side] for f in flipped], axis=0).astype(BF16)


def coadd_of(parts):
    height, side = parts[0].shape[1:]
    return pl.pallas_call(
        functools.partial(coadd_kernel, len(parts)),
        out_shape=[
            jax.ShapeDtypeStruct((2, height, side), F32),
            jax.ShapeDtypeStruct((16, height), BF16),
            jax.ShapeDtypeStruct((16, height), BF16),
        ],
        name="coadd",
    )(*parts)


def join_kernel(place_ref, own_ref, other_ref, left_own, left_other, right_own, right_other, sky_ref, tile_ref):
    here = place_ref[0] == 0
    side = own_ref.shape[2]
    for k in range(2):
        own, other = own_ref[k], other_ref[k]
        tile = jnp.concatenate([jnp.where(here, own, other), jnp.where(here, other, own)], axis=0)
        sky_ref[k, 0:side, :] = tile.astype(BF16)
        if k == 1:
            tile_ref[...] = tile
        edges = []
        for mine, theirs in ((left_own, left_other), (right_own, right_other)):
            a = mine[8 * k : 8 * k + 8, :].astype(F32)
            c = theirs[8 * k : 8 * k + 8, :].astype(F32)
            edges.append(jnp.concatenate([jnp.where(here, a, c), jnp.where(here, c, a)], axis=1))
        sky_ref[k, side : side + 16, :] = jnp.concatenate(edges, axis=0).astype(BF16)


def join(place, own, other, edges):
    side = own.shape[2]
    return pl.pallas_call(
        join_kernel,
        out_shape=[jax.ShapeDtypeStruct((2, side + 16, side), BF16), jax.ShapeDtypeStruct((side, side), F32)],
        in_specs=[smem()] + [vmem()] * 6,
        out_specs=[vmem(), vmem()],
        name="join",
    )(place, own, other, *edges)


def band_of(values, diagonal):
    total = jnp.zeros(diagonal.shape, F32)
    for q, value in enumerate(values):
        total = jnp.where(diagonal == q, value, total)
    high = total.astype(BF16)
    return jnp.concatenate([high, (total - high.astype(F32)).astype(BF16)], axis=1)


def gradient_kernel(tiles, step_blocks, place_ref, tile_ref, psf_ref, *rest):
    skies = rest[:tiles]
    slope_ref, part_ref, out_ref, smooth, model = rest[tiles:]
    step = pl.program_id(0)
    side = 128

    @pl.when(step == 0)
    def _():
        along = lax.broadcasted_iota(jnp.int32, (side, side), 0)
        across = lax.broadcasted_iota(jnp.int32, (side, side), 1)
        edge = lax.broadcasted_iota(jnp.int32, (16, side), 0)
        edge = jnp.where(edge < 8, edge - 8, edge + side - 8)
        for k in range(2):
            taps = [psf_ref[k, 1, q] for q in range(TAPS)]
            inner = band_of(taps, along - across + RAD)
            outer = band_of(taps, edge - across[:16] + RAD)
            smooth[k, 0:8, :] = jnp.zeros((8, side), F32)
            smooth[k, 8 + tiles * side : 16 + tiles * side, :] = jnp.zeros((8, side), F32)
            for turn in range(tiles):
                tile = lax.rem(place_ref[1] + tiles - turn, tiles)
                both = dot(skies[turn][k, 0:side, :], inner) + dot_t(skies[turn][k, side : side + 16, :], outer)
                smooth[k, pl.ds(pl.multiple_of(8 + tile * side, 8), side), :] = both[:, :side] + both[:, side:]
            chunk = 64

            def rows(c, carry, k=k):
                start = pl.multiple_of(c * chunk, chunk)
                seen = smooth[k, pl.ds(start, chunk + 16), :]
                total = psf_ref[k, 0, 0] * seen[4 : 4 + chunk]
                for p in range(1, TAPS):
                    total = total + psf_ref[k, 0, p] * seen[4 + p : 4 + p + chunk]
                model[k, pl.ds(start, chunk), :] = total.astype(BF16).astype(F32)
                return carry

            lax.fori_loop(0, tiles * side // chunk, rows, 0)

    def body(j, carry):
        b = step * step_blocks + j
        start = pl.multiple_of(tile_ref[0, b] * side, side)
        for k in range(2):
            cutout = model[k, pl.ds(start, side), :]
            rows = moments(cutout * slope_ref[j, 2 * k], cutout * slope_ref[j, 2 * k + 1])
            for m, row in enumerate(rows):
                out_ref[j, 4 * k + m : 4 * k + m + 1, :] = part_ref[j, 4 * k + m : 4 * k + m + 1, :] - row
        return carry

    lax.fori_loop(0, step_blocks, body, 0)


def gradients_of(place, target, psf, skies, slopes, parts):
    count, _, side, _ = slopes.shape
    tiles = len(skies)
    step_blocks = 4
    return pl.pallas_call(
        functools.partial(gradient_kernel, tiles, step_blocks),
        grid=(count // step_blocks,),
        out_shape=jax.ShapeDtypeStruct((count, 8, side), F32),
        in_specs=[smem(), smem(), smem()]
        + [vmem()] * tiles
        + [
            pl.BlockSpec((step_blocks, 4, side, side), lambda i: (i, 0, 0, 0)),
            pl.BlockSpec((step_blocks, 8, side), lambda i: (i, 0, 0)),
        ],
        out_specs=pl.BlockSpec((step_blocks, 8, side), lambda i: (i, 0, 0)),
        scratch_shapes=[
            pltpu.VMEM((2, tiles * side + 16, side), F32),
            pltpu.VMEM((2, tiles * side, side), F32),
        ],
        compiler_params=pltpu.CompilerParams(vmem_limit_bytes=VMEM_BYTES),
        cost_estimate=pl.CostEstimate(flops=int(1e9), bytes_accessed=int(20e6), transcendentals=0),
        name="gradients",
    )(place, target, psf, *skies, slopes, parts)


def to_owners(pieces, tiles, halves):
    got = [pieces[0]]
    for index in range(1, tiles * halves):
        de, dz = divmod(index, tiles)
        perm = [(e * tiles + z, (e + de) % halves * tiles + (z + dz) % tiles) for e in range(halves) for z in range(tiles)]
        got.append(lax.ppermute(pieces[index], ("exp", "tx"), perm))
    return got


def sides_of(first, last, halves, columns):
    found = []
    for cells, turn in ((last, 1), (first, -1)):
        for flip in range(halves):
            perm = [
                (e * columns + y, (e + flip) % halves * columns + y + turn)
                for e in range(halves)
                for y in range(columns)
                if 0 <= y + turn < columns
            ]
            found.append(lax.ppermute(cells, ("exp", "ty"), perm))
    return found


def local(exposures, block_tile, affine, col_mask, block_weight, psf):
    blocks = exposures[0]
    count, side = blocks.shape[0], blocks.shape[1]
    tiles, halves, columns = lax.axis_size("tx"), lax.axis_size("exp"), lax.axis_size("ty")
    coef = jnp.asarray(series())
    place = jnp.stack([lax.axis_index("exp"), lax.axis_index("tx")]).astype(jnp.int32)
    target = block_tile.reshape(1, count)
    terms = affine.reshape(count, 8)
    masks = col_mask[0]
    small = halves == 2 and tiles <= 4
    pieces = tile_sums(place, target, terms, block_weight, coef, masks, blocks, tiles, halves if small else 1)
    if small:
        got = to_owners(pieces, tiles, halves)
        slopes, parts = slopes_of(terms, coef, masks, blocks)
        piece, first, last = coadd_of(got)
        other = lax.ppermute(piece, "exp", [(0, 1), (1, 0)])
        edges = sides_of(first, last, halves, columns)
        sky, coadd_tile = join(place, piece, other, edges)
        skies = [sky] + [
            lax.ppermute(sky, "tx", [(z, (z + dz) % tiles) for z in range(tiles)]) for dz in range(1, tiles)
        ]
    else:
        zero = jnp.zeros((), jnp.int32)
        me = lax.axis_index("tx")
        order = (jnp.arange(tiles, dtype=jnp.int32) - me) % tiles
        summed = lax.psum_scatter(jnp.take(jnp.stack(pieces), order, axis=0).astype(F32), "tx", scatter_dimension=0, tiled=True)
        summed = lax.psum(summed[0], "exp")
        one = summed[0] / (1.0 + summed[2])
        coadd_tile = (summed[1] + one) / (1.0 + summed[3])
        both = jnp.stack([one, coadd_tile])
        flipped = jnp.swapaxes(both, 1, 2).astype(BF16)
        left = lax.ppermute(flipped[:, side - 8 :], "ty", [(y, y + 1) for y in range(columns - 1)])
        right = lax.ppermute(flipped[:, :8], "ty", [(y + 1, y) for y in range(columns - 1)])
        sky = jnp.concatenate([both.astype(BF16), left, right], axis=1)
        gathered = lax.all_gather(sky, "tx", axis=0)
        slopes, parts = slopes_of(terms, coef, masks, blocks)
        skies = [lax.dynamic_index_in_dim(gathered, (me + tiles - turn) % tiles, 0, False) for turn in range(tiles)]
    rows = gradients_of(place, target, psf, skies, slopes, parts)
    gradients = (jnp.sum(rows, axis=2) / side).reshape(1, count, 2, 4)
    return gradients, coadd_tile


def solution(mesh):
    placed = (
        P("ty", ("exp", "tx"), None, None),
        P("ty", ("exp", "tx"), None),
        P("ty", ("exp", "tx"), None, None),
        P("ty", ("exp", "tx"), None),
        P("ty", ("exp", "tx")),
        P(),
    )
    return jax.shard_map(
        local,
        mesh=mesh,
        in_specs=placed,
        out_specs=(P("ty", ("exp", "tx"), None, None), P("tx", "ty")),
        check_vma=False,
    )
```

```python
import functools

import jax
import jax.numpy as jnp
import numpy as np
from jax import lax
from jax.experimental import pallas as pl
from jax.experimental.pallas import tpu as pltpu
from jax.sharding import PartitionSpec as P

RAD = 4
TAPS = 2 * RAD + 1
DEGREE = 10
F32 = jnp.float32
BF16 = jnp.bfloat16
GROUP1 = 8
GROUP2 = 4
GROUP3 = 4
CHUNKS = 4
SLOPE = jnp.float32
CODE_TILE, CODE_EXP, CODE_ROW = 8, 9, 10
VMEM_BYTES = 56 * 1024 * 1024


def series():
    count = 64
    nodes = np.cos(np.pi * (np.arange(count) + 0.5) / count)
    table = np.zeros((2, DEGREE + 1, 8), np.float64)
    for row in range(1, 7):
        d = nodes * 0.5 + 0.5 - (row - 3)
        a, b = np.sinc(d), np.sinc(d / 3.0)
        da = (np.cos(np.pi * d) - a) / d
        db = (np.cos(np.pi * d / 3.0) - b) / d
        for which, values in enumerate((a * b, da * b + a * db)):
            fit = np.polynomial.chebyshev.Chebyshev.fit(nodes * 0.5, values, DEGREE, domain=[-0.5, 0.5])
            table[which, :, row] = fit.convert(kind=np.polynomial.Polynomial).coef
    return np.repeat(table.reshape(2 * (DEGREE + 1), 8, 1), 128, axis=2).astype(np.float32)


def taps_of(shift_code, stretch_code, coef_ref, slopes):
    side = 128
    centre = (side - 1) / 2.0
    lane = lax.broadcasted_iota(jnp.int32, (8, side), 1).astype(F32)
    shift = jnp.full((8, side), shift_code, jnp.int32).astype(F32) * (1.0 / 256.0)
    stretch = jnp.full((8, side), stretch_code, jnp.int32).astype(F32) * (1.0 / 51200.0)
    source = centre + (1.0 + stretch) * (lane - centre) + shift
    whole = jnp.floor(source)
    v = (source - whole) - 0.5
    found = []
    for which in range(2 if slopes else 1):
        base = which * (DEGREE + 1)
        total = coef_ref[base + DEGREE]
        for power in range(DEGREE - 1, -1, -1):
            total = total * v + coef_ref[base + power]
        found.append(total)
    return found, whole.astype(jnp.int32)


def pick(taps, index):
    numbers = lax.GatherDimensionNumbers(
        offset_dims=(),
        collapsed_slice_dims=(0,),
        start_index_map=(0,),
        operand_batching_dims=(1,),
        start_indices_batching_dims=(1,),
    )
    mode = lax.GatherScatterMode.PROMISE_IN_BOUNDS
    return lax.gather(taps, index[..., None], numbers, slice_sizes=(1, 1), mode=mode)


def spread(tap_list, whole):
    side = 128
    base = lax.broadcasted_iota(jnp.int32, (8, side), 0) + 3 - whole
    indices = [jnp.clip(base + 8 * v, 0, 7) for v in range(side // 8)]
    return [
        jnp.concatenate([pick(taps, index) for index in indices], axis=0).astype(BF16)
        for taps in tap_list
    ]


def dot(a, b):
    return jnp.dot(a, b, preferred_element_type=F32)


def dot_t(a, b):
    return lax.dot_general(a, b, (((0,), (0,)), ((), ())), preferred_element_type=F32)


def mask_rows(mask_row):
    side = mask_row.shape[1]
    first = lax.broadcasted_iota(jnp.int32, (16, side), 0) == 0
    return jnp.where(first, jnp.broadcast_to(mask_row, (16, side)), 0.0).astype(BF16)


def halves_of(first, second):
    side = first.shape[1]
    left = lax.broadcasted_iota(jnp.int32, first.shape, 1) < side // 2
    low = jnp.where(left, first, pltpu.roll(second, side // 2, 1))
    high = jnp.where(left, pltpu.roll(first, side // 2, 1), second)
    return low, high


def sums_kernel(tiles, packed, step_blocks, code_ref, weight_ref, coef_ref, mask_ref, block_ref, *rest):
    outs = rest[:-4]
    acc, rows_sc, cols_sc, den_sc = rest[-4:]
    step = pl.program_id(0)
    side = 128

    @pl.when(step == 0)
    def _():
        acc[...] = jnp.zeros_like(acc)
        rows_sc[...] = jnp.zeros_like(rows_sc)

    def body(group, carry):
        work = []
        for u in range(GROUP1):
            j = group * GROUP1 + u
            b = step * step_blocks + j
            mask_row = mask_ref[pl.ds(j, 1), :].astype(F32)
            masked = block_ref[j] * mask_row.astype(BF16)
            for k in range(2):
                (tap_y,), whole_y = taps_of(code_ref[b, 4 * k + 1], code_ref[b, 4 * k + 3], coef_ref, False)
                (tap_x,), whole_x = taps_of(code_ref[b, 4 * k], code_ref[b, 4 * k + 2], coef_ref, False)
                work.append([b, k, mask_row, masked, tap_y, whole_y, tap_x, whole_x])
        passes = []
        for b, k, mask_row, masked, tap_y, whole_y, tap_x, whole_x in work:
            (ly_t,) = spread([tap_y], whole_y)
            passes.append(dot_t(ly_t, masked).astype(BF16))
        warps = []
        for (b, k, mask_row, masked, tap_y, whole_y, tap_x, whole_x), row_pass in zip(work, passes):
            (lx_t,) = spread([tap_x], whole_x)
            warps.append(dot(jnp.concatenate([row_pass, mask_rows(mask_row)], axis=0), lx_t))
        for (b, k, mask_row, masked, tap_y, whole_y, tap_x, whole_x), both in zip(work, warps):
            tile = code_ref[b, CODE_TILE]
            weight = weight_ref[0, b]
            sent = (weight * both[:side]).astype(BF16).astype(F32)
            acc[k, tile] = acc[k, tile] + sent
            at = whole_y + lax.broadcasted_iota(jnp.int32, (8, side), 0) - 3
            used = jnp.where((at >= 0) & (at < side), tap_y.astype(BF16).astype(F32), 0.0)
            rows_sum = jnp.sum(used, axis=0, keepdims=True)
            rows_sc[k, tile, pl.ds(b, 1), :] = (weight * rows_sum).astype(BF16).astype(F32)
            cols_sc[k, pl.ds(b, 1), :] = both[side : side + 1].astype(BF16).astype(F32)
        return carry

    lax.fori_loop(0, step_blocks // GROUP1, body, 0)

    @pl.when(step == pl.num_programs(0) - 1)
    def _():
        for k in range(2):
            cols = cols_sc[k]
            cols = jnp.concatenate([jnp.maximum(cols, 0.0), jnp.maximum(-cols, 0.0)], axis=0).astype(BF16)

            def one(t, carry, k=k, cols=cols):
                rows = rows_sc[k, t]
                rows = jnp.concatenate([jnp.maximum(rows, 0.0), jnp.maximum(-rows, 0.0)], axis=0).astype(BF16)
                den_sc[k, t] = dot_t(rows, cols)
                return carry

            lax.fori_loop(0, tiles, one, 0)
        if packed:
            keep_ref, send_ref = outs
            low_end = code_ref[0, CODE_EXP] == 0
            for dz in range(tiles):
                tile = lax.rem(code_ref[0, CODE_ROW] + dz, tiles)
                for which, source in enumerate((acc, den_sc)):
                    low, high = halves_of(source[0, tile], source[1, tile])
                    keep_ref[dz, which] = jnp.where(low_end, low, high)
                    send_ref[dz, which] = jnp.where(low_end, high, low).astype(BF16)
        else:

            def whole(t, carry):
                for k in range(2):
                    outs[0][t, 0, k] = acc[k, t]
                    outs[0][t, 1, k] = den_sc[k, t]
                return carry

            lax.fori_loop(0, tiles, whole, 0)


def vmem():
    return pl.BlockSpec(memory_space=pltpu.VMEM)


def smem():
    return pl.BlockSpec(memory_space=pltpu.SMEM)


def tile_sums(codes, weights, coef, masks, blocks, tiles, packed):
    count, side = blocks.shape[0], blocks.shape[1]
    step_blocks = GROUP1
    if packed:
        shapes = [((tiles, 2, side, side), F32), ((tiles, 2, side, side), BF16)]
    else:
        shapes = [((tiles, 2, 2, side, side), F32)]
    return pl.pallas_call(
        functools.partial(sums_kernel, tiles, packed, step_blocks),
        grid=(count // step_blocks,),
        out_shape=[jax.ShapeDtypeStruct(*shape) for shape in shapes],
        in_specs=[
            smem(),
            smem(),
            pl.BlockSpec(coef.shape, lambda i: (0, 0, 0)),
            pl.BlockSpec((step_blocks, side), lambda i: (i, 0)),
            pl.BlockSpec((step_blocks, side, side), lambda i: (i, 0, 0)),
        ],
        out_specs=[pl.BlockSpec(shape, lambda i, rank=len(shape): (0,) * rank) for shape, _ in shapes],
        scratch_shapes=[
            pltpu.VMEM((2, tiles, side, side), F32),
            pltpu.VMEM((2, tiles, count, side), F32),
            pltpu.VMEM((2, count, side), F32),
            pltpu.VMEM((2, tiles, side, side), F32),
        ],
        compiler_params=pltpu.CompilerParams(vmem_limit_bytes=VMEM_BYTES),
        cost_estimate=pl.CostEstimate(flops=int(8e9), bytes_accessed=int(3e6), transcendentals=0),
        name="tile_sums",
    )(codes, weights, coef, masks, blocks)


def pair_kernel(keep_ref, got_ref, *outs):
    for dz, out in enumerate(outs):
        for which in range(2):
            total = keep_ref[dz, which] + got_ref[dz, which].astype(F32)
            out[which] = total.astype(out.dtype)


def pair(keep, got):
    tiles, _, side, _ = keep.shape
    return pl.pallas_call(
        pair_kernel,
        out_shape=[jax.ShapeDtypeStruct((2, side, side), BF16 if dz else F32) for dz in range(tiles)],
        name="pair",
    )(keep, got)


def moments(product_x, product_y):
    side = product_x.shape[0]
    centre = (side - 1) / 2.0
    sum_x = product_x[side - 8 : side]
    sum_y = product_y[side - 8 : side]
    later = sum_y
    for v in range(side // 8 - 2, -1, -1):
        sum_x = sum_x + product_x[8 * v : 8 * v + 8]
        sum_y = sum_y + product_y[8 * v : 8 * v + 8]
        if v:
            later = later + sum_y
    sub = lax.broadcasted_iota(jnp.int32, (8, side), 0).astype(F32) - centre
    lane = lax.broadcasted_iota(jnp.int32, (1, side), 1).astype(F32) - centre
    tilted_y = 8.0 * later + sub * sum_y
    first = jnp.sum(sum_x, axis=0, keepdims=True)
    second = jnp.sum(sum_y, axis=0, keepdims=True)
    fourth = jnp.sum(tilted_y, axis=0, keepdims=True)
    return [first, second, first * lane * (1.0 / side), fourth * (1.0 / side)]


def slopes_kernel(step_blocks, start, code_ref, coef_ref, mask_ref, block_ref, *rest):
    slope_ref, part_ref = rest[-2:]
    step = pl.program_id(0) + start
    side = 128

    def body(group, carry):
        ones = jnp.ones((side, side), BF16)
        work = []
        for u in range(GROUP2):
            j = group * GROUP2 + u
            b = step * step_blocks + j
            mask_row = mask_ref[pl.ds(j, 1), :].astype(F32)
            masked = block_ref[j] * mask_row.astype(BF16)
            taps = []
            for k in range(2):
                taps.append(taps_of(code_ref[b, 4 * k], code_ref[b, 4 * k + 2], coef_ref, True))
                taps.append(taps_of(code_ref[b, 4 * k + 1], code_ref[b, 4 * k + 3], coef_ref, True))
            work.append([j, masked, mask_rows(mask_row), taps])
        cols, rights, rows, downs = [], [], [], []
        for j, masked, extra, taps in work:
            x0, x1 = spread(*taps[0]), spread(*taps[2])
            cols.append(dot(jnp.concatenate([masked, extra], axis=0), jnp.concatenate([x0[0], x1[0]], axis=1)))
            rights.append([jnp.concatenate(x0, axis=1), jnp.concatenate(x1, axis=1)])
        for j, masked, extra, taps in work:
            with_ones = jnp.concatenate([masked, ones], axis=1)
            y0, y1 = spread(*taps[1]), spread(*taps[3])
            rows.append([dot_t(y0[0], with_ones), dot_t(y1[0], with_ones)])
            downs.append([y0[1], y1[1]])
        late = []
        for (j, masked, extra, taps), col_both, right, row, down in zip(work, cols, rights, rows, downs):
            for k in range(2):
                row_pass = row[k][:, :side].astype(BF16)
                col_pass = col_both[:side, k * side : (k + 1) * side].astype(BF16)
                late.append((j, k, dot(row_pass, right[k]), dot_t(down[k], col_pass), row[k][:, side:], col_both[side : side + 1, k * side : (k + 1) * side]))
        for j, k, both, slope_y, rows_sum, cols_sum in late:
            warped = both[:, :side]
            weight_map = jnp.maximum(rows_sum * cols_sum, 0.0)
            value_x = weight_map * both[:, side:]
            value_y = weight_map * slope_y
            slope_ref[j, 2 * k] = value_x.astype(SLOPE)
            slope_ref[j, 2 * k + 1] = value_y.astype(SLOPE)
            for m, row in enumerate(moments(warped * value_x, warped * value_y)):
                part_ref[j, 4 * k + m : 4 * k + m + 1, :] = row
        return carry

    lax.fori_loop(0, step_blocks // GROUP2, body, 0)


def slopes_of(codes, coef, masks, blocks, first, size, filled):
    count, side = blocks.shape[0], blocks.shape[1]
    step_blocks = 8
    start = first // step_blocks
    return pl.pallas_call(
        functools.partial(slopes_kernel, step_blocks, start),
        grid=(size // step_blocks,),
        out_shape=[
            jax.ShapeDtypeStruct((count, 4, side, side), SLOPE),
            jax.ShapeDtypeStruct((count, 8, side), F32),
        ],
        in_specs=[
            smem(),
            pl.BlockSpec(coef.shape, lambda i: (0, 0, 0)),
            pl.BlockSpec((step_blocks, side), lambda i: (i + start, 0)),
            pl.BlockSpec((step_blocks, side, side), lambda i: (i + start, 0, 0)),
        ]
        + [pl.BlockSpec(memory_space=pl.ANY)] * len(filled),
        out_specs=[
            pl.BlockSpec((step_blocks, 4, side, side), lambda i: (i + start, 0, 0, 0)),
            pl.BlockSpec((step_blocks, 8, side), lambda i: (i + start, 0, 0)),
        ],
        input_output_aliases={4 + n: n for n in range(len(filled))},
        compiler_params=pltpu.CompilerParams(vmem_limit_bytes=VMEM_BYTES),
        cost_estimate=pl.CostEstimate(flops=int(1.5e8) * size, bytes_accessed=int(3e5) * size, transcendentals=0),
        name="slopes",
    )(codes, coef, masks, blocks, *filled)


def coadd_kernel(code_ref, *refs):
    parts, (piece_ref, edge_ref) = refs[:-2], refs[-2:]
    num, den = parts[0][0], parts[0][1]
    for part in parts[1:]:
        num = num + part[0].astype(F32)
        den = den + part[1].astype(F32)
    side = num.shape[1]
    left = lax.broadcasted_iota(jnp.int32, num.shape, 1) < side // 2
    first = num / (1.0 + den)
    piece = (num + jnp.where(left, 0.0, pltpu.roll(first, side // 2, 1))) / (1.0 + den)
    piece_ref[...] = piece
    flipped = jnp.transpose(piece)
    half = side // 2
    outer = jnp.concatenate([flipped[0:8], flipped[half : half + 8]], axis=0)
    inner = jnp.concatenate([flipped[half - 8 : half], flipped[side - 8 : side]], axis=0)
    edge_ref[...] = jnp.where(code_ref[0, CODE_EXP] == 0, outer, inner).astype(BF16)


def coadd_of(codes, parts):
    side = parts[0].shape[2]
    return pl.pallas_call(
        coadd_kernel,
        out_shape=[jax.ShapeDtypeStruct((side, side), F32), jax.ShapeDtypeStruct((16, side), BF16)],
        in_specs=[smem()] + [vmem()] * len(parts),
        out_specs=[vmem(), vmem()],
        name="coadd",
    )(codes, *parts)


def join_kernel(code_ref, own_ref, other_ref, edge_ref, far_ref, sky_ref, tile_ref):
    here = code_ref[0, CODE_EXP] == 0
    side = own_ref.shape[1]
    own, other = own_ref[...], other_ref[...]
    tiles = halves_of(jnp.where(here, own, other), jnp.where(here, other, own))
    edge, far = edge_ref[...].astype(F32), far_ref[...].astype(F32)
    left, right = jnp.where(here, far, edge), jnp.where(here, edge, far)
    for k in range(2):
        sky_ref[k, 0:side, :] = tiles[k].astype(BF16)
        at = slice(8 * k, 8 * k + 8)
        sky_ref[k, side : side + 16, :] = jnp.concatenate([left[at], right[at]], axis=0).astype(BF16)
    tile_ref[...] = tiles[1]


def join(codes, own, other, edge, far):
    side = own.shape[1]
    return pl.pallas_call(
        join_kernel,
        out_shape=[jax.ShapeDtypeStruct((2, side + 16, side), BF16), jax.ShapeDtypeStruct((side, side), F32)],
        in_specs=[smem()] + [vmem()] * 4,
        out_specs=[vmem(), vmem()],
        name="join",
    )(codes, own, other, edge, far)


def band_of(values, diagonal):
    total = jnp.zeros(diagonal.shape, F32)
    for q, value in enumerate(values):
        total = jnp.where(diagonal == q, value, total)
    high = total.astype(BF16)
    return jnp.concatenate([high, (total - high.astype(F32)).astype(BF16)], axis=1)


def gradient_kernel(tiles, step_blocks, code_ref, psf_ref, *rest):
    skies = rest[:tiles]
    slope_ref, part_ref, out_ref, smooth, model = rest[tiles:]
    step = pl.program_id(0)
    side = 128

    @pl.when(step == 0)
    def _():
        along = lax.broadcasted_iota(jnp.int32, (side, side), 0)
        across = lax.broadcasted_iota(jnp.int32, (side, side), 1)
        edge = lax.broadcasted_iota(jnp.int32, (16, side), 0)
        edge = jnp.where(edge < 8, edge - 8, edge + side - 8)
        for k in range(2):
            taps = [psf_ref[k, 1, q] for q in range(TAPS)]
            inner = band_of(taps, along - across + RAD)
            outer = band_of(taps, edge - across[:16] + RAD)
            smooth[k, 0:8, :] = jnp.zeros((8, side), F32)
            smooth[k, 8 + tiles * side : 16 + tiles * side, :] = jnp.zeros((8, side), F32)
            for turn in range(tiles):
                tile = lax.rem(code_ref[0, CODE_ROW] + tiles - turn, tiles)
                both = dot(skies[turn][k, 0:side, :], inner) + dot_t(skies[turn][k, side : side + 16, :], outer)
                smooth[k, pl.ds(pl.multiple_of(8 + tile * side, 8), side), :] = both[:, :side] + both[:, side:]
            chunk = 64

            def rows(c, carry, k=k):
                start = pl.multiple_of(c * chunk, chunk)
                seen = smooth[k, pl.ds(start, chunk + 16), :]
                total = psf_ref[k, 0, 0] * seen[4 : 4 + chunk]
                for p in range(1, TAPS):
                    total = total + psf_ref[k, 0, p] * seen[4 + p : 4 + p + chunk]
                model[k, pl.ds(start, chunk), :] = total.astype(BF16).astype(F32)
                return carry

            lax.fori_loop(0, tiles * side // chunk, rows, 0)

    def body(group, carry):
        found = []
        for u in range(GROUP3):
            j = group * GROUP3 + u
            start = pl.multiple_of(code_ref[step * step_blocks + j, CODE_TILE] * side, side)
            for k in range(2):
                cutout = model[k, pl.ds(start, side), :]
                slope_x, slope_y = slope_ref[j, 2 * k].astype(F32), slope_ref[j, 2 * k + 1].astype(F32)
                found.append((j, k, moments(cutout * slope_x, cutout * slope_y)))
        for j, k, rows in found:
            for m, row in enumerate(rows):
                out_ref[j, 4 * k + m : 4 * k + m + 1, :] = part_ref[j, 4 * k + m : 4 * k + m + 1, :] - row
        return carry

    lax.fori_loop(0, step_blocks // GROUP3, body, 0)


def gradients_of(codes, psf, skies, slopes, parts):
    count, _, side, _ = slopes.shape
    tiles = len(skies)
    step_blocks = 8
    sky_shape = skies[0].shape
    return pl.pallas_call(
        functools.partial(gradient_kernel, tiles, step_blocks),
        grid=(count // step_blocks,),
        out_shape=jax.ShapeDtypeStruct((count, 8, side), F32),
        in_specs=[smem(), smem()]
        + [pl.BlockSpec(sky_shape, lambda i: (0, 0, 0))] * tiles
        + [
            pl.BlockSpec((step_blocks, 4, side, side), lambda i: (i, 0, 0, 0)),
            pl.BlockSpec((step_blocks, 8, side), lambda i: (i, 0, 0)),
        ],
        out_specs=pl.BlockSpec((step_blocks, 8, side), lambda i: (i, 0, 0)),
        scratch_shapes=[
            pltpu.VMEM((2, tiles * side + 16, side), F32),
            pltpu.VMEM((2, tiles * side, side), F32),
        ],
        compiler_params=pltpu.CompilerParams(vmem_limit_bytes=VMEM_BYTES),
        cost_estimate=pl.CostEstimate(flops=int(4e9), bytes_accessed=int(20e6), transcendentals=0),
        name="gradients",
    )(codes, psf, *skies, slopes, parts)


def swap(cells):
    return lax.ppermute(cells, "exp", [(0, 1), (1, 0)])


def turned(cells, dz, tiles):
    return lax.ppermute(cells, "tx", [(z, (z + dz) % tiles) for z in range(tiles)])


def to_sides(edge, columns):
    perm = [(y, y - 1) for y in range(1, columns)] + [(columns + y, columns + y + 1) for y in range(columns - 1)]
    return lax.ppermute(edge, ("exp", "ty"), perm)


def local(exposures, block_tile, affine, col_mask, block_weight, psf):
    blocks = exposures[0]
    count, side = blocks.shape[0], blocks.shape[1]
    tiles, halves, columns = lax.axis_size("tx"), lax.axis_size("exp"), lax.axis_size("ty")
    coef = jnp.asarray(series())
    place = [jnp.full((count, 1), lax.axis_index(axis), jnp.int32) for axis in ("exp", "tx")]
    codes = jnp.concatenate([affine.reshape(count, 8), block_tile[0]] + place, axis=1)
    masks = col_mask[0]
    small = halves == 2 and tiles <= 4
    sums = tile_sums(codes, block_weight, coef, masks, blocks, tiles, small)
    filled = ()
    for chunk in range(CHUNKS):
        size = count // CHUNKS
        filled = slopes_of(codes, coef, masks, blocks, chunk * size, size, filled)
    slopes, parts = filled
    if small:
        keep, send = sums
        totals = pair(keep, swap(send))
        got = [totals[0]] + [turned(totals[dz], dz, tiles) for dz in range(1, tiles)]
        piece, edge = coadd_of(codes, got)
        other = swap(piece)
        edge = to_sides(edge, columns)
        sky, coadd_tile = join(codes, piece, other, edge, swap(edge))
        skies = [sky] + [turned(sky, dz, tiles) for dz in range(1, tiles)]
    else:
        me = lax.axis_index("tx")
        summed = lax.psum_scatter(sums[0], "tx", scatter_dimension=0, tiled=True)
        (num, den) = lax.psum(summed[0], "exp")
        one = num[0] / (1.0 + den[0])
        coadd_tile = (num[1] + one) / (1.0 + den[1])
        both = jnp.stack([one, coadd_tile])
        flipped = jnp.swapaxes(both, 1, 2).astype(BF16)
        left = lax.ppermute(flipped[:, side - 8 :], "ty", [(y, y + 1) for y in range(columns - 1)])
        right = lax.ppermute(flipped[:, :8], "ty", [(y + 1, y) for y in range(columns - 1)])
        sky = jnp.concatenate([both.astype(BF16), left, right], axis=1)
        gathered = lax.all_gather(sky, "tx", axis=0)
        skies = [lax.dynamic_index_in_dim(gathered, (me + tiles - turn) % tiles, 0, False) for turn in range(tiles)]
    rows = gradients_of(codes, psf, skies, slopes, parts)
    gradients = (jnp.sum(rows, axis=2) / side).reshape(1, count, 2, 4)
    return gradients, coadd_tile


def solution(mesh):
    placed = (
        P("ty", ("exp", "tx"), None, None),
        P("ty", ("exp", "tx"), None),
        P("ty", ("exp", "tx"), None, None),
        P("ty", ("exp", "tx"), None),
        P("ty", ("exp", "tx")),
        P(),
    )
    return jax.shard_map(
        local,
        mesh=mesh,
        in_specs=placed,
        out_specs=(P("ty", ("exp", "tx"), None, None), P("tx", "ty")),
        check_vma=False,
    )
```

```python
import functools

import jax
import jax.numpy as jnp
import numpy as np
from jax import lax
from jax.experimental import pallas as pl
from jax.experimental.pallas import tpu as pltpu
from jax.sharding import PartitionSpec as P

RAD = 4
TAPS = 2 * RAD + 1
DEGREE = 10
F32 = jnp.float32
BF16 = jnp.bfloat16
GROUP1 = 8
GROUP2 = 4
GROUP3 = 4
CHUNKS = (24, 20, 20)
SLOPE = jnp.bfloat16
VMEM_BYTES = 56 * 1024 * 1024
SMALL_BYTES = 20 * 1024 * 1024
TINY_BYTES = 6 * 1024 * 1024


def series():
    count = 64
    nodes = np.cos(np.pi * (np.arange(count) + 0.5) / count)
    table = np.zeros((2, DEGREE + 1, 8), np.float64)
    for row in range(1, 7):
        d = nodes * 0.5 + 0.5 - (row - 3)
        a, b = np.sinc(d), np.sinc(d / 3.0)
        da = (np.cos(np.pi * d) - a) / d
        db = (np.cos(np.pi * d / 3.0) - b) / d
        for which, values in enumerate((a * b, da * b + a * db)):
            fit = np.polynomial.chebyshev.Chebyshev.fit(nodes * 0.5, values, DEGREE, domain=[-0.5, 0.5])
            table[which, :, row] = fit.convert(kind=np.polynomial.Polynomial).coef
    return np.repeat(table.reshape(2 * (DEGREE + 1), 8, 1), 128, axis=2).astype(np.float32)


def taps_of(shift_code, stretch_code, coef_ref, slopes):
    side = 128
    centre = (side - 1) / 2.0
    lane = lax.broadcasted_iota(jnp.int32, (8, side), 1).astype(F32)
    shift = jnp.full((8, side), shift_code, jnp.int32).astype(F32) * (1.0 / 256.0)
    stretch = jnp.full((8, side), stretch_code, jnp.int32).astype(F32) * (1.0 / 51200.0)
    source = centre + (1.0 + stretch) * (lane - centre) + shift
    whole = jnp.floor(source)
    v = (source - whole) - 0.5
    found = []
    for which in range(2 if slopes else 1):
        base = which * (DEGREE + 1)
        total = coef_ref[base + DEGREE]
        for power in range(DEGREE - 1, -1, -1):
            total = total * v + coef_ref[base + power]
        found.append(total)
    return found, whole.astype(jnp.int32)


def pick(taps, index):
    numbers = lax.GatherDimensionNumbers(
        offset_dims=(),
        collapsed_slice_dims=(0,),
        start_index_map=(0,),
        operand_batching_dims=(1,),
        start_indices_batching_dims=(1,),
    )
    mode = lax.GatherScatterMode.PROMISE_IN_BOUNDS
    return lax.gather(taps, index[..., None], numbers, slice_sizes=(1, 1), mode=mode)


def spread(tap_list, whole):
    side = 128
    base = lax.broadcasted_iota(jnp.int32, (8, side), 0) + 3 - whole
    indices = [jnp.clip(base + 8 * v, 0, 7) for v in range(side // 8)]
    return [
        jnp.concatenate([pick(taps, index) for index in indices], axis=0).astype(BF16)
        for taps in tap_list
    ]


def dot(a, b):
    return jnp.dot(a, b, preferred_element_type=F32)


def dot_t(a, b):
    return lax.dot_general(a, b, (((0,), (0,)), ((), ())), preferred_element_type=F32)


def mask_rows(mask_row):
    side = mask_row.shape[1]
    first = lax.broadcasted_iota(jnp.int32, (16, side), 0) == 0
    return jnp.where(first, jnp.broadcast_to(mask_row, (16, side)), 0.0).astype(BF16)


def halves_of(first, second):
    side = first.shape[1]
    left = lax.broadcasted_iota(jnp.int32, first.shape, 1) < side // 2
    low = jnp.where(left, first, pltpu.roll(second, side // 2, 1))
    high = jnp.where(left, pltpu.roll(first, side // 2, 1), second)
    return low, high


def sums_kernel(tiles, packed, step_blocks, affine_ref, target_ref, weight_ref, coef_ref, mask_ref, block_ref, *rest):
    outs = rest[:-4]
    acc, rows_sc, cols_sc, den_sc = rest[-4:]
    step = pl.program_id(0)
    side = 128

    @pl.when(step == 0)
    def _():
        acc[...] = jnp.zeros_like(acc)
        rows_sc[...] = jnp.zeros_like(rows_sc)

    def body(group, carry):
        work = []
        for u in range(GROUP1):
            j = group * GROUP1 + u
            b = step * step_blocks + j
            mask_row = mask_ref[pl.ds(j, 1), :].astype(F32)
            masked = block_ref[j] * mask_row.astype(BF16)
            for k in range(2):
                (tap_y,), whole_y = taps_of(affine_ref[0, k, 1, b], affine_ref[0, k, 3, b], coef_ref, False)
                (tap_x,), whole_x = taps_of(affine_ref[0, k, 0, b], affine_ref[0, k, 2, b], coef_ref, False)
                work.append([b, k, mask_row, masked, tap_y, whole_y, tap_x, whole_x])
        passes = []
        for b, k, mask_row, masked, tap_y, whole_y, tap_x, whole_x in work:
            (ly_t,) = spread([tap_y], whole_y)
            passes.append(dot_t(ly_t, masked).astype(BF16))
        warps = []
        for (b, k, mask_row, masked, tap_y, whole_y, tap_x, whole_x), row_pass in zip(work, passes):
            (lx_t,) = spread([tap_x], whole_x)
            warps.append(dot(jnp.concatenate([row_pass, mask_rows(mask_row)], axis=0), lx_t))
        for (b, k, mask_row, masked, tap_y, whole_y, tap_x, whole_x), both in zip(work, warps):
            tile = target_ref[0, 0, b]
            weight = weight_ref[0, b]
            sent = (weight * both[:side]).astype(BF16).astype(F32)
            acc[k, tile] = acc[k, tile] + sent
            at = whole_y + lax.broadcasted_iota(jnp.int32, (8, side), 0) - 3
            used = jnp.where((at >= 0) & (at < side), tap_y.astype(BF16).astype(F32), 0.0)
            rows_sum = jnp.sum(used, axis=0, keepdims=True)
            rows_sc[k, tile, pl.ds(b, 1), :] = (weight * rows_sum).astype(BF16).astype(F32)
            cols_sc[k, pl.ds(b, 1), :] = both[side : side + 1].astype(BF16).astype(F32)
        return carry

    lax.fori_loop(0, step_blocks // GROUP1, body, 0)

    @pl.when(step == pl.num_programs(0) - 1)
    def _():
        for k in range(2):
            cols = cols_sc[k]
            cols = jnp.concatenate([jnp.maximum(cols, 0.0), jnp.maximum(-cols, 0.0)], axis=0).astype(BF16)

            def one(t, carry, k=k, cols=cols):
                rows = rows_sc[k, t]
                rows = jnp.concatenate([jnp.maximum(rows, 0.0), jnp.maximum(-rows, 0.0)], axis=0).astype(BF16)
                den_sc[k, t] = dot_t(rows, cols)
                return carry

            lax.fori_loop(0, tiles, one, 0, unroll=tiles if packed else 1)
        if packed:
            keep_ref, send_ref = outs
            low_end = lax.axis_index("exp") == 0
            for dz in range(tiles):
                tile = lax.rem(lax.axis_index("tx") + dz, tiles)
                for which, source in enumerate((acc, den_sc)):
                    low, high = halves_of(source[0, tile], source[1, tile])
                    keep_ref[dz, which] = jnp.where(low_end, low, high)
                    send_ref[dz, which] = jnp.where(low_end, high, low).astype(BF16)
        else:

            def whole(t, carry):
                for k in range(2):
                    outs[0][t, 0, k] = acc[k, t]
                    outs[0][t, 1, k] = den_sc[k, t]
                return carry

            lax.fori_loop(0, tiles, whole, 0)


def vmem():
    return pl.BlockSpec(memory_space=pltpu.VMEM)


def scalars(array):
    rank = array.ndim
    return pl.BlockSpec(array.shape, lambda i: (0,) * rank, memory_space=pltpu.SMEM)


def smem():
    return pl.BlockSpec(memory_space=pltpu.SMEM)


def tile_sums(affine, target, weights, coef, masks, blocks, tiles, packed):
    count, side = blocks.shape[0], blocks.shape[1]
    step_blocks = GROUP1
    if packed:
        shapes = [((tiles, 2, side, side), F32), ((tiles, 2, side, side), BF16)]
    else:
        shapes = [((tiles, 2, 2, side, side), F32)]
    return pl.pallas_call(
        functools.partial(sums_kernel, tiles, packed, step_blocks),
        grid=(count // step_blocks,),
        out_shape=[jax.ShapeDtypeStruct(*shape) for shape in shapes],
        in_specs=[
            scalars(affine),
            scalars(target),
            scalars(weights),
            pl.BlockSpec(coef.shape, lambda i: (0, 0, 0)),
            pl.BlockSpec((step_blocks, side), lambda i: (i, 0)),
            pl.BlockSpec((step_blocks, side, side), lambda i: (i, 0, 0)),
        ],
        out_specs=[pl.BlockSpec(shape, lambda i, rank=len(shape): (0,) * rank) for shape, _ in shapes],
        scratch_shapes=[
            pltpu.VMEM((2, tiles, side, side), F32),
            pltpu.VMEM((2, tiles, count, side), F32),
            pltpu.VMEM((2, count, side), F32),
            pltpu.VMEM((2, tiles, side, side), F32),
        ],
        compiler_params=pltpu.CompilerParams(vmem_limit_bytes=VMEM_BYTES),
        cost_estimate=pl.CostEstimate(flops=int(8e9), bytes_accessed=int(3e6), transcendentals=0),
        name="tile_sums",
    )(affine, target, weights, coef, masks, blocks)


def pair_kernel(keep_ref, got_ref, after_ref, *outs):
    del after_ref
    for dz, out in enumerate(outs):
        for which in range(2):
            total = keep_ref[dz, which] + got_ref[dz, which].astype(F32)
            out[which] = total.astype(out.dtype)


def pair(keep, got, after):
    tiles, _, side, _ = keep.shape
    return pl.pallas_call(
        pair_kernel,
        out_shape=[jax.ShapeDtypeStruct((2, side, side), BF16 if dz else F32) for dz in range(tiles)],
        in_specs=[vmem(), vmem(), smem()],
        out_specs=[vmem()] * tiles,
        compiler_params=pltpu.CompilerParams(vmem_limit_bytes=TINY_BYTES),
        name="pair",
    )(keep, got, after)


def moments(product_x, product_y):
    side = product_x.shape[0]
    centre = (side - 1) / 2.0
    sum_x = product_x[side - 8 : side]
    sum_y = product_y[side - 8 : side]
    later = sum_y
    for v in range(side // 8 - 2, -1, -1):
        sum_x = sum_x + product_x[8 * v : 8 * v + 8]
        sum_y = sum_y + product_y[8 * v : 8 * v + 8]
        if v:
            later = later + sum_y
    sub = lax.broadcasted_iota(jnp.int32, (8, side), 0).astype(F32) - centre
    lane = lax.broadcasted_iota(jnp.int32, (1, side), 1).astype(F32) - centre
    tilted_y = 8.0 * later + sub * sum_y
    first = jnp.sum(sum_x, axis=0, keepdims=True)
    second = jnp.sum(sum_y, axis=0, keepdims=True)
    fourth = jnp.sum(tilted_y, axis=0, keepdims=True)
    return [first, second, first * lane * (1.0 / side), fourth * (1.0 / side)]


def slopes_kernel(step_blocks, start, affine_ref, coef_ref, mask_ref, block_ref, *rest):
    slope_ref, part_ref, token_ref = rest[-3:]
    token_ref[0] = 0
    step = pl.program_id(0) + start
    side = 128

    def body(group, carry):
        ones = jnp.ones((side, side), BF16)
        work = []
        for u in range(GROUP2):
            j = group * GROUP2 + u
            b = step * step_blocks + j
            mask_row = mask_ref[pl.ds(b, 1), :].astype(F32)
            masked = block_ref[j] * mask_row.astype(BF16)
            taps = []
            for k in range(2):
                taps.append(taps_of(affine_ref[0, k, 0, b], affine_ref[0, k, 2, b], coef_ref, True))
                taps.append(taps_of(affine_ref[0, k, 1, b], affine_ref[0, k, 3, b], coef_ref, True))
            work.append([j, masked, mask_rows(mask_row), taps])
        cols, rights, rows, downs = [], [], [], []
        for j, masked, extra, taps in work:
            x0, x1 = spread(*taps[0]), spread(*taps[2])
            cols.append(dot(jnp.concatenate([masked, extra], axis=0), jnp.concatenate([x0[0], x1[0]], axis=1)))
            rights.append([jnp.concatenate(x0, axis=1), jnp.concatenate(x1, axis=1)])
        for j, masked, extra, taps in work:
            with_ones = jnp.concatenate([masked, ones], axis=1)
            y0, y1 = spread(*taps[1]), spread(*taps[3])
            rows.append([dot_t(y0[0], with_ones), dot_t(y1[0], with_ones)])
            downs.append([y0[1], y1[1]])
        late = []
        for (j, masked, extra, taps), col_both, right, row, down in zip(work, cols, rights, rows, downs):
            for k in range(2):
                row_pass = row[k][:, :side].astype(BF16)
                col_pass = col_both[:side, k * side : (k + 1) * side].astype(BF16)
                late.append((j, k, dot(row_pass, right[k]), dot_t(down[k], col_pass), row[k][:, side:], col_both[side : side + 1, k * side : (k + 1) * side]))
        for j, k, both, slope_y, rows_sum, cols_sum in late:
            warped = both[:, :side]
            weight_map = jnp.maximum(rows_sum * cols_sum, 0.0)
            value_x = weight_map * both[:, side:]
            value_y = weight_map * slope_y
            slope_ref[j, 2 * k] = value_x.astype(SLOPE)
            slope_ref[j, 2 * k + 1] = value_y.astype(SLOPE)
            for m, row in enumerate(moments(warped * value_x, warped * value_y)):
                part_ref[j, 4 * k + m : 4 * k + m + 1, :] = row
        return carry

    lax.fori_loop(0, step_blocks // GROUP2, body, 0)


def slopes_of(affine, coef, masks, blocks, first, size):
    side = blocks.shape[1]
    step_blocks = GROUP2
    start = first // step_blocks
    return pl.pallas_call(
        functools.partial(slopes_kernel, step_blocks, start),
        grid=(size // step_blocks,),
        out_shape=[
            jax.ShapeDtypeStruct((size, 4, side, side), SLOPE),
            jax.ShapeDtypeStruct((size, 8, side), F32),
            jax.ShapeDtypeStruct((1,), jnp.int32),
        ],
        in_specs=[
            scalars(affine),
            pl.BlockSpec(coef.shape, lambda i: (0, 0, 0)),
            pl.BlockSpec(masks.shape, lambda i: (0, 0)),
            pl.BlockSpec((step_blocks, side, side), lambda i: (i + start, 0, 0)),
        ],
        out_specs=[
            pl.BlockSpec((step_blocks, 4, side, side), lambda i: (i, 0, 0, 0)),
            pl.BlockSpec((step_blocks, 8, side), lambda i: (i, 0, 0)),
            smem(),
        ],
        compiler_params=pltpu.CompilerParams(vmem_limit_bytes=SMALL_BYTES),
        cost_estimate=pl.CostEstimate(flops=int(1.5e8) * size, bytes_accessed=int(3e5) * size, transcendentals=0),
        name="slopes",
    )(affine, coef, masks, blocks)


def coadd_kernel(after_ref, *refs):
    del after_ref
    parts, (piece_ref, edge_ref) = refs[:-2], refs[-2:]
    num, den = parts[0][0], parts[0][1]
    for part in parts[1:]:
        num = num + part[0].astype(F32)
        den = den + part[1].astype(F32)
    side = num.shape[1]
    left = lax.broadcasted_iota(jnp.int32, num.shape, 1) < side // 2
    first = num / (1.0 + den)
    piece = (num + jnp.where(left, 0.0, pltpu.roll(first, side // 2, 1))) / (1.0 + den)
    piece_ref[...] = piece
    flipped = jnp.transpose(piece)
    half = side // 2
    outer = jnp.concatenate([flipped[0:8], flipped[half : half + 8]], axis=0)
    inner = jnp.concatenate([flipped[half - 8 : half], flipped[side - 8 : side]], axis=0)
    edge_ref[...] = jnp.where(lax.axis_index("exp") == 0, outer, inner).astype(BF16)


def coadd_of(after, parts):
    side = parts[0].shape[2]
    return pl.pallas_call(
        coadd_kernel,
        out_shape=[jax.ShapeDtypeStruct((side, side), F32), jax.ShapeDtypeStruct((16, side), BF16)],
        in_specs=[smem()] + [vmem()] * len(parts),
        out_specs=[vmem(), vmem()],
        compiler_params=pltpu.CompilerParams(vmem_limit_bytes=TINY_BYTES),
        name="coadd",
    )(after, *parts)


def band_of(values, diagonal):
    total = jnp.zeros(diagonal.shape, F32)
    for q, value in enumerate(values):
        total = jnp.where(diagonal == q, value, total)
    high = total.astype(BF16)
    return jnp.concatenate([high, (total - high.astype(F32)).astype(BF16)], axis=1)


def smoothed(tile, edges, taps):
    side = tile.shape[1]
    along = lax.broadcasted_iota(jnp.int32, (side, side), 0)
    across = lax.broadcasted_iota(jnp.int32, (side, side), 1)
    edge = along[:16]
    edge = jnp.where(edge < 8, edge - 8, edge + side - 8)
    inner = band_of(taps, along - across + RAD)
    outer = band_of(taps, edge - across[:16] + RAD)
    high = tile.astype(BF16)
    low = (tile - high.astype(F32)).astype(BF16)
    both = dot(high, inner) + dot_t(edges, outer)
    return both[:, :side] + both[:, side:] + dot(low, inner[:, :side])


def join_kernel(psf_ref, own_ref, other_ref, edge_ref, far_ref, after_ref, sky_ref, tile_ref):
    del after_ref
    here = lax.axis_index("exp") == 0
    own, other = own_ref[...], other_ref[...]
    tiles = halves_of(jnp.where(here, own, other), jnp.where(here, other, own))
    edge, far = edge_ref[...].astype(F32), far_ref[...].astype(F32)
    left, right = jnp.where(here, far, edge), jnp.where(here, edge, far)
    for k in range(2):
        at = slice(8 * k, 8 * k + 8)
        edges = jnp.concatenate([left[at], right[at]], axis=0).astype(BF16)
        sky_ref[k] = smoothed(tiles[k], edges, [psf_ref[k, 1, q] for q in range(TAPS)]).astype(BF16)
    tile_ref[...] = tiles[1]


def join(psf, own, other, edge, far, after):
    side = own.shape[1]
    return pl.pallas_call(
        join_kernel,
        out_shape=[jax.ShapeDtypeStruct((2, side, side), BF16), jax.ShapeDtypeStruct((side, side), F32)],
        in_specs=[smem()] + [vmem()] * 4 + [smem()],
        out_specs=[vmem(), vmem()],
        compiler_params=pltpu.CompilerParams(vmem_limit_bytes=TINY_BYTES),
        name="join",
    )(psf, own, other, edge, far, after)


def whole_kernel(psf_ref, tile_ref, edge_ref, sky_ref):
    for k in range(2):
        sky_ref[k] = smoothed(tile_ref[k], edge_ref[k], [psf_ref[k, 1, q] for q in range(TAPS)]).astype(BF16)


def whole_sky(psf, tiles, edges):
    return pl.pallas_call(
        whole_kernel,
        out_shape=jax.ShapeDtypeStruct(tiles.shape, BF16),
        in_specs=[smem(), vmem(), vmem()],
        out_specs=vmem(),
        compiler_params=pltpu.CompilerParams(vmem_limit_bytes=TINY_BYTES),
        name="whole_sky",
    )(psf, tiles, edges)


def gradient_kernel(tiles, target_ref, psf_ref, *rest):
    skies = rest[:tiles]
    chunk_refs, (out_ref, smooth, model) = rest[tiles:-3], rest[-3:]
    side = 128
    for k in range(2):
        smooth[k, 0:8, :] = jnp.zeros((8, side), F32)
        smooth[k, 8 + tiles * side : 16 + tiles * side, :] = jnp.zeros((8, side), F32)
        for turn in range(tiles):
            tile = lax.rem(lax.axis_index("tx") + tiles - turn, tiles)
            smooth[k, pl.ds(pl.multiple_of(8 + tile * side, 8), side), :] = skies[turn][k].astype(F32)
        chunk = 64

        def rows(c, carry, k=k):
            start = pl.multiple_of(c * chunk, chunk)
            seen = smooth[k, pl.ds(start, chunk + 16), :]
            total = psf_ref[k, 0, 0] * seen[4 : 4 + chunk]
            for p in range(1, TAPS):
                total = total + psf_ref[k, 0, p] * seen[4 + p : 4 + p + chunk]
            model[k, pl.ds(start, chunk), :] = total.astype(BF16).astype(F32)
            return carry

        lax.fori_loop(0, tiles * side // chunk, rows, 0, unroll=2)

    lane = lax.broadcasted_iota(jnp.int32, out_ref.shape[1:], 2)
    gathered = jnp.zeros(out_ref.shape[1:], F32)
    first = 0
    for slope_ref, part_ref in zip(chunk_refs[::2], chunk_refs[1::2]):

        def body(group, gathered, first=first, slope_ref=slope_ref, part_ref=part_ref):
            found = []
            for u in range(GROUP3):
                j = group * GROUP3 + u
                start = pl.multiple_of(target_ref[0, 0, first + j] * side, side)
                rows = []
                for k in range(2):
                    cutout = model[k, pl.ds(start, side), :]
                    slope_x, slope_y = slope_ref[j, 2 * k].astype(F32), slope_ref[j, 2 * k + 1].astype(F32)
                    rows += moments(cutout * slope_x, cutout * slope_y)
                found.append((j, rows))
            for j, rows in found:
                total = jnp.sum(part_ref[j] - jnp.concatenate(rows, axis=0), axis=1, keepdims=True) * (1.0 / side)
                gathered = jnp.where(lane == first + j, total.reshape(2, 4, 1), gathered)
            return gathered

        gathered = lax.fori_loop(0, slope_ref.shape[0] // GROUP3, body, gathered)
        first += slope_ref.shape[0]
    out_ref[0] = gathered


def gradients_of(target, psf, skies, chunks):
    side = skies[0].shape[1]
    tiles, count = len(skies), target.shape[2]
    arrays = [array for pair_of in chunks for array in pair_of]
    return pl.pallas_call(
        functools.partial(gradient_kernel, tiles),
        out_shape=jax.ShapeDtypeStruct((1, 2, 4, count), F32),
        in_specs=[smem(), smem()] + [vmem()] * (tiles + len(arrays)),
        out_specs=vmem(),
        scratch_shapes=[
            pltpu.VMEM((2, tiles * side + 16, side), F32),
            pltpu.VMEM((2, tiles * side, side), F32),
        ],
        compiler_params=pltpu.CompilerParams(vmem_limit_bytes=SMALL_BYTES),
        cost_estimate=pl.CostEstimate(flops=int(4e9), bytes_accessed=int(20e6), transcendentals=0),
        name="gradients",
    )(target, psf, *skies, *arrays)


def swap(cells):
    return lax.ppermute(cells, "exp", [(0, 1), (1, 0)])


def turned(cells, dz, tiles):
    return lax.ppermute(cells, "tx", [(z, (z + dz) % tiles) for z in range(tiles)])


def to_sides(edge, columns):
    perm = [(y, y - 1) for y in range(1, columns)] + [(columns + y, columns + y + 1) for y in range(columns - 1)]
    return lax.ppermute(edge, ("exp", "ty"), perm)


def local(exposures, block_tile, affine, col_mask, block_weight, psf):
    blocks = exposures[0]
    count, side = blocks.shape[0], blocks.shape[1]
    tiles, halves, columns = lax.axis_size("tx"), lax.axis_size("exp"), lax.axis_size("ty")
    coef = jnp.asarray(series())
    affine = affine.transpose(0, 2, 3, 1)
    block_tile = block_tile.transpose(0, 2, 1)
    masks = col_mask[0]
    small = halves == 2 and tiles <= 4
    sums = tile_sums(affine, block_tile, block_weight, coef, masks, blocks, tiles, small)
    chunks, tokens, first = [], [], 0
    scale = count // sum(CHUNKS)
    for size in CHUNKS:
        *found, token = slopes_of(affine, coef, masks, blocks, first, size * scale)
        chunks.append(found)
        tokens.append(token)
        first += size * scale
    if small:
        keep, send = sums
        totals = pair(keep, swap(send), tokens[0])
        got = [totals[0]] + [turned(totals[dz], dz, tiles) for dz in range(1, tiles)]
        piece, edge = coadd_of(tokens[1], got)
        other = swap(piece)
        edge = to_sides(edge, columns)
        sky, coadd_tile = join(psf, piece, other, edge, swap(edge), tokens[1])
        skies = [sky] + [turned(sky, dz, tiles) for dz in range(1, tiles)]
    else:
        me = lax.axis_index("tx")
        summed = lax.psum_scatter(sums[0], "tx", scatter_dimension=0, tiled=True)
        (num, den) = lax.psum(summed[0], "exp")
        one = num[0] / (1.0 + den[0])
        coadd_tile = (num[1] + one) / (1.0 + den[1])
        both = jnp.stack([one, coadd_tile])
        flipped = jnp.swapaxes(both, 1, 2).astype(BF16)
        left = lax.ppermute(flipped[:, side - 8 :], "ty", [(y, y + 1) for y in range(columns - 1)])
        right = lax.ppermute(flipped[:, :8], "ty", [(y + 1, y) for y in range(columns - 1)])
        sky = whole_sky(psf, both, jnp.concatenate([left, right], axis=1))
        gathered = lax.all_gather(sky, "tx", axis=0)
        skies = [lax.dynamic_index_in_dim(gathered, (me + tiles - turn) % tiles, 0, False) for turn in range(tiles)]
    gradients = gradients_of(block_tile, psf, skies, chunks)
    return gradients.transpose(0, 3, 1, 2), coadd_tile


def solution(mesh):
    placed = (
        P("ty", ("exp", "tx"), None, None),
        P("ty", ("exp", "tx"), None),
        P("ty", ("exp", "tx"), None, None),
        P("ty", ("exp", "tx"), None),
        P("ty", ("exp", "tx")),
        P(),
    )
    return jax.shard_map(
        local,
        mesh=mesh,
        in_specs=placed,
        out_specs=(P("ty", ("exp", "tx"), None, None), P("tx", "ty")),
        check_vma=False,
    )
```

```python
import functools

import jax
import jax.numpy as jnp
import numpy as np
from jax import lax
from jax.experimental import pallas as pl
from jax.experimental.pallas import tpu as pltpu
from jax.sharding import PartitionSpec as P

RAD = 4
TAPS = 2 * RAD + 1
DEGREE = 10
F32 = jnp.float32
BF16 = jnp.bfloat16
GROUP1 = 8
GROUP2 = 4
GROUP3 = 8
CHUNKS = (24, 16, 24)
SLOPE = jnp.bfloat16
VMEM_BYTES = 56 * 1024 * 1024
SMALL_BYTES = 20 * 1024 * 1024
TINY_BYTES = 6 * 1024 * 1024


def series():
    count = 64
    nodes = np.cos(np.pi * (np.arange(count) + 0.5) / count)
    table = np.zeros((2, DEGREE + 1, 8), np.float64)
    for row in range(1, 7):
        d = nodes * 0.5 + 0.5 - (row - 3)
        a, b = np.sinc(d), np.sinc(d / 3.0)
        da = (np.cos(np.pi * d) - a) / d
        db = (np.cos(np.pi * d / 3.0) - b) / d
        for which, values in enumerate((a * b, da * b + a * db)):
            fit = np.polynomial.chebyshev.Chebyshev.fit(nodes * 0.5, values, DEGREE, domain=[-0.5, 0.5])
            table[which, :, row] = fit.convert(kind=np.polynomial.Polynomial).coef
    return np.repeat(table.reshape(2 * (DEGREE + 1), 8, 1), 128, axis=2).astype(np.float32)


def taps_of(shift_code, stretch_code, coef_ref, slopes):
    side = 128
    centre = (side - 1) / 2.0
    lane = lax.broadcasted_iota(jnp.int32, (8, side), 1).astype(F32)
    shift = jnp.full((8, side), shift_code, jnp.int32).astype(F32) * (1.0 / 256.0)
    stretch = jnp.full((8, side), stretch_code, jnp.int32).astype(F32) * (1.0 / 51200.0)
    source = centre + (1.0 + stretch) * (lane - centre) + shift
    whole = jnp.floor(source)
    v = (source - whole) - 0.5
    found = []
    for which in range(2 if slopes else 1):
        base = which * (DEGREE + 1)
        total = coef_ref[base + DEGREE]
        for power in range(DEGREE - 1, -1, -1):
            total = total * v + coef_ref[base + power]
        found.append(total)
    return found, whole.astype(jnp.int32)


def pick(taps, index):
    numbers = lax.GatherDimensionNumbers(
        offset_dims=(),
        collapsed_slice_dims=(0,),
        start_index_map=(0,),
        operand_batching_dims=(1,),
        start_indices_batching_dims=(1,),
    )
    mode = lax.GatherScatterMode.PROMISE_IN_BOUNDS
    return lax.gather(taps, index[..., None], numbers, slice_sizes=(1, 1), mode=mode)


def spread(tap_list, whole):
    side = 128
    base = lax.broadcasted_iota(jnp.int32, (8, side), 0) + 3 - whole
    indices = [jnp.clip(base + 8 * v, 0, 7) for v in range(side // 8)]
    return [
        jnp.concatenate([pick(taps, index) for index in indices], axis=0).astype(BF16)
        for taps in tap_list
    ]


def dot(a, b):
    return jnp.dot(a, b, preferred_element_type=F32)


def dot_t(a, b):
    return lax.dot_general(a, b, (((0,), (0,)), ((), ())), preferred_element_type=F32)


def mask_rows(mask_row):
    side = mask_row.shape[1]
    first = lax.broadcasted_iota(jnp.int32, (16, side), 0) == 0
    return jnp.where(first, jnp.broadcast_to(mask_row, (16, side)), 0.0).astype(BF16)


def halves_of(first, second):
    side = first.shape[1]
    left = lax.broadcasted_iota(jnp.int32, first.shape, 1) < side // 2
    low = jnp.where(left, first, pltpu.roll(second, side // 2, 1))
    high = jnp.where(left, pltpu.roll(first, side // 2, 1), second)
    return low, high


def sums_kernel(tiles, packed, step_blocks, affine_ref, target_ref, weight_ref, coef_ref, mask_ref, block_ref, *rest):
    outs = rest[:-4]
    acc, rows_sc, cols_sc, den_sc = rest[-4:]
    step = pl.program_id(0)
    side = 128

    @pl.when(step == 0)
    def _():
        acc[...] = jnp.zeros_like(acc)
        rows_sc[...] = jnp.zeros_like(rows_sc)

    def body(group, carry):
        work = []
        for u in range(GROUP1):
            j = group * GROUP1 + u
            b = step * step_blocks + j
            mask_row = mask_ref[pl.ds(j, 1), :].astype(F32)
            masked = block_ref[j] * mask_row.astype(BF16)
            for k in range(2):
                (tap_y,), whole_y = taps_of(affine_ref[0, k, 1, b], affine_ref[0, k, 3, b], coef_ref, False)
                (tap_x,), whole_x = taps_of(affine_ref[0, k, 0, b], affine_ref[0, k, 2, b], coef_ref, False)
                work.append([b, k, mask_row, masked, tap_y, whole_y, tap_x, whole_x])
        passes = []
        for b, k, mask_row, masked, tap_y, whole_y, tap_x, whole_x in work:
            (ly_t,) = spread([tap_y], whole_y)
            passes.append(dot_t(ly_t, masked).astype(BF16))
        warps = []
        for (b, k, mask_row, masked, tap_y, whole_y, tap_x, whole_x), row_pass in zip(work, passes):
            (lx_t,) = spread([tap_x], whole_x)
            warps.append(dot(jnp.concatenate([row_pass, mask_rows(mask_row)], axis=0), lx_t))
        for (b, k, mask_row, masked, tap_y, whole_y, tap_x, whole_x), both in zip(work, warps):
            tile = target_ref[0, 0, b]
            weight = weight_ref[0, b]
            sent = (weight * both[:side]).astype(BF16).astype(F32)
            acc[k, tile] = acc[k, tile] + sent
            at = whole_y + lax.broadcasted_iota(jnp.int32, (8, side), 0) - 3
            used = jnp.where((at >= 0) & (at < side), tap_y.astype(BF16).astype(F32), 0.0)
            rows_sum = jnp.sum(used, axis=0, keepdims=True)
            rows_sc[k, tile, pl.ds(b, 1), :] = (weight * rows_sum).astype(BF16).astype(F32)
            cols_sc[k, pl.ds(b, 1), :] = both[side : side + 1].astype(BF16).astype(F32)
        return carry

    lax.fori_loop(0, step_blocks // GROUP1, body, 0)

    @pl.when(step == pl.num_programs(0) - 1)
    def _():
        for k in range(2):
            cols = cols_sc[k]
            cols = jnp.concatenate([jnp.maximum(cols, 0.0), jnp.maximum(-cols, 0.0)], axis=0).astype(BF16)

            def one(t, carry, k=k, cols=cols):
                rows = rows_sc[k, t]
                rows = jnp.concatenate([jnp.maximum(rows, 0.0), jnp.maximum(-rows, 0.0)], axis=0).astype(BF16)
                den_sc[k, t] = dot_t(rows, cols)
                return carry

            lax.fori_loop(0, tiles, one, 0, unroll=tiles if packed else 1)
        if packed:
            keep_ref, send_ref = outs
            low_end = lax.axis_index("exp") == 0
            for dz in range(tiles):
                tile = lax.rem(lax.axis_index("tx") + dz, tiles)
                for which, source in enumerate((acc, den_sc)):
                    low, high = halves_of(source[0, tile], source[1, tile])
                    keep_ref[dz, which] = jnp.where(low_end, low, high)
                    send_ref[dz, which] = jnp.where(low_end, high, low).astype(BF16)
        else:

            def whole(t, carry):
                for k in range(2):
                    outs[0][t, 0, k] = acc[k, t]
                    outs[0][t, 1, k] = den_sc[k, t]
                return carry

            lax.fori_loop(0, tiles, whole, 0)


def vmem():
    return pl.BlockSpec(memory_space=pltpu.VMEM)


def scalars(array):
    rank = array.ndim
    return pl.BlockSpec(array.shape, lambda i: (0,) * rank, memory_space=pltpu.SMEM)


def smem():
    return pl.BlockSpec(memory_space=pltpu.SMEM)


def tile_sums(affine, target, weights, coef, masks, blocks, tiles, packed):
    count, side = blocks.shape[0], blocks.shape[1]
    step_blocks = GROUP1
    if packed:
        shapes = [((tiles, 2, side, side), F32), ((tiles, 2, side, side), BF16)]
    else:
        shapes = [((tiles, 2, 2, side, side), F32)]
    return pl.pallas_call(
        functools.partial(sums_kernel, tiles, packed, step_blocks),
        grid=(count // step_blocks,),
        out_shape=[jax.ShapeDtypeStruct(*shape) for shape in shapes],
        in_specs=[
            scalars(affine),
            scalars(target),
            scalars(weights),
            pl.BlockSpec(coef.shape, lambda i: (0, 0, 0)),
            pl.BlockSpec((step_blocks, side), lambda i: (i, 0)),
            pl.BlockSpec((step_blocks, side, side), lambda i: (i, 0, 0)),
        ],
        out_specs=[pl.BlockSpec(shape, lambda i, rank=len(shape): (0,) * rank) for shape, _ in shapes],
        scratch_shapes=[
            pltpu.VMEM((2, tiles, side, side), F32),
            pltpu.VMEM((2, tiles, count, side), F32),
            pltpu.VMEM((2, count, side), F32),
            pltpu.VMEM((2, tiles, side, side), F32),
        ],
        compiler_params=pltpu.CompilerParams(vmem_limit_bytes=VMEM_BYTES),
        cost_estimate=pl.CostEstimate(flops=int(8e9), bytes_accessed=int(3e6), transcendentals=0),
        name="tile_sums",
    )(affine, target, weights, coef, masks, blocks)


def pair_kernel(keep_ref, got_ref, after_ref, *outs):
    del after_ref
    for dz, out in enumerate(outs):
        for which in range(2):
            total = keep_ref[dz, which] + got_ref[dz, which].astype(F32)
            out[which] = total.astype(out.dtype)


def pair(keep, got, after):
    tiles, _, side, _ = keep.shape
    return pl.pallas_call(
        pair_kernel,
        out_shape=[jax.ShapeDtypeStruct((2, side, side), BF16 if dz else F32) for dz in range(tiles)],
        in_specs=[vmem(), vmem(), smem()],
        out_specs=[vmem()] * tiles,
        compiler_params=pltpu.CompilerParams(vmem_limit_bytes=TINY_BYTES),
        name="pair",
    )(keep, got, after)


def moments(product_x, product_y):
    side = product_x.shape[0]
    centre = (side - 1) / 2.0
    sum_x = product_x[side - 8 : side]
    sum_y = product_y[side - 8 : side]
    later = sum_y
    for v in range(side // 8 - 2, -1, -1):
        sum_x = sum_x + product_x[8 * v : 8 * v + 8]
        sum_y = sum_y + product_y[8 * v : 8 * v + 8]
        if v:
            later = later + sum_y
    sub = lax.broadcasted_iota(jnp.int32, (8, side), 0).astype(F32) - centre
    lane = lax.broadcasted_iota(jnp.int32, (1, side), 1).astype(F32) - centre
    tilted_y = 8.0 * later + sub * sum_y
    first = jnp.sum(sum_x, axis=0, keepdims=True)
    second = jnp.sum(sum_y, axis=0, keepdims=True)
    fourth = jnp.sum(tilted_y, axis=0, keepdims=True)
    return [first, second, first * lane * (1.0 / side), fourth * (1.0 / side)]


def slopes_kernel(step_blocks, start, affine_ref, coef_ref, mask_ref, block_ref, *rest):
    slope_ref, part_ref, token_ref = rest[-3:]
    token_ref[0] = 0
    step = pl.program_id(0) + start
    side = 128

    def body(group, carry):
        ones = jnp.ones((side, side), BF16)
        work = []
        for u in range(GROUP2):
            j = group * GROUP2 + u
            b = step * step_blocks + j
            mask_row = mask_ref[pl.ds(b, 1), :].astype(F32)
            masked = block_ref[j] * mask_row.astype(BF16)
            taps = []
            for k in range(2):
                taps.append(taps_of(affine_ref[0, k, 0, b], affine_ref[0, k, 2, b], coef_ref, True))
                taps.append(taps_of(affine_ref[0, k, 1, b], affine_ref[0, k, 3, b], coef_ref, True))
            work.append([j, masked, mask_rows(mask_row), taps])
        cols, rights, rows, downs = [], [], [], []
        for j, masked, extra, taps in work:
            x0, x1 = spread(*taps[0]), spread(*taps[2])
            cols.append(dot(jnp.concatenate([masked, extra], axis=0), jnp.concatenate([x0[0], x1[0]], axis=1)))
            rights.append([jnp.concatenate(x0, axis=1), jnp.concatenate(x1, axis=1)])
        for j, masked, extra, taps in work:
            with_ones = jnp.concatenate([masked, ones], axis=1)
            y0, y1 = spread(*taps[1]), spread(*taps[3])
            rows.append([dot_t(y0[0], with_ones), dot_t(y1[0], with_ones)])
            downs.append([y0[1], y1[1]])
        late = []
        for (j, masked, extra, taps), col_both, right, row, down in zip(work, cols, rights, rows, downs):
            for k in range(2):
                row_pass = row[k][:, :side].astype(BF16)
                col_pass = col_both[:side, k * side : (k + 1) * side].astype(BF16)
                late.append((j, k, dot(row_pass, right[k]), dot_t(down[k], col_pass), row[k][:, side:], col_both[side : side + 1, k * side : (k + 1) * side]))
        for j, k, both, slope_y, rows_sum, cols_sum in late:
            warped = both[:, :side]
            weight_map = jnp.maximum(rows_sum * cols_sum, 0.0)
            value_x = weight_map * both[:, side:]
            value_y = weight_map * slope_y
            slope_ref[j, 2 * k] = value_x.astype(SLOPE)
            slope_ref[j, 2 * k + 1] = value_y.astype(SLOPE)
            for m, row in enumerate(moments(warped * value_x, warped * value_y)):
                part_ref[j, 4 * k + m : 4 * k + m + 1, :] = row
        return carry

    lax.fori_loop(0, step_blocks // GROUP2, body, 0)


def slopes_of(affine, coef, masks, blocks, first, size):
    side = blocks.shape[1]
    step_blocks = GROUP2
    start = first // step_blocks
    return pl.pallas_call(
        functools.partial(slopes_kernel, step_blocks, start),
        grid=(size // step_blocks,),
        out_shape=[
            jax.ShapeDtypeStruct((size, 4, side, side), SLOPE),
            jax.ShapeDtypeStruct((size, 8, side), F32),
            jax.ShapeDtypeStruct((1,), jnp.int32),
        ],
        in_specs=[
            scalars(affine),
            pl.BlockSpec(coef.shape, lambda i: (0, 0, 0)),
            pl.BlockSpec(masks.shape, lambda i: (0, 0)),
            pl.BlockSpec((step_blocks, side, side), lambda i: (i + start, 0, 0)),
        ],
        out_specs=[
            pl.BlockSpec((step_blocks, 4, side, side), lambda i: (i, 0, 0, 0)),
            pl.BlockSpec((step_blocks, 8, side), lambda i: (i, 0, 0)),
            smem(),
        ],
        compiler_params=pltpu.CompilerParams(vmem_limit_bytes=SMALL_BYTES),
        cost_estimate=pl.CostEstimate(flops=int(1.5e8) * size, bytes_accessed=int(3e5) * size, transcendentals=0),
        name="slopes",
    )(affine, coef, masks, blocks)


def coadd_kernel(after_ref, *refs):
    del after_ref
    parts, (piece_ref, edge_ref) = refs[:-2], refs[-2:]
    num, den = parts[0][0], parts[0][1]
    for part in parts[1:]:
        num = num + part[0].astype(F32)
        den = den + part[1].astype(F32)
    side = num.shape[1]
    left = lax.broadcasted_iota(jnp.int32, num.shape, 1) < side // 2
    first = num / (1.0 + den)
    piece = (num + jnp.where(left, 0.0, pltpu.roll(first, side // 2, 1))) / (1.0 + den)
    piece_ref[...] = piece
    flipped = jnp.transpose(piece)
    half = side // 2
    outer = jnp.concatenate([flipped[0:8], flipped[half : half + 8]], axis=0)
    inner = jnp.concatenate([flipped[half - 8 : half], flipped[side - 8 : side]], axis=0)
    edge_ref[...] = jnp.where(lax.axis_index("exp") == 0, outer, inner).astype(BF16)


def coadd_of(after, parts):
    side = parts[0].shape[2]
    return pl.pallas_call(
        coadd_kernel,
        out_shape=[jax.ShapeDtypeStruct((side, side), F32), jax.ShapeDtypeStruct((16, side), BF16)],
        in_specs=[smem()] + [vmem()] * len(parts),
        out_specs=[vmem(), vmem()],
        compiler_params=pltpu.CompilerParams(vmem_limit_bytes=TINY_BYTES),
        name="coadd",
    )(after, *parts)


def band_of(values, diagonal):
    total = jnp.zeros(diagonal.shape, F32)
    for q, value in enumerate(values):
        total = jnp.where(diagonal == q, value, total)
    high = total.astype(BF16)
    return jnp.concatenate([high, (total - high.astype(F32)).astype(BF16)], axis=1)


def bands_kernel(psf_ref, after_ref, inner_ref, outer_ref, token_ref):
    token_ref[0] = after_ref[0]
    side = inner_ref.shape[1]
    along = lax.broadcasted_iota(jnp.int32, (side, side), 0)
    across = lax.broadcasted_iota(jnp.int32, (side, side), 1)
    edge = along[:16]
    edge = jnp.where(edge < 8, edge - 8, edge + side - 8)
    for k in range(2):
        taps = [psf_ref[k, 1, q] for q in range(TAPS)]
        inner_ref[k] = band_of(taps, along - across + RAD)
        outer_ref[k] = band_of(taps, edge - across[:16] + RAD)


def bands_of(psf, after, side=128):
    return pl.pallas_call(
        bands_kernel,
        out_shape=[jax.ShapeDtypeStruct((2, rows, 2 * side), BF16) for rows in (side, 16)]
        + [jax.ShapeDtypeStruct((1,), jnp.int32)],
        in_specs=[smem(), smem()],
        out_specs=[vmem(), vmem(), smem()],
        compiler_params=pltpu.CompilerParams(vmem_limit_bytes=TINY_BYTES),
        name="bands",
    )(psf, after)


def smoothed(tile, edges, inner, outer):
    side = tile.shape[1]
    high = tile.astype(BF16)
    low = (tile - high.astype(F32)).astype(BF16)
    both = dot(high, inner) + dot_t(edges, outer)
    return both[:, :side] + both[:, side:] + dot(low, inner[:, :side])


def join_kernel(inner_ref, outer_ref, own_ref, other_ref, edge_ref, far_ref, after_ref, sky_ref, tile_ref):
    del after_ref
    here = lax.axis_index("exp") == 0
    own, other = own_ref[...], other_ref[...]
    tiles = halves_of(jnp.where(here, own, other), jnp.where(here, other, own))
    edge, far = edge_ref[...].astype(F32), far_ref[...].astype(F32)
    left, right = jnp.where(here, far, edge), jnp.where(here, edge, far)
    column = lax.axis_index("ty")
    left = jnp.where(column > 0, left, 0.0)
    right = jnp.where(column < lax.axis_size("ty") - 1, right, 0.0)
    for k in range(2):
        at = slice(8 * k, 8 * k + 8)
        edges = jnp.concatenate([left[at], right[at]], axis=0).astype(BF16)
        sky_ref[k] = smoothed(tiles[k], edges, inner_ref[k], outer_ref[k]).astype(BF16)
    tile_ref[...] = tiles[1]


def join(bands, own, other, edge, far, after):
    side = own.shape[1]
    return pl.pallas_call(
        join_kernel,
        out_shape=[jax.ShapeDtypeStruct((2, side, side), BF16), jax.ShapeDtypeStruct((side, side), F32)],
        in_specs=[vmem()] * 6 + [smem()],
        out_specs=[vmem(), vmem()],
        compiler_params=pltpu.CompilerParams(vmem_limit_bytes=TINY_BYTES),
        name="join",
    )(*bands, own, other, edge, far, after)


def whole_kernel(inner_ref, outer_ref, tile_ref, edge_ref, sky_ref):
    for k in range(2):
        sky_ref[k] = smoothed(tile_ref[k], edge_ref[k], inner_ref[k], outer_ref[k]).astype(BF16)


def whole_sky(bands, tiles, edges):
    return pl.pallas_call(
        whole_kernel,
        out_shape=jax.ShapeDtypeStruct(tiles.shape, BF16),
        in_specs=[vmem()] * 4,
        out_specs=vmem(),
        compiler_params=pltpu.CompilerParams(vmem_limit_bytes=TINY_BYTES),
        name="whole_sky",
    )(*bands, tiles, edges)


def gradient_kernel(tiles, target_ref, psf_ref, *rest):
    skies = rest[:tiles]
    chunk_refs, (out_ref, smooth, model) = rest[tiles:-3], rest[-3:]
    side = 128
    for k in range(2):
        smooth[k, 0:8, :] = jnp.zeros((8, side), F32)
        smooth[k, 8 + tiles * side : 16 + tiles * side, :] = jnp.zeros((8, side), F32)
        for turn in range(tiles):
            tile = lax.rem(lax.axis_index("tx") + tiles - turn, tiles)
            smooth[k, pl.ds(pl.multiple_of(8 + tile * side, 8), side), :] = skies[turn][k].astype(F32)
        chunk = 64

        def rows(c, carry, k=k):
            start = pl.multiple_of(c * chunk, chunk)
            seen = smooth[k, pl.ds(start, chunk + 16), :]
            total = psf_ref[k, 0, 0] * seen[4 : 4 + chunk]
            for p in range(1, TAPS):
                total = total + psf_ref[k, 0, p] * seen[4 + p : 4 + p + chunk]
            model[k, pl.ds(start, chunk), :] = total.astype(BF16).astype(F32)
            return carry

        lax.fori_loop(0, tiles * side // chunk, rows, 0, unroll=2)

    lane = lax.broadcasted_iota(jnp.int32, out_ref.shape[1:], 2)
    gathered = jnp.zeros(out_ref.shape[1:], F32)
    first = 0
    for slope_ref, part_ref in zip(chunk_refs[::2], chunk_refs[1::2]):

        def body(group, gathered, first=first, slope_ref=slope_ref, part_ref=part_ref):
            found = []
            for u in range(GROUP3):
                j = group * GROUP3 + u
                start = pl.multiple_of(target_ref[0, 0, first + j] * side, side)
                rows = []
                for k in range(2):
                    cutout = model[k, pl.ds(start, side), :]
                    slope_x, slope_y = slope_ref[j, 2 * k].astype(F32), slope_ref[j, 2 * k + 1].astype(F32)
                    rows += moments(cutout * slope_x, cutout * slope_y)
                found.append((j, rows))
            for j, rows in found:
                total = jnp.sum(part_ref[j] - jnp.concatenate(rows, axis=0), axis=1, keepdims=True) * (1.0 / side)
                gathered = jnp.where(lane == first + j, total.reshape(2, 4, 1), gathered)
            return gathered

        gathered = lax.fori_loop(0, slope_ref.shape[0] // GROUP3, body, gathered)
        first += slope_ref.shape[0]
    out_ref[0] = gathered


def gradients_of(target, psf, skies, chunks):
    side = skies[0].shape[1]
    tiles, count = len(skies), target.shape[2]
    arrays = [array for pair_of in chunks for array in pair_of]
    return pl.pallas_call(
        functools.partial(gradient_kernel, tiles),
        out_shape=jax.ShapeDtypeStruct((1, 2, 4, count), F32),
        in_specs=[smem(), smem()] + [vmem()] * (tiles + len(arrays)),
        out_specs=vmem(),
        scratch_shapes=[
            pltpu.VMEM((2, tiles * side + 16, side), F32),
            pltpu.VMEM((2, tiles * side, side), F32),
        ],
        compiler_params=pltpu.CompilerParams(vmem_limit_bytes=SMALL_BYTES),
        cost_estimate=pl.CostEstimate(flops=int(4e9), bytes_accessed=int(20e6), transcendentals=0),
        name="gradients",
    )(target, psf, *skies, *arrays)


def swap(cells):
    return lax.ppermute(cells, "exp", [(0, 1), (1, 0)])


def turned(cells, dz, tiles):
    return lax.ppermute(cells, "tx", [(z, (z + dz) % tiles) for z in range(tiles)])


def to_sides(edge, columns, flip):
    perm = [(y, flip * columns + (y - 1) % columns) for y in range(columns)]
    perm += [(columns + y, (1 - flip) * columns + (y + 1) % columns) for y in range(columns)]
    return lax.ppermute(edge, ("exp", "ty"), perm)


def local(exposures, block_tile, affine, col_mask, block_weight, psf):
    blocks = exposures[0]
    count, side = blocks.shape[0], blocks.shape[1]
    tiles, halves, columns = lax.axis_size("tx"), lax.axis_size("exp"), lax.axis_size("ty")
    coef = jnp.asarray(series())
    affine = affine.transpose(0, 2, 3, 1)
    block_tile = block_tile.transpose(0, 2, 1)
    masks = col_mask[0]
    small = halves == 2 and tiles <= 4
    sums = tile_sums(affine, block_tile, block_weight, coef, masks, blocks, tiles, small)
    chunks, tokens, first = [], [], 0
    scale = count // sum(CHUNKS)
    for size in CHUNKS:
        *found, token = slopes_of(affine, coef, masks, blocks, first, size * scale)
        chunks.append(found)
        tokens.append(token)
        first += size * scale
    if small:
        keep, send = sums
        *bands, token = bands_of(psf, tokens[0])
        totals = pair(keep, swap(send), token)
        got = [totals[0]] + [turned(totals[dz], dz, tiles) for dz in range(1, tiles)]
        piece, edge = coadd_of(tokens[1], got)
        other = swap(piece)
        near, far = to_sides(edge, columns, 0), to_sides(edge, columns, 1)
        sky, coadd_tile = join(bands, piece, other, near, far, tokens[-2])
        skies = [sky] + [turned(sky, dz, tiles) for dz in range(1, tiles)]
    else:
        me = lax.axis_index("tx")
        summed = lax.psum_scatter(sums[0], "tx", scatter_dimension=0, tiled=True)
        (num, den) = lax.psum(summed[0], "exp")
        one = num[0] / (1.0 + den[0])
        coadd_tile = (num[1] + one) / (1.0 + den[1])
        both = jnp.stack([one, coadd_tile])
        flipped = jnp.swapaxes(both, 1, 2).astype(BF16)
        left = lax.ppermute(flipped[:, side - 8 :], "ty", [(y, y + 1) for y in range(columns - 1)])
        right = lax.ppermute(flipped[:, :8], "ty", [(y + 1, y) for y in range(columns - 1)])
        sky = whole_sky(bands_of(psf, tokens[0])[:2], both, jnp.concatenate([left, right], axis=1))
        gathered = lax.all_gather(sky, "tx", axis=0)
        skies = [lax.dynamic_index_in_dim(gathered, (me + tiles - turn) % tiles, 0, False) for turn in range(tiles)]
    gradients = gradients_of(block_tile, psf, skies, chunks)
    return gradients.transpose(0, 3, 1, 2), coadd_tile


def solution(mesh):
    placed = (
        P("ty", ("exp", "tx"), None, None),
        P("ty", ("exp", "tx"), None),
        P("ty", ("exp", "tx"), None, None),
        P("ty", ("exp", "tx"), None),
        P("ty", ("exp", "tx")),
        P(),
    )
    return jax.shard_map(
        local,
        mesh=mesh,
        in_specs=placed,
        out_specs=(P("ty", ("exp", "tx"), None, None), P("tx", "ty")),
        check_vma=False,
    )
```

```python
import functools

import jax
import jax.numpy as jnp
import numpy as np
from jax import lax
from jax.experimental import pallas as pl
from jax.experimental.pallas import tpu as pltpu
from jax.sharding import PartitionSpec as P

RAD = 4
TAPS = 2 * RAD + 1
DEGREE = 10
F32 = jnp.float32
BF16 = jnp.bfloat16
GROUP1 = 8
STEP2 = 8
LAG2 = (0, 4, 8, 12)
GROUP3 = 8
CHUNKS = (24, 16, 24)
SLOPE = jnp.bfloat16
VMEM_BYTES = 56 * 1024 * 1024
SMALL_BYTES = 20 * 1024 * 1024
TINY_BYTES = 6 * 1024 * 1024


def series():
    count = 64
    nodes = np.cos(np.pi * (np.arange(count) + 0.5) / count)
    table = np.zeros((2, DEGREE + 1, 8), np.float64)
    for row in range(1, 7):
        d = nodes * 0.5 + 0.5 - (row - 3)
        a, b = np.sinc(d), np.sinc(d / 3.0)
        da = (np.cos(np.pi * d) - a) / d
        db = (np.cos(np.pi * d / 3.0) - b) / d
        for which, values in enumerate((a * b, da * b + a * db)):
            fit = np.polynomial.chebyshev.Chebyshev.fit(nodes * 0.5, values, DEGREE, domain=[-0.5, 0.5])
            table[which, :, row] = fit.convert(kind=np.polynomial.Polynomial).coef
    return np.repeat(table.reshape(2 * (DEGREE + 1), 8, 1), 128, axis=2).astype(np.float32)


def taps_of(shift_code, stretch_code, coef_ref, slopes):
    side = 128
    centre = (side - 1) / 2.0
    lane = lax.broadcasted_iota(jnp.int32, (8, side), 1).astype(F32)
    shift = jnp.full((8, side), shift_code, jnp.int32).astype(F32) * (1.0 / 256.0)
    stretch = jnp.full((8, side), stretch_code, jnp.int32).astype(F32) * (1.0 / 51200.0)
    source = centre + (1.0 + stretch) * (lane - centre) + shift
    whole = jnp.floor(source)
    v = (source - whole) - 0.5
    found = []
    for which in range(2 if slopes else 1):
        base = which * (DEGREE + 1)
        total = coef_ref[base + DEGREE]
        for power in range(DEGREE - 1, -1, -1):
            total = total * v + coef_ref[base + power]
        found.append(total)
    return found, whole.astype(jnp.int32)


def pick(taps, index):
    numbers = lax.GatherDimensionNumbers(
        offset_dims=(),
        collapsed_slice_dims=(0,),
        start_index_map=(0,),
        operand_batching_dims=(1,),
        start_indices_batching_dims=(1,),
    )
    mode = lax.GatherScatterMode.PROMISE_IN_BOUNDS
    return lax.gather(taps, index[..., None], numbers, slice_sizes=(1, 1), mode=mode)


def windows():
    sub, lane = np.arange(8)[:, None], np.arange(128)[None, :]
    rows = [8 * (3 * ((lane + 8 - 8 * r) // 24) + r) + sub + 3 for r in range(3)]
    start = np.arange(128)[:, None] // 8 * 8 - 8
    near = (lane >= start) & (lane < start + 24)
    return np.stack(rows).astype(np.int32), near.astype(np.float32)


def spread(tap_list, whole, rows_ref, near_ref):
    indices = [jnp.clip(rows_ref[r] - whole, 0, 7) for r in range(3)]
    bands = []
    for taps in tap_list:
        classes = [pick(taps, index) for index in indices]
        pairs = [
            jnp.concatenate([classes[2 * w % 3], classes[(2 * w + 1) % 3]], axis=0).astype(BF16) for w in range(3)
        ]
        bands.append(jnp.concatenate([pairs[w % 3] for w in range(8)], axis=0) * near_ref[...])
    return bands


def dot(a, b):
    return jnp.dot(a, b, preferred_element_type=F32)


def dot_t(a, b):
    return lax.dot_general(a, b, (((0,), (0,)), ((), ())), preferred_element_type=F32)


def staged(count, lags, enter, first, second, leave):
    held = [dict() for _ in range(3)]
    for turn in range(count + max(lags)):
        for stage in range(4):
            j = turn - lags[stage]
            if not 0 <= j < count:
                continue
            if stage == 0:
                held[0][j] = enter(j)
            elif stage == 1:
                held[1][j] = first(*held[0].pop(j))
            elif stage == 2:
                held[2][j] = second(*held[1].pop(j))
            else:
                leave(j, held[2].pop(j))


def mask_rows(mask_row):
    side = mask_row.shape[1]
    first = lax.broadcasted_iota(jnp.int32, (16, side), 0) == 0
    return jnp.where(first, jnp.broadcast_to(mask_row, (16, side)), 0.0).astype(BF16)


def halves_of(first, second):
    side = first.shape[1]
    left = lax.broadcasted_iota(jnp.int32, first.shape, 1) < side // 2
    low = jnp.where(left, first, pltpu.roll(second, side // 2, 1))
    high = jnp.where(left, pltpu.roll(first, side // 2, 1), second)
    return low, high


def sums_kernel(tiles, packed, step_blocks, affine_ref, target_ref, weight_ref, coef_ref, rows_ref, near_ref, mask_ref, block_ref, *rest):
    outs = rest[:-4]
    acc, rows_sc, cols_sc, den_sc = rest[-4:]
    step = pl.program_id(0)
    side = 128

    @pl.when(step == 0)
    def _():
        acc[...] = jnp.zeros_like(acc)
        rows_sc[...] = jnp.zeros_like(rows_sc)

    def body(group, carry):
        work = []
        for u in range(GROUP1):
            j = group * GROUP1 + u
            b = step * step_blocks + j
            mask_row = mask_ref[pl.ds(j, 1), :].astype(F32)
            masked = block_ref[j] * mask_row.astype(BF16)
            for k in range(2):
                (tap_y,), whole_y = taps_of(affine_ref[0, k, 1, b], affine_ref[0, k, 3, b], coef_ref, False)
                (tap_x,), whole_x = taps_of(affine_ref[0, k, 0, b], affine_ref[0, k, 2, b], coef_ref, False)
                work.append([b, k, mask_row, masked, tap_y, whole_y, tap_x, whole_x])
        passes = []
        for b, k, mask_row, masked, tap_y, whole_y, tap_x, whole_x in work:
            (ly_t,) = spread([tap_y], whole_y, rows_ref, near_ref)
            passes.append(dot_t(ly_t, masked).astype(BF16))
        warps = []
        for (b, k, mask_row, masked, tap_y, whole_y, tap_x, whole_x), row_pass in zip(work, passes):
            (lx_t,) = spread([tap_x], whole_x, rows_ref, near_ref)
            warps.append(dot(jnp.concatenate([row_pass, mask_rows(mask_row)], axis=0), lx_t))
        for (b, k, mask_row, masked, tap_y, whole_y, tap_x, whole_x), both in zip(work, warps):
            tile = target_ref[0, 0, b]
            weight = weight_ref[0, b]
            sent = (weight * both[:side]).astype(BF16).astype(F32)
            acc[k, tile] = acc[k, tile] + sent
            at = whole_y + lax.broadcasted_iota(jnp.int32, (8, side), 0) - 3
            used = jnp.where((at >= 0) & (at < side), tap_y.astype(BF16).astype(F32), 0.0)
            rows_sum = jnp.sum(used, axis=0, keepdims=True)
            rows_sc[k, tile, pl.ds(b, 1), :] = (weight * rows_sum).astype(BF16).astype(F32)
            cols_sc[k, pl.ds(b, 1), :] = both[side : side + 1].astype(BF16).astype(F32)
        return carry

    lax.fori_loop(0, step_blocks // GROUP1, body, 0)

    @pl.when(step == pl.num_programs(0) - 1)
    def _():
        for k in range(2):
            cols = cols_sc[k]
            cols = jnp.concatenate([jnp.maximum(cols, 0.0), jnp.maximum(-cols, 0.0)], axis=0).astype(BF16)

            def one(t, carry, k=k, cols=cols):
                rows = rows_sc[k, t]
                rows = jnp.concatenate([jnp.maximum(rows, 0.0), jnp.maximum(-rows, 0.0)], axis=0).astype(BF16)
                den_sc[k, t] = dot_t(rows, cols)
                return carry

            lax.fori_loop(0, tiles, one, 0, unroll=tiles if packed else 1)
        if packed:
            keep_ref, send_ref = outs
            low_end = lax.axis_index("exp") == 0
            for dz in range(tiles):
                tile = lax.rem(lax.axis_index("tx") + dz, tiles)
                for which, source in enumerate((acc, den_sc)):
                    low, high = halves_of(source[0, tile], source[1, tile])
                    keep_ref[dz, which] = jnp.where(low_end, low, high)
                    send_ref[dz, which] = jnp.where(low_end, high, low).astype(BF16)
        else:

            def whole(t, carry):
                for k in range(2):
                    outs[0][t, 0, k] = acc[k, t]
                    outs[0][t, 1, k] = den_sc[k, t]
                return carry

            lax.fori_loop(0, tiles, whole, 0)


def vmem():
    return pl.BlockSpec(memory_space=pltpu.VMEM)


def scalars(array):
    rank = array.ndim
    return pl.BlockSpec(array.shape, lambda i: (0,) * rank, memory_space=pltpu.SMEM)


def smem():
    return pl.BlockSpec(memory_space=pltpu.SMEM)


def tile_sums(affine, target, weights, coef, masks, blocks, tiles, packed):
    count, side = blocks.shape[0], blocks.shape[1]
    step_blocks = GROUP1
    if packed:
        shapes = [((tiles, 2, side, side), F32), ((tiles, 2, side, side), BF16)]
    else:
        shapes = [((tiles, 2, 2, side, side), F32)]
    return pl.pallas_call(
        functools.partial(sums_kernel, tiles, packed, step_blocks),
        grid=(count // step_blocks,),
        out_shape=[jax.ShapeDtypeStruct(*shape) for shape in shapes],
        in_specs=[
            scalars(affine),
            scalars(target),
            scalars(weights),
            *[pl.BlockSpec(c.shape, lambda i, rank=c.ndim: (0,) * rank) for c in coef],
            pl.BlockSpec((step_blocks, side), lambda i: (i, 0)),
            pl.BlockSpec((step_blocks, side, side), lambda i: (i, 0, 0)),
        ],
        out_specs=[pl.BlockSpec(shape, lambda i, rank=len(shape): (0,) * rank) for shape, _ in shapes],
        scratch_shapes=[
            pltpu.VMEM((2, tiles, side, side), F32),
            pltpu.VMEM((2, tiles, count, side), F32),
            pltpu.VMEM((2, count, side), F32),
            pltpu.VMEM((2, tiles, side, side), F32),
        ],
        compiler_params=pltpu.CompilerParams(vmem_limit_bytes=VMEM_BYTES),
        cost_estimate=pl.CostEstimate(flops=int(8e9), bytes_accessed=int(3e6), transcendentals=0),
        name="tile_sums",
    )(affine, target, weights, *coef, masks, blocks)


def pair_kernel(keep_ref, got_ref, after_ref, *outs):
    del after_ref
    for dz, out in enumerate(outs):
        for which in range(2):
            total = keep_ref[dz, which] + got_ref[dz, which].astype(F32)
            out[which] = total.astype(out.dtype)


def pair(keep, got, after):
    tiles, _, side, _ = keep.shape
    return pl.pallas_call(
        pair_kernel,
        out_shape=[jax.ShapeDtypeStruct((2, side, side), BF16 if dz else F32) for dz in range(tiles)],
        in_specs=[vmem(), vmem(), smem()],
        out_specs=[vmem()] * tiles,
        compiler_params=pltpu.CompilerParams(vmem_limit_bytes=TINY_BYTES),
        name="pair",
    )(keep, got, after)


def moments(product_x, product_y):
    side = product_x.shape[0]
    centre = (side - 1) / 2.0
    sum_x = product_x[side - 8 : side]
    sum_y = product_y[side - 8 : side]
    later = sum_y
    for v in range(side // 8 - 2, -1, -1):
        sum_x = sum_x + product_x[8 * v : 8 * v + 8]
        sum_y = sum_y + product_y[8 * v : 8 * v + 8]
        if v:
            later = later + sum_y
    sub = lax.broadcasted_iota(jnp.int32, (8, side), 0).astype(F32) - centre
    lane = lax.broadcasted_iota(jnp.int32, (1, side), 1).astype(F32) - centre
    tilted_y = 8.0 * later + sub * sum_y
    first = jnp.sum(sum_x, axis=0, keepdims=True)
    second = jnp.sum(sum_y, axis=0, keepdims=True)
    fourth = jnp.sum(tilted_y, axis=0, keepdims=True)
    return [first, second, first * lane * (1.0 / side), fourth * (1.0 / side)]


def slopes_kernel(step_blocks, start, affine_ref, coef_ref, rows_ref, near_ref, mask_ref, block_ref, *rest):
    slope_ref, part_ref, token_ref = rest[-3:]
    token_ref[0] = 0
    step = pl.program_id(0) + start
    side = 128

    ones = jnp.ones((side, side), BF16)

    def enter(j):
        b = step * step_blocks + j
        mask_row = mask_ref[pl.ds(b, 1), :].astype(F32)
        masked = block_ref[j] * mask_row.astype(BF16)
        taps = []
        for k in range(2):
            taps.append(taps_of(affine_ref[0, k, 0, b], affine_ref[0, k, 2, b], coef_ref, True))
            taps.append(taps_of(affine_ref[0, k, 1, b], affine_ref[0, k, 3, b], coef_ref, True))
        return masked, mask_rows(mask_row), taps

    def first(masked, extra, taps):
        x0, x1 = spread(*taps[0], rows_ref, near_ref), spread(*taps[2], rows_ref, near_ref)
        col_both = dot(jnp.concatenate([masked, extra], axis=0), jnp.concatenate([x0[0], x1[0]], axis=1))
        y0, y1 = spread(*taps[1], rows_ref, near_ref), spread(*taps[3], rows_ref, near_ref)
        with_ones = jnp.concatenate([masked, ones], axis=1)
        rights = [jnp.concatenate(x0, axis=1), jnp.concatenate(x1, axis=1)]
        return col_both, [dot_t(y0[0], with_ones), dot_t(y1[0], with_ones)], rights, [y0[1], y1[1]]

    def second(col_both, rows, rights, downs):
        found = []
        for k in range(2):
            row_pass = rows[k][:, :side].astype(BF16)
            col_pass = col_both[:side, k * side : (k + 1) * side].astype(BF16)
            cols_sum = col_both[side : side + 1, k * side : (k + 1) * side]
            found.append((dot(row_pass, rights[k]), dot_t(downs[k], col_pass), rows[k][:, side:], cols_sum))
        return found

    def leave(j, found):
        for k, (both, slope_y, rows_sum, cols_sum) in enumerate(found):
            weight_map = jnp.maximum(rows_sum * cols_sum, 0.0)
            value_x = weight_map * both[:, side:]
            value_y = weight_map * slope_y
            slope_ref[j, 2 * k] = value_x.astype(SLOPE)
            slope_ref[j, 2 * k + 1] = value_y.astype(SLOPE)
            warped = both[:, :side]
            for m, row in enumerate(moments(warped * value_x, warped * value_y)):
                part_ref[j, 4 * k + m : 4 * k + m + 1, :] = row

    staged(step_blocks, LAG2, enter, first, second, leave)


def slopes_of(affine, coef, masks, blocks, first, size):
    side = blocks.shape[1]
    step_blocks = STEP2
    start = first // step_blocks
    return pl.pallas_call(
        functools.partial(slopes_kernel, step_blocks, start),
        grid=(size // step_blocks,),
        out_shape=[
            jax.ShapeDtypeStruct((size, 4, side, side), SLOPE),
            jax.ShapeDtypeStruct((size, 8, side), F32),
            jax.ShapeDtypeStruct((1,), jnp.int32),
        ],
        in_specs=[
            scalars(affine),
            *[pl.BlockSpec(c.shape, lambda i, rank=c.ndim: (0,) * rank) for c in coef],
            pl.BlockSpec(masks.shape, lambda i: (0, 0)),
            pl.BlockSpec((step_blocks, side, side), lambda i: (i + start, 0, 0)),
        ],
        out_specs=[
            pl.BlockSpec((step_blocks, 4, side, side), lambda i: (i, 0, 0, 0)),
            pl.BlockSpec((step_blocks, 8, side), lambda i: (i, 0, 0)),
            smem(),
        ],
        compiler_params=pltpu.CompilerParams(vmem_limit_bytes=SMALL_BYTES),
        cost_estimate=pl.CostEstimate(flops=int(1.5e8) * size, bytes_accessed=int(3e5) * size, transcendentals=0),
        name="slopes",
    )(affine, *coef, masks, blocks)


def coadd_kernel(after_ref, *refs):
    del after_ref
    parts, (piece_ref, edge_ref) = refs[:-2], refs[-2:]
    num, den = parts[0][0], parts[0][1]
    for part in parts[1:]:
        num = num + part[0].astype(F32)
        den = den + part[1].astype(F32)
    side = num.shape[1]
    left = lax.broadcasted_iota(jnp.int32, num.shape, 1) < side // 2
    first = num / (1.0 + den)
    piece = (num + jnp.where(left, 0.0, pltpu.roll(first, side // 2, 1))) / (1.0 + den)
    piece_ref[...] = piece
    flipped = jnp.transpose(piece)
    half = side // 2
    outer = jnp.concatenate([flipped[0:8], flipped[half : half + 8]], axis=0)
    inner = jnp.concatenate([flipped[half - 8 : half], flipped[side - 8 : side]], axis=0)
    edge_ref[...] = jnp.where(lax.axis_index("exp") == 0, outer, inner).astype(BF16)


def coadd_of(after, parts):
    side = parts[0].shape[2]
    return pl.pallas_call(
        coadd_kernel,
        out_shape=[jax.ShapeDtypeStruct((side, side), F32), jax.ShapeDtypeStruct((16, side), BF16)],
        in_specs=[smem()] + [vmem()] * len(parts),
        out_specs=[vmem(), vmem()],
        compiler_params=pltpu.CompilerParams(vmem_limit_bytes=TINY_BYTES),
        name="coadd",
    )(after, *parts)


def band_of(values, diagonal):
    total = jnp.zeros(diagonal.shape, F32)
    for q, value in enumerate(values):
        total = jnp.where(diagonal == q, value, total)
    high = total.astype(BF16)
    return jnp.concatenate([high, (total - high.astype(F32)).astype(BF16)], axis=1)


def bands_kernel(psf_ref, after_ref, inner_ref, outer_ref, token_ref):
    token_ref[0] = after_ref[0]
    side = inner_ref.shape[1]
    along = lax.broadcasted_iota(jnp.int32, (side, side), 0)
    across = lax.broadcasted_iota(jnp.int32, (side, side), 1)
    edge = along[:16]
    edge = jnp.where(edge < 8, edge - 8, edge + side - 8)
    for k in range(2):
        taps = [psf_ref[k, 1, q] for q in range(TAPS)]
        inner_ref[k] = band_of(taps, along - across + RAD)
        outer_ref[k] = band_of(taps, edge - across[:16] + RAD)


def bands_of(psf, after, side=128):
    return pl.pallas_call(
        bands_kernel,
        out_shape=[jax.ShapeDtypeStruct((2, rows, 2 * side), BF16) for rows in (side, 16)]
        + [jax.ShapeDtypeStruct((1,), jnp.int32)],
        in_specs=[smem(), smem()],
        out_specs=[vmem(), vmem(), smem()],
        compiler_params=pltpu.CompilerParams(vmem_limit_bytes=TINY_BYTES),
        name="bands",
    )(psf, after)


def smoothed(tile, edges, inner, outer):
    side = tile.shape[1]
    high = tile.astype(BF16)
    low = (tile - high.astype(F32)).astype(BF16)
    both = dot(high, inner) + dot_t(edges, outer)
    return both[:, :side] + both[:, side:] + dot(low, inner[:, :side])


def join_kernel(inner_ref, outer_ref, own_ref, other_ref, edge_ref, far_ref, after_ref, sky_ref, tile_ref):
    del after_ref
    here = lax.axis_index("exp") == 0
    own, other = own_ref[...], other_ref[...]
    tiles = halves_of(jnp.where(here, own, other), jnp.where(here, other, own))
    edge, far = edge_ref[...].astype(F32), far_ref[...].astype(F32)
    left, right = jnp.where(here, far, edge), jnp.where(here, edge, far)
    column = lax.axis_index("ty")
    left = jnp.where(column > 0, left, 0.0)
    right = jnp.where(column < lax.axis_size("ty") - 1, right, 0.0)
    for k in range(2):
        at = slice(8 * k, 8 * k + 8)
        edges = jnp.concatenate([left[at], right[at]], axis=0).astype(BF16)
        sky_ref[k] = smoothed(tiles[k], edges, inner_ref[k], outer_ref[k]).astype(BF16)
    tile_ref[...] = tiles[1]


def join(bands, own, other, edge, far, after):
    side = own.shape[1]
    return pl.pallas_call(
        join_kernel,
        out_shape=[jax.ShapeDtypeStruct((2, side, side), BF16), jax.ShapeDtypeStruct((side, side), F32)],
        in_specs=[vmem()] * 6 + [smem()],
        out_specs=[vmem(), vmem()],
        compiler_params=pltpu.CompilerParams(vmem_limit_bytes=TINY_BYTES),
        name="join",
    )(*bands, own, other, edge, far, after)


def whole_kernel(inner_ref, outer_ref, tile_ref, edge_ref, sky_ref):
    for k in range(2):
        sky_ref[k] = smoothed(tile_ref[k], edge_ref[k], inner_ref[k], outer_ref[k]).astype(BF16)


def whole_sky(bands, tiles, edges):
    return pl.pallas_call(
        whole_kernel,
        out_shape=jax.ShapeDtypeStruct(tiles.shape, BF16),
        in_specs=[vmem()] * 4,
        out_specs=vmem(),
        compiler_params=pltpu.CompilerParams(vmem_limit_bytes=TINY_BYTES),
        name="whole_sky",
    )(*bands, tiles, edges)


def gradient_kernel(tiles, target_ref, psf_ref, *rest):
    skies = rest[:tiles]
    chunk_refs, (out_ref, smooth, model) = rest[tiles:-3], rest[-3:]
    side = 128
    for k in range(2):
        smooth[k, 0:8, :] = jnp.zeros((8, side), F32)
        smooth[k, 8 + tiles * side : 16 + tiles * side, :] = jnp.zeros((8, side), F32)
        for turn in range(tiles):
            tile = lax.rem(lax.axis_index("tx") + tiles - turn, tiles)
            smooth[k, pl.ds(pl.multiple_of(8 + tile * side, 8), side), :] = skies[turn][k].astype(F32)
        chunk = 64

        def rows(c, carry, k=k):
            start = pl.multiple_of(c * chunk, chunk)
            seen = smooth[k, pl.ds(start, chunk + 16), :]
            total = psf_ref[k, 0, 0] * seen[4 : 4 + chunk]
            for p in range(1, TAPS):
                total = total + psf_ref[k, 0, p] * seen[4 + p : 4 + p + chunk]
            model[k, pl.ds(start, chunk), :] = total.astype(BF16).astype(F32)
            return carry

        lax.fori_loop(0, tiles * side // chunk, rows, 0, unroll=2)

    lane = lax.broadcasted_iota(jnp.int32, out_ref.shape[1:], 2)
    gathered = jnp.zeros(out_ref.shape[1:], F32)
    first = 0
    for slope_ref, part_ref in zip(chunk_refs[::2], chunk_refs[1::2]):

        def body(group, gathered, first=first, slope_ref=slope_ref, part_ref=part_ref):
            found = []
            for u in range(GROUP3):
                j = group * GROUP3 + u
                start = pl.multiple_of(target_ref[0, 0, first + j] * side, side)
                rows = []
                for k in range(2):
                    cutout = model[k, pl.ds(start, side), :]
                    slope_x, slope_y = slope_ref[j, 2 * k].astype(F32), slope_ref[j, 2 * k + 1].astype(F32)
                    rows += moments(cutout * slope_x, cutout * slope_y)
                found.append((j, rows))
            for j, rows in found:
                total = jnp.sum(part_ref[j] - jnp.concatenate(rows, axis=0), axis=1, keepdims=True) * (1.0 / side)
                gathered = jnp.where(lane == first + j, total.reshape(2, 4, 1), gathered)
            return gathered

        gathered = lax.fori_loop(0, slope_ref.shape[0] // GROUP3, body, gathered)
        first += slope_ref.shape[0]
    out_ref[0] = gathered


def gradients_of(target, psf, skies, chunks):
    side = skies[0].shape[1]
    tiles, count = len(skies), target.shape[2]
    arrays = [array for pair_of in chunks for array in pair_of]
    return pl.pallas_call(
        functools.partial(gradient_kernel, tiles),
        out_shape=jax.ShapeDtypeStruct((1, 2, 4, count), F32),
        in_specs=[smem(), smem()] + [vmem()] * (tiles + len(arrays)),
        out_specs=vmem(),
        scratch_shapes=[
            pltpu.VMEM((2, tiles * side + 16, side), F32),
            pltpu.VMEM((2, tiles * side, side), F32),
        ],
        compiler_params=pltpu.CompilerParams(vmem_limit_bytes=SMALL_BYTES),
        cost_estimate=pl.CostEstimate(flops=int(4e9), bytes_accessed=int(20e6), transcendentals=0),
        name="gradients",
    )(target, psf, *skies, *arrays)


def swap(cells):
    return lax.ppermute(cells, "exp", [(0, 1), (1, 0)])


def turned(cells, dz, tiles):
    return lax.ppermute(cells, "tx", [(z, (z + dz) % tiles) for z in range(tiles)])


def to_sides(edge, columns, flip):
    perm = [(y, flip * columns + (y - 1) % columns) for y in range(columns)]
    perm += [(columns + y, (1 - flip) * columns + (y + 1) % columns) for y in range(columns)]
    return lax.ppermute(edge, ("exp", "ty"), perm)


def local(exposures, block_tile, affine, col_mask, block_weight, psf):
    blocks = exposures[0]
    count, side = blocks.shape[0], blocks.shape[1]
    tiles, halves, columns = lax.axis_size("tx"), lax.axis_size("exp"), lax.axis_size("ty")
    rows, near = windows()
    coef = (jnp.asarray(series()), jnp.asarray(rows), jnp.asarray(near, BF16))
    affine = affine.transpose(0, 2, 3, 1)
    block_tile = block_tile.transpose(0, 2, 1)
    masks = col_mask[0]
    small = halves == 2 and tiles <= 4
    sums = tile_sums(affine, block_tile, block_weight, coef, masks, blocks, tiles, small)
    chunks, tokens, first = [], [], 0
    scale = count // sum(CHUNKS)
    for size in CHUNKS:
        *found, token = slopes_of(affine, coef, masks, blocks, first, size * scale)
        chunks.append(found)
        tokens.append(token)
        first += size * scale
    if small:
        keep, send = sums
        *bands, token = bands_of(psf, tokens[0])
        totals = pair(keep, swap(send), token)
        got = [totals[0]] + [turned(totals[dz], dz, tiles) for dz in range(1, tiles)]
        piece, edge = coadd_of(tokens[1], got)
        other = swap(piece)
        near, far = to_sides(edge, columns, 0), to_sides(edge, columns, 1)
        sky, coadd_tile = join(bands, piece, other, near, far, tokens[-2])
        skies = [sky] + [turned(sky, dz, tiles) for dz in range(1, tiles)]
    else:
        me = lax.axis_index("tx")
        summed = lax.psum_scatter(sums[0], "tx", scatter_dimension=0, tiled=True)
        (num, den) = lax.psum(summed[0], "exp")
        one = num[0] / (1.0 + den[0])
        coadd_tile = (num[1] + one) / (1.0 + den[1])
        both = jnp.stack([one, coadd_tile])
        flipped = jnp.swapaxes(both, 1, 2).astype(BF16)
        left = lax.ppermute(flipped[:, side - 8 :], "ty", [(y, y + 1) for y in range(columns - 1)])
        right = lax.ppermute(flipped[:, :8], "ty", [(y + 1, y) for y in range(columns - 1)])
        sky = whole_sky(bands_of(psf, tokens[0])[:2], both, jnp.concatenate([left, right], axis=1))
        gathered = lax.all_gather(sky, "tx", axis=0)
        skies = [lax.dynamic_index_in_dim(gathered, (me + tiles - turn) % tiles, 0, False) for turn in range(tiles)]
    gradients = gradients_of(block_tile, psf, skies, chunks)
    return gradients.transpose(0, 3, 1, 2), coadd_tile


def solution(mesh):
    placed = (
        P("ty", ("exp", "tx"), None, None),
        P("ty", ("exp", "tx"), None),
        P("ty", ("exp", "tx"), None, None),
        P("ty", ("exp", "tx"), None),
        P("ty", ("exp", "tx")),
        P(),
    )
    return jax.shard_map(
        local,
        mesh=mesh,
        in_specs=placed,
        out_specs=(P("ty", ("exp", "tx"), None, None), P("tx", "ty")),
        check_vma=False,
    )
```

```python
import functools

import jax
import jax.numpy as jnp
import numpy as np
from jax import lax
from jax.experimental import pallas as pl
from jax.experimental.pallas import tpu as pltpu
from jax.sharding import PartitionSpec as P

RAD = 4
TAPS = 2 * RAD + 1
DEGREE = 10
F32 = jnp.float32
BF16 = jnp.bfloat16
GROUP1 = 16
STEP2 = 8
LAG2 = (0, 4, 8, 12)
GROUP3 = 8
CHUNKS = (24, 16, 24)
SLOPE = jnp.bfloat16
VMEM_BYTES = 56 * 1024 * 1024
SMALL_BYTES = 20 * 1024 * 1024
TINY_BYTES = 6 * 1024 * 1024


def series():
    count = 64
    nodes = np.cos(np.pi * (np.arange(count) + 0.5) / count)
    table = np.zeros((2, DEGREE + 1, 8), np.float64)
    for row in range(1, 7):
        d = nodes * 0.5 + 0.5 - (row - 3)
        a, b = np.sinc(d), np.sinc(d / 3.0)
        da = (np.cos(np.pi * d) - a) / d
        db = (np.cos(np.pi * d / 3.0) - b) / d
        for which, values in enumerate((a * b, da * b + a * db)):
            fit = np.polynomial.chebyshev.Chebyshev.fit(nodes * 0.5, values, DEGREE, domain=[-0.5, 0.5])
            table[which, :, row] = fit.convert(kind=np.polynomial.Polynomial).coef
    return np.repeat(table.reshape(2 * (DEGREE + 1), 8, 1), 128, axis=2).astype(np.float32)


def taps_of(shift_code, stretch_code, coef_ref, slopes):
    side = 128
    centre = (side - 1) / 2.0
    lane = lax.broadcasted_iota(jnp.int32, (8, side), 1).astype(F32)
    shift = jnp.full((8, side), shift_code, jnp.int32).astype(F32) * (1.0 / 256.0)
    stretch = jnp.full((8, side), stretch_code, jnp.int32).astype(F32) * (1.0 / 51200.0)
    source = centre + (1.0 + stretch) * (lane - centre) + shift
    whole = jnp.floor(source)
    v = (source - whole) - 0.5
    found = []
    for which in range(2 if slopes else 1):
        base = which * (DEGREE + 1)
        total = coef_ref[base + DEGREE]
        for power in range(DEGREE - 1, -1, -1):
            total = total * v + coef_ref[base + power]
        found.append(total)
    return found, whole.astype(jnp.int32)


def pick(taps, index):
    numbers = lax.GatherDimensionNumbers(
        offset_dims=(),
        collapsed_slice_dims=(0,),
        start_index_map=(0,),
        operand_batching_dims=(1,),
        start_indices_batching_dims=(1,),
    )
    mode = lax.GatherScatterMode.PROMISE_IN_BOUNDS
    return lax.gather(taps, index[..., None], numbers, slice_sizes=(1, 1), mode=mode)


def windows():
    sub, lane = np.arange(8)[:, None], np.arange(128)[None, :]
    rows = [8 * (3 * ((lane + 8 - 8 * r) // 24) + r) + sub + 3 for r in range(3)]
    start = np.arange(128)[:, None] // 8 * 8 - 8
    near = (lane >= start) & (lane < start + 24)
    return np.stack(rows).astype(np.int32), near.astype(np.float32)


def spread(tap_list, whole, rows_ref, near_ref):
    indices = [jnp.clip(rows_ref[r] - whole, 0, 7) for r in range(3)]
    bands = []
    for taps in tap_list:
        classes = [pick(taps, index) for index in indices]
        pairs = [
            jnp.concatenate([classes[2 * w % 3], classes[(2 * w + 1) % 3]], axis=0).astype(BF16) for w in range(3)
        ]
        bands.append(jnp.concatenate([pairs[w % 3] for w in range(8)], axis=0) * near_ref[...])
    return bands


def dot(a, b):
    return jnp.dot(a, b, preferred_element_type=F32)


def dot_t(a, b):
    return lax.dot_general(a, b, (((0,), (0,)), ((), ())), preferred_element_type=F32)


def staged(count, lags, enter, first, second, leave):
    held = [dict() for _ in range(3)]
    for turn in range(count + max(lags)):
        for stage in range(4):
            j = turn - lags[stage]
            if not 0 <= j < count:
                continue
            if stage == 0:
                held[0][j] = enter(j)
            elif stage == 1:
                held[1][j] = first(*held[0].pop(j))
            elif stage == 2:
                held[2][j] = second(*held[1].pop(j))
            else:
                leave(j, held[2].pop(j))


def mask_rows(mask_row):
    side = mask_row.shape[1]
    first = lax.broadcasted_iota(jnp.int32, (16, side), 0) == 0
    return jnp.where(first, jnp.broadcast_to(mask_row, (16, side)), 0.0).astype(BF16)


def halves_of(first, second):
    side = first.shape[1]
    left = lax.broadcasted_iota(jnp.int32, first.shape, 1) < side // 2
    low = jnp.where(left, first, pltpu.roll(second, side // 2, 1))
    high = jnp.where(left, pltpu.roll(first, side // 2, 1), second)
    return low, high


def sums_kernel(tiles, packed, step_blocks, affine_ref, target_ref, weight_ref, coef_ref, rows_ref, near_ref, mask_ref, block_ref, *rest):
    outs = rest[:-4]
    acc, rows_sc, cols_sc, den_sc = rest[-4:]
    step = pl.program_id(0)
    side = 128

    @pl.when(step == 0)
    def _():
        acc[...] = jnp.zeros_like(acc)
        rows_sc[...] = jnp.zeros_like(rows_sc)

    def body(group, carry):
        work = []
        for u in range(GROUP1):
            j = group * GROUP1 + u
            b = step * step_blocks + j
            mask_row = mask_ref[pl.ds(j, 1), :].astype(F32)
            masked = block_ref[j] * mask_row.astype(BF16)
            for k in range(2):
                (tap_y,), whole_y = taps_of(affine_ref[0, k, 1, b], affine_ref[0, k, 3, b], coef_ref, False)
                (tap_x,), whole_x = taps_of(affine_ref[0, k, 0, b], affine_ref[0, k, 2, b], coef_ref, False)
                work.append([b, k, mask_row, masked, tap_y, whole_y, tap_x, whole_x])
        zero = jnp.zeros((side, side), BF16)

        def corner(a, c):
            return jnp.concatenate([jnp.concatenate([a, zero], axis=1), jnp.concatenate([zero, c], axis=1)], axis=0)

        duos = [(work[4 * g + k], work[4 * g + 2 + k]) for g in range(GROUP1 // 2) for k in range(2)]
        passes = []
        for one, two in duos:
            (ly_a,) = spread([one[4]], one[5], rows_ref, near_ref)
            (ly_b,) = spread([two[4]], two[5], rows_ref, near_ref)
            both = dot_t(jnp.concatenate([ly_a, ly_b], axis=0), corner(one[3], two[3]))
            passes.append(both.astype(BF16))
        warps = {}
        for (one, two), row_pass in zip(duos, passes):
            (lx_a,) = spread([one[6]], one[7], rows_ref, near_ref)
            (lx_b,) = spread([two[6]], two[7], rows_ref, near_ref)
            extra = jnp.concatenate([mask_rows(one[2]), mask_rows(two[2])], axis=1)
            both = dot(jnp.concatenate([row_pass, extra], axis=0), corner(lx_a, lx_b))
            warps[id(one)], warps[id(two)] = both[:, :side], both[:, side:]
        warps = [warps[id(item)] for item in work]
        for (b, k, mask_row, masked, tap_y, whole_y, tap_x, whole_x), both in zip(work, warps):
            tile = target_ref[0, 0, b]
            weight = weight_ref[0, b]
            sent = (weight * both[:side]).astype(BF16).astype(F32)
            acc[k, tile] = acc[k, tile] + sent
            at = whole_y + lax.broadcasted_iota(jnp.int32, (8, side), 0) - 3
            used = jnp.where((at >= 0) & (at < side), tap_y.astype(BF16).astype(F32), 0.0)
            rows_sum = jnp.sum(used, axis=0, keepdims=True)
            rows_sc[k, tile, pl.ds(b, 1), :] = (weight * rows_sum).astype(BF16).astype(F32)
            cols_sc[k, pl.ds(b, 1), :] = both[side : side + 1].astype(BF16).astype(F32)
        return carry

    lax.fori_loop(0, step_blocks // GROUP1, body, 0)

    @pl.when(step == pl.num_programs(0) - 1)
    def _():
        for k in range(2):
            cols = cols_sc[k]
            cols = jnp.concatenate([jnp.maximum(cols, 0.0), jnp.maximum(-cols, 0.0)], axis=0).astype(BF16)

            def one(t, carry, k=k, cols=cols):
                rows = rows_sc[k, t]
                rows = jnp.concatenate([jnp.maximum(rows, 0.0), jnp.maximum(-rows, 0.0)], axis=0).astype(BF16)
                den_sc[k, t] = dot_t(rows, cols)
                return carry

            lax.fori_loop(0, tiles, one, 0, unroll=tiles if packed else 1)
        if packed:
            keep_ref, send_ref = outs
            low_end = lax.axis_index("exp") == 0
            for dz in range(tiles):
                tile = lax.rem(lax.axis_index("tx") + dz, tiles)
                for which, source in enumerate((acc, den_sc)):
                    low, high = halves_of(source[0, tile], source[1, tile])
                    keep_ref[dz, which] = jnp.where(low_end, low, high)
                    send_ref[dz, which] = jnp.where(low_end, high, low).astype(BF16)
        else:

            def whole(t, carry):
                for k in range(2):
                    outs[0][t, 0, k] = acc[k, t]
                    outs[0][t, 1, k] = den_sc[k, t]
                return carry

            lax.fori_loop(0, tiles, whole, 0)


def vmem():
    return pl.BlockSpec(memory_space=pltpu.VMEM)


def scalars(array):
    rank = array.ndim
    return pl.BlockSpec(array.shape, lambda i: (0,) * rank, memory_space=pltpu.SMEM)


def smem():
    return pl.BlockSpec(memory_space=pltpu.SMEM)


def tile_sums(affine, target, weights, coef, masks, blocks, tiles, packed):
    count, side = blocks.shape[0], blocks.shape[1]
    step_blocks = GROUP1
    if packed:
        shapes = [((tiles, 2, side, side), F32), ((tiles, 2, side, side), BF16)]
    else:
        shapes = [((tiles, 2, 2, side, side), F32)]
    return pl.pallas_call(
        functools.partial(sums_kernel, tiles, packed, step_blocks),
        grid=(count // step_blocks,),
        out_shape=[jax.ShapeDtypeStruct(*shape) for shape in shapes],
        in_specs=[
            scalars(affine),
            scalars(target),
            scalars(weights),
            *[pl.BlockSpec(c.shape, lambda i, rank=c.ndim: (0,) * rank) for c in coef],
            pl.BlockSpec((step_blocks, side), lambda i: (i, 0)),
            pl.BlockSpec((step_blocks, side, side), lambda i: (i, 0, 0)),
        ],
        out_specs=[pl.BlockSpec(shape, lambda i, rank=len(shape): (0,) * rank) for shape, _ in shapes],
        scratch_shapes=[
            pltpu.VMEM((2, tiles, side, side), F32),
            pltpu.VMEM((2, tiles, count, side), F32),
            pltpu.VMEM((2, count, side), F32),
            pltpu.VMEM((2, tiles, side, side), F32),
        ],
        compiler_params=pltpu.CompilerParams(vmem_limit_bytes=VMEM_BYTES),
        cost_estimate=pl.CostEstimate(flops=int(8e9), bytes_accessed=int(3e6), transcendentals=0),
        name="tile_sums",
    )(affine, target, weights, *coef, masks, blocks)


def pair_kernel(keep_ref, got_ref, after_ref, *outs):
    del after_ref
    for dz, out in enumerate(outs):
        for which in range(2):
            total = keep_ref[dz, which] + got_ref[dz, which].astype(F32)
            out[which] = total.astype(out.dtype)


def pair(keep, got, after):
    tiles, _, side, _ = keep.shape
    return pl.pallas_call(
        pair_kernel,
        out_shape=[jax.ShapeDtypeStruct((2, side, side), BF16 if dz else F32) for dz in range(tiles)],
        in_specs=[vmem(), vmem(), smem()],
        out_specs=[vmem()] * tiles,
        compiler_params=pltpu.CompilerParams(vmem_limit_bytes=TINY_BYTES),
        name="pair",
    )(keep, got, after)


def moments(product_x, product_y):
    side = product_x.shape[0]
    centre = (side - 1) / 2.0
    sum_x = product_x[side - 8 : side]
    sum_y = product_y[side - 8 : side]
    later = sum_y
    for v in range(side // 8 - 2, -1, -1):
        sum_x = sum_x + product_x[8 * v : 8 * v + 8]
        sum_y = sum_y + product_y[8 * v : 8 * v + 8]
        if v:
            later = later + sum_y
    sub = lax.broadcasted_iota(jnp.int32, (8, side), 0).astype(F32) - centre
    lane = lax.broadcasted_iota(jnp.int32, (1, side), 1).astype(F32) - centre
    tilted_y = 8.0 * later + sub * sum_y
    first = jnp.sum(sum_x, axis=0, keepdims=True)
    second = jnp.sum(sum_y, axis=0, keepdims=True)
    fourth = jnp.sum(tilted_y, axis=0, keepdims=True)
    return [first, second, first * lane * (1.0 / side), fourth * (1.0 / side)]


def slopes_kernel(step_blocks, start, affine_ref, coef_ref, rows_ref, near_ref, mask_ref, block_ref, *rest):
    slope_ref, part_ref, token_ref = rest[-3:]
    token_ref[0] = 0
    step = pl.program_id(0) + start
    side = 128

    ones = jnp.ones((side, side), BF16)

    def enter(j):
        b = step * step_blocks + j
        mask_row = mask_ref[pl.ds(b, 1), :].astype(F32)
        masked = block_ref[j] * mask_row.astype(BF16)
        taps = []
        for k in range(2):
            taps.append(taps_of(affine_ref[0, k, 0, b], affine_ref[0, k, 2, b], coef_ref, True))
            taps.append(taps_of(affine_ref[0, k, 1, b], affine_ref[0, k, 3, b], coef_ref, True))
        return masked, mask_rows(mask_row), taps

    def first(masked, extra, taps):
        x0, x1 = spread(*taps[0], rows_ref, near_ref), spread(*taps[2], rows_ref, near_ref)
        col_both = dot(jnp.concatenate([masked, extra], axis=0), jnp.concatenate([x0[0], x1[0]], axis=1))
        y0, y1 = spread(*taps[1], rows_ref, near_ref), spread(*taps[3], rows_ref, near_ref)
        with_ones = jnp.concatenate([masked, ones], axis=1)
        rights = [jnp.concatenate(x0, axis=1), jnp.concatenate(x1, axis=1)]
        return col_both, [dot_t(y0[0], with_ones), dot_t(y1[0], with_ones)], rights, [y0[1], y1[1]]

    def second(col_both, rows, rights, downs):
        found = []
        for k in range(2):
            row_pass = rows[k][:, :side].astype(BF16)
            col_pass = col_both[:side, k * side : (k + 1) * side].astype(BF16)
            cols_sum = col_both[side : side + 1, k * side : (k + 1) * side]
            found.append((dot(row_pass, rights[k]), dot_t(downs[k], col_pass), rows[k][:, side:], cols_sum))
        return found

    def leave(j, found):
        for k, (both, slope_y, rows_sum, cols_sum) in enumerate(found):
            weight_map = jnp.maximum(rows_sum * cols_sum, 0.0)
            value_x = weight_map * both[:, side:]
            value_y = weight_map * slope_y
            slope_ref[j, 2 * k] = value_x.astype(SLOPE)
            slope_ref[j, 2 * k + 1] = value_y.astype(SLOPE)
            warped = both[:, :side]
            for m, row in enumerate(moments(warped * value_x, warped * value_y)):
                part_ref[j, 4 * k + m : 4 * k + m + 1, :] = row

    staged(step_blocks, LAG2, enter, first, second, leave)


def slopes_of(affine, coef, masks, blocks, first, size):
    side = blocks.shape[1]
    step_blocks = STEP2
    start = first // step_blocks
    return pl.pallas_call(
        functools.partial(slopes_kernel, step_blocks, start),
        grid=(size // step_blocks,),
        out_shape=[
            jax.ShapeDtypeStruct((size, 4, side, side), SLOPE),
            jax.ShapeDtypeStruct((size, 8, side), F32),
            jax.ShapeDtypeStruct((1,), jnp.int32),
        ],
        in_specs=[
            scalars(affine),
            *[pl.BlockSpec(c.shape, lambda i, rank=c.ndim: (0,) * rank) for c in coef],
            pl.BlockSpec(masks.shape, lambda i: (0, 0)),
            pl.BlockSpec((step_blocks, side, side), lambda i: (i + start, 0, 0)),
        ],
        out_specs=[
            pl.BlockSpec((step_blocks, 4, side, side), lambda i: (i, 0, 0, 0)),
            pl.BlockSpec((step_blocks, 8, side), lambda i: (i, 0, 0)),
            smem(),
        ],
        compiler_params=pltpu.CompilerParams(vmem_limit_bytes=SMALL_BYTES),
        cost_estimate=pl.CostEstimate(flops=int(1.5e8) * size, bytes_accessed=int(3e5) * size, transcendentals=0),
        name="slopes",
    )(affine, *coef, masks, blocks)


def coadd_kernel(after_ref, *refs):
    del after_ref
    parts, (piece_ref, edge_ref) = refs[:-2], refs[-2:]
    num, den = parts[0][0], parts[0][1]
    for part in parts[1:]:
        num = num + part[0].astype(F32)
        den = den + part[1].astype(F32)
    side = num.shape[1]
    left = lax.broadcasted_iota(jnp.int32, num.shape, 1) < side // 2
    first = num / (1.0 + den)
    piece = (num + jnp.where(left, 0.0, pltpu.roll(first, side // 2, 1))) / (1.0 + den)
    piece_ref[...] = piece
    flipped = jnp.transpose(piece)
    half = side // 2
    outer = jnp.concatenate([flipped[0:8], flipped[half : half + 8]], axis=0)
    inner = jnp.concatenate([flipped[half - 8 : half], flipped[side - 8 : side]], axis=0)
    edge_ref[...] = jnp.where(lax.axis_index("exp") == 0, outer, inner).astype(BF16)


def coadd_of(after, parts):
    side = parts[0].shape[2]
    return pl.pallas_call(
        coadd_kernel,
        out_shape=[jax.ShapeDtypeStruct((side, side), F32), jax.ShapeDtypeStruct((16, side), BF16)],
        in_specs=[smem()] + [vmem()] * len(parts),
        out_specs=[vmem(), vmem()],
        compiler_params=pltpu.CompilerParams(vmem_limit_bytes=TINY_BYTES),
        name="coadd",
    )(after, *parts)


def band_of(values, diagonal):
    total = jnp.zeros(diagonal.shape, F32)
    for q, value in enumerate(values):
        total = jnp.where(diagonal == q, value, total)
    high = total.astype(BF16)
    return jnp.concatenate([high, (total - high.astype(F32)).astype(BF16)], axis=1)


def bands_kernel(psf_ref, after_ref, inner_ref, outer_ref, rows_ref, token_ref):
    token_ref[0] = after_ref[0]
    side = inner_ref.shape[1]
    along = lax.broadcasted_iota(jnp.int32, (side, side), 0)
    across = lax.broadcasted_iota(jnp.int32, (side, side), 1)
    edge = along[:16]
    edge = jnp.where(edge < 8, edge - 8, edge + side - 8)
    for k in range(2):
        taps = [psf_ref[k, 1, q] for q in range(TAPS)]
        inner_ref[k] = band_of(taps, along - across + RAD)
        outer_ref[k] = band_of(taps, edge - across[:16] + RAD)
        wide = (side, side + 32)
        below = lax.broadcasted_iota(jnp.int32, wide, 1) - lax.broadcasted_iota(jnp.int32, wide, 0) - 16 + RAD
        total = jnp.zeros(wide, F32)
        for q in range(TAPS):
            total = jnp.where(below == q, psf_ref[k, 0, q], total)
        high = total.astype(BF16)
        rows_ref[k, 0:side, :] = high
        rows_ref[k, side : 2 * side, :] = (total - high.astype(F32)).astype(BF16)


def bands_of(psf, after, side=128):
    return pl.pallas_call(
        bands_kernel,
        out_shape=[jax.ShapeDtypeStruct((2, rows, 2 * side), BF16) for rows in (side, 16)]
        + [jax.ShapeDtypeStruct((2, 2 * side, side + 32), BF16), jax.ShapeDtypeStruct((1,), jnp.int32)],
        in_specs=[smem(), smem()],
        out_specs=[vmem(), vmem(), vmem(), smem()],
        compiler_params=pltpu.CompilerParams(vmem_limit_bytes=TINY_BYTES),
        name="bands",
    )(psf, after)


def smoothed(tile, edges, inner, outer):
    side = tile.shape[1]
    high = tile.astype(BF16)
    low = (tile - high.astype(F32)).astype(BF16)
    both = dot(high, inner) + dot_t(edges, outer)
    return both[:, :side] + both[:, side:] + dot(low, inner[:, :side])


def join_kernel(inner_ref, outer_ref, own_ref, other_ref, edge_ref, far_ref, after_ref, sky_ref, tile_ref):
    del after_ref
    here = lax.axis_index("exp") == 0
    own, other = own_ref[...], other_ref[...]
    tiles = halves_of(jnp.where(here, own, other), jnp.where(here, other, own))
    edge, far = edge_ref[...].astype(F32), far_ref[...].astype(F32)
    left, right = jnp.where(here, far, edge), jnp.where(here, edge, far)
    column = lax.axis_index("ty")
    left = jnp.where(column > 0, left, 0.0)
    right = jnp.where(column < lax.axis_size("ty") - 1, right, 0.0)
    for k in range(2):
        at = slice(8 * k, 8 * k + 8)
        edges = jnp.concatenate([left[at], right[at]], axis=0).astype(BF16)
        sky_ref[k] = smoothed(tiles[k], edges, inner_ref[k], outer_ref[k]).astype(BF16)
    tile_ref[...] = tiles[1]


def join(bands, own, other, edge, far, after):
    side = own.shape[1]
    return pl.pallas_call(
        join_kernel,
        out_shape=[jax.ShapeDtypeStruct((2, side, side), BF16), jax.ShapeDtypeStruct((side, side), F32)],
        in_specs=[vmem()] * 6 + [smem()],
        out_specs=[vmem(), vmem()],
        compiler_params=pltpu.CompilerParams(vmem_limit_bytes=TINY_BYTES),
        name="join",
    )(*bands, own, other, edge, far, after)


def whole_kernel(inner_ref, outer_ref, tile_ref, edge_ref, sky_ref):
    for k in range(2):
        sky_ref[k] = smoothed(tile_ref[k], edge_ref[k], inner_ref[k], outer_ref[k]).astype(BF16)


def whole_sky(bands, tiles, edges):
    return pl.pallas_call(
        whole_kernel,
        out_shape=jax.ShapeDtypeStruct(tiles.shape, BF16),
        in_specs=[vmem()] * 4,
        out_specs=vmem(),
        compiler_params=pltpu.CompilerParams(vmem_limit_bytes=TINY_BYTES),
        name="whole_sky",
    )(*bands, tiles, edges)


def gradient_kernel(tiles, target_ref, band_ref, *rest):
    skies = rest[:tiles]
    chunk_refs, (out_ref, smooth, model) = rest[tiles:-3], rest[-3:]
    side = 128
    for k in range(2):
        smooth[k, 0:16, :] = jnp.zeros((16, side), BF16)
        smooth[k, 16 + tiles * side : 32 + tiles * side, :] = jnp.zeros((16, side), BF16)
        for turn in range(tiles):
            tile = lax.rem(lax.axis_index("tx") + tiles - turn, tiles)
            smooth[k, pl.ds(pl.multiple_of(16 + tile * side, 16), side), :] = skies[turn][k]
        for tile in range(tiles):
            both = dot(band_ref[k], smooth[k, tile * side : (tile + 1) * side + 32, :])
            total = both[:side] + both[side:]
            model[k, tile * side : (tile + 1) * side, :] = total.astype(BF16).astype(F32)

    count = out_ref.shape[3]
    lane = lax.broadcasted_iota(jnp.int32, (8, count), 1)
    gathered = jnp.zeros((8, count), F32)
    first = 0
    for slope_ref, part_ref in zip(chunk_refs[::2], chunk_refs[1::2]):

        def body(group, gathered, first=first, slope_ref=slope_ref, part_ref=part_ref):
            found = []
            for u in range(GROUP3):
                j = group * GROUP3 + u
                start = pl.multiple_of(target_ref[0, 0, first + j] * side, side)
                rows = []
                for k in range(2):
                    cutout = model[k, pl.ds(start, side), :]
                    slope_x, slope_y = slope_ref[j, 2 * k].astype(F32), slope_ref[j, 2 * k + 1].astype(F32)
                    rows += moments(cutout * slope_x, cutout * slope_y)
                found.append((j, rows))
            for j, rows in found:
                total = jnp.sum(part_ref[j] - jnp.concatenate(rows, axis=0), axis=1, keepdims=True) * (1.0 / side)
                gathered = jnp.where(lane == first + j, total, gathered)
            return gathered

        gathered = lax.fori_loop(0, slope_ref.shape[0] // GROUP3, body, gathered)
        first += slope_ref.shape[0]
    out_ref[0, 0] = gathered[0:4]
    out_ref[0, 1] = gathered[4:8]


def gradients_of(target, row_bands, skies, chunks):
    side = skies[0].shape[1]
    tiles, count = len(skies), target.shape[2]
    arrays = [array for pair_of in chunks for array in pair_of]
    return pl.pallas_call(
        functools.partial(gradient_kernel, tiles),
        out_shape=jax.ShapeDtypeStruct((1, 2, 4, count), F32),
        in_specs=[smem()] + [vmem()] * (1 + tiles + len(arrays)),
        out_specs=vmem(),
        scratch_shapes=[
            pltpu.VMEM((2, tiles * side + 32, side), BF16),
            pltpu.VMEM((2, tiles * side, side), F32),
        ],
        compiler_params=pltpu.CompilerParams(vmem_limit_bytes=SMALL_BYTES),
        cost_estimate=pl.CostEstimate(flops=int(4e9), bytes_accessed=int(20e6), transcendentals=0),
        name="gradients",
    )(target, row_bands, *skies, *arrays)


def swap(cells):
    return lax.ppermute(cells, "exp", [(0, 1), (1, 0)])


def turned(cells, dz, tiles):
    return lax.ppermute(cells, "tx", [(z, (z + dz) % tiles) for z in range(tiles)])


def to_sides(edge, columns, flip):
    perm = [(y, flip * columns + (y - 1) % columns) for y in range(columns)]
    perm += [(columns + y, (1 - flip) * columns + (y + 1) % columns) for y in range(columns)]
    return lax.ppermute(edge, ("exp", "ty"), perm)


def local(exposures, block_tile, affine, col_mask, block_weight, psf):
    blocks = exposures[0]
    count, side = blocks.shape[0], blocks.shape[1]
    tiles, halves, columns = lax.axis_size("tx"), lax.axis_size("exp"), lax.axis_size("ty")
    rows, near = windows()
    coef = (jnp.asarray(series()), jnp.asarray(rows), jnp.asarray(near, BF16))
    affine = affine.transpose(0, 2, 3, 1)
    block_tile = block_tile.transpose(0, 2, 1)
    masks = col_mask[0]
    small = halves == 2 and tiles <= 4
    sums = tile_sums(affine, block_tile, block_weight, coef, masks, blocks, tiles, small)
    chunks, tokens, first = [], [], 0
    scale = count // sum(CHUNKS)
    for size in CHUNKS:
        *found, token = slopes_of(affine, coef, masks, blocks, first, size * scale)
        chunks.append(found)
        tokens.append(token)
        first += size * scale
    if small:
        keep, send = sums
        *bands, row_bands, token = bands_of(psf, tokens[0])
        totals = pair(keep, swap(send), token)
        got = [totals[0]] + [turned(totals[dz], dz, tiles) for dz in range(1, tiles)]
        piece, edge = coadd_of(tokens[1], got)
        other = swap(piece)
        near, far = to_sides(edge, columns, 0), to_sides(edge, columns, 1)
        sky, coadd_tile = join(bands, piece, other, near, far, tokens[-2])
        skies = [sky] + [turned(sky, dz, tiles) for dz in range(1, tiles)]
    else:
        me = lax.axis_index("tx")
        summed = lax.psum_scatter(sums[0], "tx", scatter_dimension=0, tiled=True)
        (num, den) = lax.psum(summed[0], "exp")
        one = num[0] / (1.0 + den[0])
        coadd_tile = (num[1] + one) / (1.0 + den[1])
        both = jnp.stack([one, coadd_tile])
        flipped = jnp.swapaxes(both, 1, 2).astype(BF16)
        left = lax.ppermute(flipped[:, side - 8 :], "ty", [(y, y + 1) for y in range(columns - 1)])
        right = lax.ppermute(flipped[:, :8], "ty", [(y + 1, y) for y in range(columns - 1)])
        *bands, row_bands, _ = bands_of(psf, tokens[0])
        sky = whole_sky(bands, both, jnp.concatenate([left, right], axis=1))
        gathered = lax.all_gather(sky, "tx", axis=0)
        skies = [lax.dynamic_index_in_dim(gathered, (me + tiles - turn) % tiles, 0, False) for turn in range(tiles)]
    gradients = gradients_of(block_tile, row_bands, skies, chunks)
    return gradients.transpose(0, 3, 1, 2), coadd_tile


def solution(mesh):
    placed = (
        P("ty", ("exp", "tx"), None, None),
        P("ty", ("exp", "tx"), None),
        P("ty", ("exp", "tx"), None, None),
        P("ty", ("exp", "tx"), None),
        P("ty", ("exp", "tx")),
        P(),
    )
    return jax.shard_map(
        local,
        mesh=mesh,
        in_specs=placed,
        out_specs=(P("ty", ("exp", "tx"), None, None), P("tx", "ty")),
        check_vma=False,
    )
```

```python
import functools

import jax
import jax.numpy as jnp
import numpy as np
from jax import lax
from jax.experimental import pallas as pl
from jax.experimental.pallas import tpu as pltpu
from jax.sharding import PartitionSpec as P

RAD = 4
TAPS = 2 * RAD + 1
DEGREE = 10
F32 = jnp.float32
BF16 = jnp.bfloat16
GROUP1 = 16
STEP2 = 8
LAG2 = (0, 4, 8, 12)
GROUP3 = 8
CHUNKS = (24, 16, 24)
SLOPE = jnp.bfloat16
VMEM_BYTES = 56 * 1024 * 1024
SMALL_BYTES = 20 * 1024 * 1024
TINY_BYTES = 6 * 1024 * 1024


def series():
    count = 64
    nodes = np.cos(np.pi * (np.arange(count) + 0.5) / count)
    table = np.zeros((2, DEGREE + 1, 8), np.float64)
    for row in range(1, 7):
        d = nodes * 0.5 + 0.5 - (row - 3)
        a, b = np.sinc(d), np.sinc(d / 3.0)
        da = (np.cos(np.pi * d) - a) / d
        db = (np.cos(np.pi * d / 3.0) - b) / d
        for which, values in enumerate((a * b, da * b + a * db)):
            fit = np.polynomial.chebyshev.Chebyshev.fit(nodes * 0.5, values, DEGREE, domain=[-0.5, 0.5])
            table[which, :, row] = fit.convert(kind=np.polynomial.Polynomial).coef
    return np.repeat(table.reshape(2 * (DEGREE + 1), 8, 1), 128, axis=2).astype(np.float32)


def taps_of(shift_code, stretch_code, coef_ref, slopes):
    side = 128
    centre = (side - 1) / 2.0
    lane = lax.broadcasted_iota(jnp.int32, (8, side), 1).astype(F32)
    shift = jnp.full((8, side), shift_code, jnp.int32).astype(F32) * (1.0 / 256.0)
    stretch = jnp.full((8, side), stretch_code, jnp.int32).astype(F32) * (1.0 / 51200.0)
    source = centre + (1.0 + stretch) * (lane - centre) + shift
    whole = jnp.floor(source)
    v = (source - whole) - 0.5
    found = []
    for which in range(2 if slopes else 1):
        base = which * (DEGREE + 1)
        total = coef_ref[base + DEGREE]
        for power in range(DEGREE - 1, -1, -1):
            total = total * v + coef_ref[base + power]
        found.append(total)
    return found, whole.astype(jnp.int32)


def pick(taps, index):
    numbers = lax.GatherDimensionNumbers(
        offset_dims=(),
        collapsed_slice_dims=(0,),
        start_index_map=(0,),
        operand_batching_dims=(1,),
        start_indices_batching_dims=(1,),
    )
    mode = lax.GatherScatterMode.PROMISE_IN_BOUNDS
    return lax.gather(taps, index[..., None], numbers, slice_sizes=(1, 1), mode=mode)


def windows():
    sub, lane = np.arange(8)[:, None], np.arange(128)[None, :]
    rows = [8 * (3 * ((lane + 8 - 8 * r) // 24) + r) + sub + 3 for r in range(3)]
    start = np.arange(128)[:, None] // 8 * 8 - 8
    near = (lane >= start) & (lane < start + 24)
    return np.stack(rows).astype(np.int32), near.astype(np.float32)


def spread(tap_list, whole, rows_ref, near_ref):
    indices = [jnp.clip(rows_ref[r] - whole, 0, 7) for r in range(3)]
    bands = []
    for taps in tap_list:
        classes = [pick(taps, index) for index in indices]
        pairs = [
            jnp.concatenate([classes[2 * w % 3], classes[(2 * w + 1) % 3]], axis=0).astype(BF16) for w in range(3)
        ]
        bands.append(jnp.concatenate([pairs[w % 3] for w in range(8)], axis=0) * near_ref[...])
    return bands


def dot(a, b):
    return jnp.dot(a, b, preferred_element_type=F32)


def dot_t(a, b):
    return lax.dot_general(a, b, (((0,), (0,)), ((), ())), preferred_element_type=F32)


def staged(count, lags, enter, first, second, leave):
    held = [dict() for _ in range(3)]
    for turn in range(count + max(lags)):
        for stage in range(4):
            j = turn - lags[stage]
            if not 0 <= j < count:
                continue
            if stage == 0:
                held[0][j] = enter(j)
            elif stage == 1:
                held[1][j] = first(*held[0].pop(j))
            elif stage == 2:
                held[2][j] = second(*held[1].pop(j))
            else:
                leave(j, held[2].pop(j))


def mask_rows(mask_row):
    side = mask_row.shape[1]
    first = lax.broadcasted_iota(jnp.int32, (16, side), 0) == 0
    return jnp.where(first, jnp.broadcast_to(mask_row, (16, side)), 0.0).astype(BF16)


def halves_of(first, second):
    side = first.shape[1]
    left = lax.broadcasted_iota(jnp.int32, first.shape, 1) < side // 2
    low = jnp.where(left, first, pltpu.roll(second, side // 2, 1))
    high = jnp.where(left, pltpu.roll(first, side // 2, 1), second)
    return low, high


def sums_kernel(tiles, packed, step_blocks, affine_ref, target_ref, weight_ref, coef_ref, rows_ref, near_ref, mask_ref, block_ref, *rest):
    outs = rest[:-4]
    acc, rows_sc, cols_sc, den_sc = rest[-4:]
    step = pl.program_id(0)
    side = 128

    @pl.when(step == 0)
    def _():
        acc[...] = jnp.zeros_like(acc)
        rows_sc[...] = jnp.zeros_like(rows_sc)

    def body(group, carry):
        work = []
        for u in range(GROUP1):
            j = group * GROUP1 + u
            b = step * step_blocks + j
            mask_row = mask_ref[pl.ds(j, 1), :].astype(F32)
            masked = block_ref[j] * mask_row.astype(BF16)
            for k in range(2):
                (tap_y,), whole_y = taps_of(affine_ref[0, k, 1, b], affine_ref[0, k, 3, b], coef_ref, False)
                (tap_x,), whole_x = taps_of(affine_ref[0, k, 0, b], affine_ref[0, k, 2, b], coef_ref, False)
                work.append([b, k, mask_row, masked, tap_y, whole_y, tap_x, whole_x])
        zero = jnp.zeros((side, side), BF16)

        def corner(a, c):
            return jnp.concatenate([jnp.concatenate([a, zero], axis=1), jnp.concatenate([zero, c], axis=1)], axis=0)

        duos = [(work[4 * g + k], work[4 * g + 2 + k]) for g in range(GROUP1 // 2) for k in range(2)]
        passes = []
        for one, two in duos:
            (ly_a,) = spread([one[4]], one[5], rows_ref, near_ref)
            (ly_b,) = spread([two[4]], two[5], rows_ref, near_ref)
            both = dot_t(jnp.concatenate([ly_a, ly_b], axis=0), corner(one[3], two[3]))
            passes.append(both.astype(BF16))
        warps = {}
        for (one, two), row_pass in zip(duos, passes):
            (lx_a,) = spread([one[6]], one[7], rows_ref, near_ref)
            (lx_b,) = spread([two[6]], two[7], rows_ref, near_ref)
            extra = jnp.concatenate([mask_rows(one[2]), mask_rows(two[2])], axis=1)
            both = dot(jnp.concatenate([row_pass, extra], axis=0), corner(lx_a, lx_b))
            warps[id(one)], warps[id(two)] = both[:, :side], both[:, side:]
        warps = [warps[id(item)] for item in work]
        for (b, k, mask_row, masked, tap_y, whole_y, tap_x, whole_x), both in zip(work, warps):
            tile = target_ref[0, 0, b]
            weight = weight_ref[0, b]
            sent = (weight * both[:side]).astype(BF16).astype(F32)
            acc[k, tile] = acc[k, tile] + sent
            at = whole_y + lax.broadcasted_iota(jnp.int32, (8, side), 0) - 3
            used = jnp.where((at >= 0) & (at < side), tap_y.astype(BF16).astype(F32), 0.0)
            rows_sum = jnp.sum(used, axis=0, keepdims=True)
            rows_sc[k, tile, pl.ds(b, 1), :] = (weight * rows_sum).astype(BF16).astype(F32)
            cols_sc[k, pl.ds(b, 1), :] = both[side : side + 1].astype(BF16).astype(F32)
        return carry

    lax.fori_loop(0, step_blocks // GROUP1, body, 0)

    @pl.when(step == pl.num_programs(0) - 1)
    def _():
        for k in range(2):
            cols = cols_sc[k]
            cols = jnp.concatenate([jnp.maximum(cols, 0.0), jnp.maximum(-cols, 0.0)], axis=0).astype(BF16)

            def one(t, carry, k=k, cols=cols):
                rows = rows_sc[k, t]
                rows = jnp.concatenate([jnp.maximum(rows, 0.0), jnp.maximum(-rows, 0.0)], axis=0).astype(BF16)
                den_sc[k, t] = dot_t(rows, cols)
                return carry

            lax.fori_loop(0, tiles, one, 0, unroll=tiles if packed else 1)
        if packed:
            keep_ref, send_ref = outs
            low_end = lax.axis_index("exp") == 0
            for dz in range(tiles):
                tile = lax.rem(lax.axis_index("tx") + dz, tiles)
                for which, source in enumerate((acc, den_sc)):
                    low, high = halves_of(source[0, tile], source[1, tile])
                    keep_ref[dz, which] = jnp.where(low_end, low, high)
                    send_ref[dz, which] = jnp.where(low_end, high, low).astype(BF16)
        else:

            def whole(t, carry):
                for k in range(2):
                    outs[0][t, 0, k] = acc[k, t]
                    outs[0][t, 1, k] = den_sc[k, t]
                return carry

            lax.fori_loop(0, tiles, whole, 0)


def vmem():
    return pl.BlockSpec(memory_space=pltpu.VMEM)


def scalars(array):
    rank = array.ndim
    return pl.BlockSpec(array.shape, lambda i: (0,) * rank, memory_space=pltpu.SMEM)


def smem():
    return pl.BlockSpec(memory_space=pltpu.SMEM)


def tile_sums(affine, target, weights, coef, masks, blocks, tiles, packed):
    count, side = blocks.shape[0], blocks.shape[1]
    step_blocks = GROUP1
    if packed:
        shapes = [((tiles, 2, side, side), F32), ((tiles, 2, side, side), BF16)]
    else:
        shapes = [((tiles, 2, 2, side, side), F32)]
    return pl.pallas_call(
        functools.partial(sums_kernel, tiles, packed, step_blocks),
        grid=(count // step_blocks,),
        out_shape=[jax.ShapeDtypeStruct(*shape) for shape in shapes],
        in_specs=[
            scalars(affine),
            scalars(target),
            scalars(weights),
            *[pl.BlockSpec(c.shape, lambda i, rank=c.ndim: (0,) * rank) for c in coef],
            pl.BlockSpec((step_blocks, side), lambda i: (i, 0)),
            pl.BlockSpec((step_blocks, side, side), lambda i: (i, 0, 0)),
        ],
        out_specs=[pl.BlockSpec(shape, lambda i, rank=len(shape): (0,) * rank) for shape, _ in shapes],
        scratch_shapes=[
            pltpu.VMEM((2, tiles, side, side), F32),
            pltpu.VMEM((2, tiles, count, side), F32),
            pltpu.VMEM((2, count, side), F32),
            pltpu.VMEM((2, tiles, side, side), F32),
        ],
        compiler_params=pltpu.CompilerParams(vmem_limit_bytes=VMEM_BYTES),
        cost_estimate=pl.CostEstimate(flops=int(8e9), bytes_accessed=int(3e6), transcendentals=0),
        name="tile_sums",
    )(affine, target, weights, *coef, masks, blocks)


def pair_kernel(keep_ref, got_ref, after_ref, *outs):
    del after_ref
    for dz, out in enumerate(outs):
        for which in range(2):
            total = keep_ref[dz, which] + got_ref[dz, which].astype(F32)
            out[which] = total.astype(out.dtype)


def pair(keep, got, after):
    tiles, _, side, _ = keep.shape
    return pl.pallas_call(
        pair_kernel,
        out_shape=[jax.ShapeDtypeStruct((2, side, side), BF16 if dz else F32) for dz in range(tiles)],
        in_specs=[vmem(), vmem(), smem()],
        out_specs=[vmem()] * tiles,
        compiler_params=pltpu.CompilerParams(vmem_limit_bytes=TINY_BYTES),
        name="pair",
    )(keep, got, after)


def moments(product_x, product_y):
    side = product_x.shape[0]
    centre = (side - 1) / 2.0
    sum_x = product_x[side - 8 : side]
    sum_y = product_y[side - 8 : side]
    later = sum_y
    for v in range(side // 8 - 2, -1, -1):
        sum_x = sum_x + product_x[8 * v : 8 * v + 8]
        sum_y = sum_y + product_y[8 * v : 8 * v + 8]
        if v:
            later = later + sum_y
    sub = lax.broadcasted_iota(jnp.int32, (8, side), 0).astype(F32) - centre
    lane = lax.broadcasted_iota(jnp.int32, (1, side), 1).astype(F32) - centre
    tilted_y = 8.0 * later + sub * sum_y
    first = jnp.sum(sum_x, axis=0, keepdims=True)
    second = jnp.sum(sum_y, axis=0, keepdims=True)
    fourth = jnp.sum(tilted_y, axis=0, keepdims=True)
    return [first, second, first * lane * (1.0 / side), fourth * (1.0 / side)]


def slopes_kernel(step_blocks, start, affine_ref, coef_ref, rows_ref, near_ref, mask_ref, block_ref, *rest):
    slope_ref, part_ref, token_ref = rest[-3:]
    token_ref[0] = 0
    step = pl.program_id(0) + start
    side = 128

    ones = jnp.ones((side, side), BF16)

    def enter(j):
        b = step * step_blocks + j
        mask_row = mask_ref[pl.ds(b, 1), :].astype(F32)
        masked = block_ref[j] * mask_row.astype(BF16)
        taps = []
        for k in range(2):
            taps.append(taps_of(affine_ref[0, k, 0, b], affine_ref[0, k, 2, b], coef_ref, True))
            taps.append(taps_of(affine_ref[0, k, 1, b], affine_ref[0, k, 3, b], coef_ref, True))
        return masked, mask_rows(mask_row), taps

    def first(masked, extra, taps):
        x0, x1 = spread(*taps[0], rows_ref, near_ref), spread(*taps[2], rows_ref, near_ref)
        col_both = dot(jnp.concatenate([masked, extra], axis=0), jnp.concatenate([x0[0], x1[0]], axis=1))
        y0, y1 = spread(*taps[1], rows_ref, near_ref), spread(*taps[3], rows_ref, near_ref)
        with_ones = jnp.concatenate([masked, ones], axis=1)
        rights = [jnp.concatenate(x0, axis=1), jnp.concatenate(x1, axis=1)]
        return col_both, [dot_t(y0[0], with_ones), dot_t(y1[0], with_ones)], rights, [y0[1], y1[1]]

    def second(col_both, rows, rights, downs):
        found = []
        for k in range(2):
            row_pass = rows[k][:, :side].astype(BF16)
            col_pass = col_both[:side, k * side : (k + 1) * side].astype(BF16)
            cols_sum = col_both[side : side + 1, k * side : (k + 1) * side]
            found.append((dot(row_pass, rights[k]), dot_t(downs[k], col_pass), rows[k][:, side:], cols_sum))
        return found

    def leave(j, found):
        for k, (both, slope_y, rows_sum, cols_sum) in enumerate(found):
            weight_map = jnp.maximum(rows_sum * cols_sum, 0.0)
            value_x = weight_map * both[:, side:]
            value_y = weight_map * slope_y
            slope_ref[j, 2 * k] = value_x.astype(SLOPE)
            slope_ref[j, 2 * k + 1] = value_y.astype(SLOPE)
            warped = both[:, :side]
            for m, row in enumerate(moments(warped * value_x, warped * value_y)):
                part_ref[j, 4 * k + m : 4 * k + m + 1, :] = row

    staged(step_blocks, LAG2, enter, first, second, leave)


def slopes_of(affine, coef, masks, blocks, first, size):
    side = blocks.shape[1]
    step_blocks = STEP2
    start = first // step_blocks
    return pl.pallas_call(
        functools.partial(slopes_kernel, step_blocks, start),
        grid=(size // step_blocks,),
        out_shape=[
            jax.ShapeDtypeStruct((size, 4, side, side), SLOPE),
            jax.ShapeDtypeStruct((size, 8, side), F32),
            jax.ShapeDtypeStruct((1,), jnp.int32),
        ],
        in_specs=[
            scalars(affine),
            *[pl.BlockSpec(c.shape, lambda i, rank=c.ndim: (0,) * rank) for c in coef],
            pl.BlockSpec(masks.shape, lambda i: (0, 0)),
            pl.BlockSpec((step_blocks, side, side), lambda i: (i + start, 0, 0)),
        ],
        out_specs=[
            pl.BlockSpec((step_blocks, 4, side, side), lambda i: (i, 0, 0, 0)),
            pl.BlockSpec((step_blocks, 8, side), lambda i: (i, 0, 0)),
            smem(),
        ],
        compiler_params=pltpu.CompilerParams(vmem_limit_bytes=SMALL_BYTES),
        cost_estimate=pl.CostEstimate(flops=int(1.5e8) * size, bytes_accessed=int(3e5) * size, transcendentals=0),
        name="slopes",
    )(affine, *coef, masks, blocks)


def coadd_kernel(after_ref, *refs):
    del after_ref
    parts, (piece_ref, short_ref, edge_ref) = refs[:-3], refs[-3:]
    num, den = parts[0][0], parts[0][1]
    for part in parts[1:]:
        num = num + part[0].astype(F32)
        den = den + part[1].astype(F32)
    side = num.shape[1]
    left = lax.broadcasted_iota(jnp.int32, num.shape, 1) < side // 2
    first = num / (1.0 + den)
    piece = (num + jnp.where(left, 0.0, pltpu.roll(first, side // 2, 1))) / (1.0 + den)
    piece_ref[...] = piece
    short_ref[...] = piece.astype(BF16)
    flipped = jnp.transpose(piece)
    half = side // 2
    outer = jnp.concatenate([flipped[0:8], flipped[half : half + 8]], axis=0)
    inner = jnp.concatenate([flipped[half - 8 : half], flipped[side - 8 : side]], axis=0)
    edge_ref[...] = jnp.where(lax.axis_index("exp") == 0, outer, inner).astype(BF16)


def coadd_of(after, parts):
    side = parts[0].shape[2]
    return pl.pallas_call(
        coadd_kernel,
        out_shape=[
            jax.ShapeDtypeStruct((side, side), F32),
            jax.ShapeDtypeStruct((side, side), BF16),
            jax.ShapeDtypeStruct((16, side), BF16),
        ],
        in_specs=[smem()] + [vmem()] * len(parts),
        out_specs=[vmem()] * 3,
        compiler_params=pltpu.CompilerParams(vmem_limit_bytes=TINY_BYTES),
        name="coadd",
    )(after, *parts)


def band_of(values, diagonal):
    total = jnp.zeros(diagonal.shape, F32)
    for q, value in enumerate(values):
        total = jnp.where(diagonal == q, value, total)
    high = total.astype(BF16)
    return jnp.concatenate([high, (total - high.astype(F32)).astype(BF16)], axis=1)


def bands_kernel(psf_ref, after_ref, inner_ref, outer_ref, rows_ref, token_ref):
    token_ref[0] = after_ref[0]
    side = inner_ref.shape[1]
    along = lax.broadcasted_iota(jnp.int32, (side, side), 0)
    across = lax.broadcasted_iota(jnp.int32, (side, side), 1)
    edge = along[:16]
    edge = jnp.where(edge < 8, edge - 8, edge + side - 8)
    for k in range(2):
        taps = [psf_ref[k, 1, q] for q in range(TAPS)]
        inner_ref[k] = band_of(taps, along - across + RAD)
        outer_ref[k] = band_of(taps, edge - across[:16] + RAD)
        wide = (side, side + 32)
        below = lax.broadcasted_iota(jnp.int32, wide, 1) - lax.broadcasted_iota(jnp.int32, wide, 0) - 16 + RAD
        total = jnp.zeros(wide, F32)
        for q in range(TAPS):
            total = jnp.where(below == q, psf_ref[k, 0, q], total)
        high = total.astype(BF16)
        rows_ref[k, 0:side, :] = high
        rows_ref[k, side : 2 * side, :] = (total - high.astype(F32)).astype(BF16)


def bands_of(psf, after, side=128):
    return pl.pallas_call(
        bands_kernel,
        out_shape=[jax.ShapeDtypeStruct((2, rows, 2 * side), BF16) for rows in (side, 16)]
        + [jax.ShapeDtypeStruct((2, 2 * side, side + 32), BF16), jax.ShapeDtypeStruct((1,), jnp.int32)],
        in_specs=[smem(), smem()],
        out_specs=[vmem(), vmem(), vmem(), smem()],
        compiler_params=pltpu.CompilerParams(vmem_limit_bytes=TINY_BYTES),
        name="bands",
    )(psf, after)


def smoothed(tile, edges, inner, outer):
    side = tile.shape[1]
    high = tile.astype(BF16)
    low = (tile - high.astype(F32)).astype(BF16)
    both = dot(high, inner) + dot_t(edges, outer)
    return both[:, :side] + both[:, side:] + dot(low, inner[:, :side])


def join_kernel(inner_ref, outer_ref, own_ref, other_ref, edge_ref, far_ref, after_ref, sky_ref):
    del after_ref
    here = lax.axis_index("exp") == 0
    own, other = own_ref[...], other_ref[...].astype(F32)
    tiles = halves_of(jnp.where(here, own, other), jnp.where(here, other, own))
    edge, far = edge_ref[...].astype(F32), far_ref[...].astype(F32)
    left, right = jnp.where(here, far, edge), jnp.where(here, edge, far)
    column = lax.axis_index("ty")
    left = jnp.where(column > 0, left, 0.0)
    right = jnp.where(column < lax.axis_size("ty") - 1, right, 0.0)
    for k in range(2):
        at = slice(8 * k, 8 * k + 8)
        edges = jnp.concatenate([left[at], right[at]], axis=0).astype(BF16)
        sky_ref[k] = smoothed(tiles[k], edges, inner_ref[k], outer_ref[k]).astype(BF16)


def join(bands, own, other, edge, far, after):
    side = own.shape[1]
    return pl.pallas_call(
        join_kernel,
        out_shape=jax.ShapeDtypeStruct((2, side, side), BF16),
        in_specs=[vmem()] * 6 + [smem()],
        out_specs=vmem(),
        compiler_params=pltpu.CompilerParams(vmem_limit_bytes=TINY_BYTES),
        name="join",
    )(*bands, own, other, edge, far, after)


def tile_kernel(own_ref, other_ref, tile_ref):
    here = lax.axis_index("exp") == 0
    own, other = own_ref[...], other_ref[...]
    tile_ref[...] = halves_of(jnp.where(here, own, other), jnp.where(here, other, own))[1]


def tile_of(own, other):
    return pl.pallas_call(
        tile_kernel,
        out_shape=jax.ShapeDtypeStruct(own.shape, F32),
        in_specs=[vmem(), vmem()],
        out_specs=vmem(),
        compiler_params=pltpu.CompilerParams(vmem_limit_bytes=TINY_BYTES),
        name="tile",
    )(own, other)


def whole_kernel(inner_ref, outer_ref, tile_ref, edge_ref, sky_ref):
    for k in range(2):
        sky_ref[k] = smoothed(tile_ref[k], edge_ref[k], inner_ref[k], outer_ref[k]).astype(BF16)


def whole_sky(bands, tiles, edges):
    return pl.pallas_call(
        whole_kernel,
        out_shape=jax.ShapeDtypeStruct(tiles.shape, BF16),
        in_specs=[vmem()] * 4,
        out_specs=vmem(),
        compiler_params=pltpu.CompilerParams(vmem_limit_bytes=TINY_BYTES),
        name="whole_sky",
    )(*bands, tiles, edges)


def gradient_kernel(tiles, target_ref, band_ref, *rest):
    skies = rest[:tiles]
    chunk_refs, (out_ref, smooth, model) = rest[tiles:-3], rest[-3:]
    side = 128
    for k in range(2):
        smooth[k, 0:16, :] = jnp.zeros((16, side), BF16)
        smooth[k, 16 + tiles * side : 32 + tiles * side, :] = jnp.zeros((16, side), BF16)
        for turn in range(tiles):
            tile = lax.rem(lax.axis_index("tx") + tiles - turn, tiles)
            smooth[k, pl.ds(pl.multiple_of(16 + tile * side, 16), side), :] = skies[turn][k]
        for tile in range(tiles):
            both = dot(band_ref[k], smooth[k, tile * side : (tile + 1) * side + 32, :])
            total = both[:side] + both[side:]
            model[k, tile * side : (tile + 1) * side, :] = total.astype(BF16).astype(F32)

    count = out_ref.shape[3]
    lane = lax.broadcasted_iota(jnp.int32, (8, count), 1)
    gathered = jnp.zeros((8, count), F32)
    first = 0
    for slope_ref, part_ref in zip(chunk_refs[::2], chunk_refs[1::2]):

        def body(group, gathered, first=first, slope_ref=slope_ref, part_ref=part_ref):
            found = []
            for u in range(GROUP3):
                j = group * GROUP3 + u
                start = pl.multiple_of(target_ref[0, 0, first + j] * side, side)
                rows = []
                for k in range(2):
                    cutout = model[k, pl.ds(start, side), :]
                    slope_x, slope_y = slope_ref[j, 2 * k].astype(F32), slope_ref[j, 2 * k + 1].astype(F32)
                    rows += moments(cutout * slope_x, cutout * slope_y)
                found.append((j, rows))
            for j, rows in found:
                total = jnp.sum(part_ref[j] - jnp.concatenate(rows, axis=0), axis=1, keepdims=True) * (1.0 / side)
                gathered = jnp.where(lane == first + j, total, gathered)
            return gathered

        gathered = lax.fori_loop(0, slope_ref.shape[0] // GROUP3, body, gathered)
        first += slope_ref.shape[0]
    out_ref[0, 0] = gathered[0:4]
    out_ref[0, 1] = gathered[4:8]


def gradients_of(target, row_bands, skies, chunks):
    side = skies[0].shape[1]
    tiles, count = len(skies), target.shape[2]
    arrays = [array for pair_of in chunks for array in pair_of]
    return pl.pallas_call(
        functools.partial(gradient_kernel, tiles),
        out_shape=jax.ShapeDtypeStruct((1, 2, 4, count), F32),
        in_specs=[smem()] + [vmem()] * (1 + tiles + len(arrays)),
        out_specs=vmem(),
        scratch_shapes=[
            pltpu.VMEM((2, tiles * side + 32, side), BF16),
            pltpu.VMEM((2, tiles * side, side), F32),
        ],
        compiler_params=pltpu.CompilerParams(vmem_limit_bytes=SMALL_BYTES),
        cost_estimate=pl.CostEstimate(flops=int(4e9), bytes_accessed=int(20e6), transcendentals=0),
        name="gradients",
    )(target, row_bands, *skies, *arrays)


def swap(cells):
    return lax.ppermute(cells, "exp", [(0, 1), (1, 0)])


def turned(cells, dz, tiles):
    return lax.ppermute(cells, "tx", [(z, (z + dz) % tiles) for z in range(tiles)])


def to_sides(edge, columns, flip):
    perm = [(y, flip * columns + (y - 1) % columns) for y in range(columns)]
    perm += [(columns + y, (1 - flip) * columns + (y + 1) % columns) for y in range(columns)]
    return lax.ppermute(edge, ("exp", "ty"), perm)


def local(exposures, block_tile, affine, col_mask, block_weight, psf):
    blocks = exposures[0]
    count, side = blocks.shape[0], blocks.shape[1]
    tiles, halves, columns = lax.axis_size("tx"), lax.axis_size("exp"), lax.axis_size("ty")
    rows, near = windows()
    coef = (jnp.asarray(series()), jnp.asarray(rows), jnp.asarray(near, BF16))
    affine = affine.transpose(0, 2, 3, 1)
    block_tile = block_tile.transpose(0, 2, 1)
    masks = col_mask[0]
    small = halves == 2 and tiles <= 4
    sums = tile_sums(affine, block_tile, block_weight, coef, masks, blocks, tiles, small)
    chunks, tokens, first = [], [], 0
    scale = count // sum(CHUNKS)
    for size in CHUNKS:
        *found, token = slopes_of(affine, coef, masks, blocks, first, size * scale)
        chunks.append(found)
        tokens.append(token)
        first += size * scale
    if small:
        keep, send = sums
        *bands, row_bands, token = bands_of(psf, tokens[0])
        totals = pair(keep, swap(send), token)
        got = [totals[0]] + [turned(totals[dz], dz, tiles) for dz in range(1, tiles)]
        piece, short, edge = coadd_of(tokens[1], got)
        other = swap(short)
        near, far = to_sides(edge, columns, 0), to_sides(edge, columns, 1)
        coadd_tile = tile_of(piece, swap(piece))
        sky = join(bands, piece, other, near, far, tokens[-2])
        skies = [sky] + [turned(sky, dz, tiles) for dz in range(1, tiles)]
    else:
        me = lax.axis_index("tx")
        summed = lax.psum_scatter(sums[0], "tx", scatter_dimension=0, tiled=True)
        (num, den) = lax.psum(summed[0], "exp")
        one = num[0] / (1.0 + den[0])
        coadd_tile = (num[1] + one) / (1.0 + den[1])
        both = jnp.stack([one, coadd_tile])
        flipped = jnp.swapaxes(both, 1, 2).astype(BF16)
        left = lax.ppermute(flipped[:, side - 8 :], "ty", [(y, y + 1) for y in range(columns - 1)])
        right = lax.ppermute(flipped[:, :8], "ty", [(y + 1, y) for y in range(columns - 1)])
        *bands, row_bands, _ = bands_of(psf, tokens[0])
        sky = whole_sky(bands, both, jnp.concatenate([left, right], axis=1))
        gathered = lax.all_gather(sky, "tx", axis=0)
        skies = [lax.dynamic_index_in_dim(gathered, (me + tiles - turn) % tiles, 0, False) for turn in range(tiles)]
    gradients = gradients_of(block_tile, row_bands, skies, chunks)
    return gradients.transpose(0, 3, 1, 2), coadd_tile


def solution(mesh):
    placed = (
        P("ty", ("exp", "tx"), None, None),
        P("ty", ("exp", "tx"), None),
        P("ty", ("exp", "tx"), None, None),
        P("ty", ("exp", "tx"), None),
        P("ty", ("exp", "tx")),
        P(),
    )
    return jax.shard_map(
        local,
        mesh=mesh,
        in_specs=placed,
        out_specs=(P("ty", ("exp", "tx"), None, None), P("tx", "ty")),
        check_vma=False,
    )
```

```python
import functools

import jax
import jax.numpy as jnp
import numpy as np
from jax import lax
from jax.experimental import pallas as pl
from jax.experimental.pallas import tpu as pltpu
from jax.sharding import PartitionSpec as P

RAD = 4
TAPS = 2 * RAD + 1
DEGREE = 10
F32 = jnp.float32
BF16 = jnp.bfloat16
GROUP1 = 16
STEP2 = 8
LAG2 = (0, 4, 8, 12)
GROUP3 = 8
CHUNKS = (24, 16, 24)
SLOPE = jnp.bfloat16
VMEM_BYTES = 56 * 1024 * 1024
SMALL_BYTES = 20 * 1024 * 1024
TINY_BYTES = 6 * 1024 * 1024


def series():
    count = 64
    nodes = np.cos(np.pi * (np.arange(count) + 0.5) / count)
    table = np.zeros((2, DEGREE + 1, 8), np.float64)
    for row in range(1, 7):
        d = nodes * 0.5 + 0.5 - (row - 3)
        a, b = np.sinc(d), np.sinc(d / 3.0)
        da = (np.cos(np.pi * d) - a) / d
        db = (np.cos(np.pi * d / 3.0) - b) / d
        for which, values in enumerate((a * b, da * b + a * db)):
            fit = np.polynomial.chebyshev.Chebyshev.fit(nodes * 0.5, values, DEGREE, domain=[-0.5, 0.5])
            table[which, :, row] = fit.convert(kind=np.polynomial.Polynomial).coef
    return np.repeat(table.reshape(2 * (DEGREE + 1), 8, 1), 128, axis=2).astype(np.float32)


def taps_of(shift_code, stretch_code, coef_ref, slopes):
    side = 128
    centre = (side - 1) / 2.0
    lane = lax.broadcasted_iota(jnp.int32, (8, side), 1).astype(F32)
    shift = jnp.full((8, side), shift_code, jnp.int32).astype(F32) * (1.0 / 256.0)
    stretch = jnp.full((8, side), stretch_code, jnp.int32).astype(F32) * (1.0 / 51200.0)
    source = centre + (1.0 + stretch) * (lane - centre) + shift
    whole = jnp.floor(source)
    v = (source - whole) - 0.5
    found = []
    for which in range(2 if slopes else 1):
        base = which * (DEGREE + 1)
        total = coef_ref[base + DEGREE]
        for power in range(DEGREE - 1, -1, -1):
            total = total * v + coef_ref[base + power]
        found.append(total)
    return found, whole.astype(jnp.int32)


def pick(taps, index):
    numbers = lax.GatherDimensionNumbers(
        offset_dims=(),
        collapsed_slice_dims=(0,),
        start_index_map=(0,),
        operand_batching_dims=(1,),
        start_indices_batching_dims=(1,),
    )
    mode = lax.GatherScatterMode.PROMISE_IN_BOUNDS
    return lax.gather(taps, index[..., None], numbers, slice_sizes=(1, 1), mode=mode)


def windows():
    sub, lane = np.arange(8)[:, None], np.arange(128)[None, :]
    rows = [8 * (3 * ((lane + 8 - 8 * r) // 24) + r) + sub + 3 for r in range(3)]
    start = np.arange(128)[:, None] // 8 * 8 - 8
    near = (lane >= start) & (lane < start + 24)
    return np.stack(rows).astype(np.int32), near.astype(np.float32)


def spread(tap_list, whole, rows_ref, near_ref):
    indices = [jnp.clip(rows_ref[r] - whole, 0, 7) for r in range(3)]
    bands = []
    for taps in tap_list:
        classes = [pick(taps, index) for index in indices]
        pairs = [
            jnp.concatenate([classes[2 * w % 3], classes[(2 * w + 1) % 3]], axis=0).astype(BF16) for w in range(3)
        ]
        bands.append(jnp.concatenate([pairs[w % 3] for w in range(8)], axis=0) * near_ref[...])
    return bands


def dot(a, b):
    return jnp.dot(a, b, preferred_element_type=F32)


def dot_t(a, b):
    return lax.dot_general(a, b, (((0,), (0,)), ((), ())), preferred_element_type=F32)


def staged(count, lags, enter, first, second, leave):
    held = [dict() for _ in range(3)]
    for turn in range(count + max(lags)):
        for stage in range(4):
            j = turn - lags[stage]
            if not 0 <= j < count:
                continue
            if stage == 0:
                held[0][j] = enter(j)
            elif stage == 1:
                held[1][j] = first(*held[0].pop(j))
            elif stage == 2:
                held[2][j] = second(*held[1].pop(j))
            else:
                leave(j, held[2].pop(j))


def mask_rows(mask_row):
    side = mask_row.shape[1]
    first = lax.broadcasted_iota(jnp.int32, (16, side), 0) == 0
    return jnp.where(first, jnp.broadcast_to(mask_row, (16, side)), 0.0).astype(BF16)


def halves_of(first, second):
    side = first.shape[1]
    left = lax.broadcasted_iota(jnp.int32, first.shape, 1) < side // 2
    low = jnp.where(left, first, pltpu.roll(second, side // 2, 1))
    high = jnp.where(left, pltpu.roll(first, side // 2, 1), second)
    return low, high


def sums_kernel(tiles, packed, step_blocks, affine_ref, target_ref, weight_ref, coef_ref, rows_ref, near_ref, mask_ref, block_ref, *rest):
    outs = rest[:-4]
    acc, rows_sc, cols_sc, den_sc = rest[-4:]
    step = pl.program_id(0)
    side = 128

    @pl.when(step == 0)
    def _():
        acc[...] = jnp.zeros_like(acc)
        rows_sc[...] = jnp.zeros_like(rows_sc)

    def body(group, carry):
        work = []
        for u in range(GROUP1):
            j = group * GROUP1 + u
            b = step * step_blocks + j
            mask_row = mask_ref[pl.ds(j, 1), :].astype(F32)
            masked = block_ref[j] * mask_row.astype(BF16)
            for k in range(2):
                (tap_y,), whole_y = taps_of(affine_ref[0, k, 1, b], affine_ref[0, k, 3, b], coef_ref, False)
                (tap_x,), whole_x = taps_of(affine_ref[0, k, 0, b], affine_ref[0, k, 2, b], coef_ref, False)
                work.append([b, k, mask_row, masked, tap_y, whole_y, tap_x, whole_x])
        zero = jnp.zeros((side, side), BF16)

        def corner(a, c):
            return jnp.concatenate([jnp.concatenate([a, zero], axis=1), jnp.concatenate([zero, c], axis=1)], axis=0)

        duos = [(work[4 * g + k], work[4 * g + 2 + k]) for g in range(GROUP1 // 2) for k in range(2)]
        passes = []
        for one, two in duos:
            (ly_a,) = spread([one[4]], one[5], rows_ref, near_ref)
            (ly_b,) = spread([two[4]], two[5], rows_ref, near_ref)
            both = dot_t(jnp.concatenate([ly_a, ly_b], axis=0), corner(one[3], two[3]))
            passes.append(both.astype(BF16))
        warps = {}
        for (one, two), row_pass in zip(duos, passes):
            (lx_a,) = spread([one[6]], one[7], rows_ref, near_ref)
            (lx_b,) = spread([two[6]], two[7], rows_ref, near_ref)
            extra = jnp.concatenate([mask_rows(one[2]), mask_rows(two[2])], axis=1)
            both = dot(jnp.concatenate([row_pass, extra], axis=0), corner(lx_a, lx_b))
            warps[id(one)], warps[id(two)] = both[:, :side], both[:, side:]
        warps = [warps[id(item)] for item in work]
        for (b, k, mask_row, masked, tap_y, whole_y, tap_x, whole_x), both in zip(work, warps):
            tile = target_ref[0, 0, b]
            weight = weight_ref[0, b]
            sent = (weight * both[:side]).astype(BF16).astype(F32)
            acc[k, tile] = acc[k, tile] + sent
            at = whole_y + lax.broadcasted_iota(jnp.int32, (8, side), 0) - 3
            used = jnp.where((at >= 0) & (at < side), tap_y.astype(BF16).astype(F32), 0.0)
            rows_sum = jnp.sum(used, axis=0, keepdims=True)
            rows_sc[k, tile, pl.ds(b, 1), :] = (weight * rows_sum).astype(BF16).astype(F32)
            cols_sc[k, pl.ds(b, 1), :] = both[side : side + 1].astype(BF16).astype(F32)
        return carry

    lax.fori_loop(0, step_blocks // GROUP1, body, 0)

    @pl.when(step == pl.num_programs(0) - 1)
    def _():
        for k in range(2):
            cols = cols_sc[k]
            cols = jnp.concatenate([jnp.maximum(cols, 0.0), jnp.maximum(-cols, 0.0)], axis=0).astype(BF16)

            def one(t, carry, k=k, cols=cols):
                rows = rows_sc[k, t]
                rows = jnp.concatenate([jnp.maximum(rows, 0.0), jnp.maximum(-rows, 0.0)], axis=0).astype(BF16)
                den_sc[k, t] = dot_t(rows, cols)
                return carry

            lax.fori_loop(0, tiles, one, 0, unroll=tiles if packed else 1)
        if packed:
            keep_ref, send_ref = outs
            low_end = lax.axis_index("exp") == 0
            for dz in range(tiles):
                tile = lax.rem(lax.axis_index("tx") + dz, tiles)
                for which, source in enumerate((acc, den_sc)):
                    low, high = halves_of(source[0, tile], source[1, tile])
                    keep_ref[dz, which] = jnp.where(low_end, low, high)
                    send_ref[dz, which] = jnp.where(low_end, high, low).astype(BF16)
        else:

            def whole(t, carry):
                for k in range(2):
                    outs[0][t, 0, k] = acc[k, t]
                    outs[0][t, 1, k] = den_sc[k, t]
                return carry

            lax.fori_loop(0, tiles, whole, 0)


def vmem():
    return pl.BlockSpec(memory_space=pltpu.VMEM)


def scalars(array):
    rank = array.ndim
    return pl.BlockSpec(array.shape, lambda i: (0,) * rank, memory_space=pltpu.SMEM)


def smem():
    return pl.BlockSpec(memory_space=pltpu.SMEM)


def tile_sums(affine, target, weights, coef, masks, blocks, tiles, packed):
    count, side = blocks.shape[0], blocks.shape[1]
    step_blocks = GROUP1
    if packed:
        shapes = [((tiles, 2, side, side), F32), ((tiles, 2, side, side), BF16)]
    else:
        shapes = [((tiles, 2, 2, side, side), F32)]
    return pl.pallas_call(
        functools.partial(sums_kernel, tiles, packed, step_blocks),
        grid=(count // step_blocks,),
        out_shape=[jax.ShapeDtypeStruct(*shape) for shape in shapes],
        in_specs=[
            scalars(affine),
            scalars(target),
            scalars(weights),
            *[pl.BlockSpec(c.shape, lambda i, rank=c.ndim: (0,) * rank) for c in coef],
            pl.BlockSpec((step_blocks, side), lambda i: (i, 0)),
            pl.BlockSpec((step_blocks, side, side), lambda i: (i, 0, 0)),
        ],
        out_specs=[pl.BlockSpec(shape, lambda i, rank=len(shape): (0,) * rank) for shape, _ in shapes],
        scratch_shapes=[
            pltpu.VMEM((2, tiles, side, side), F32),
            pltpu.VMEM((2, tiles, count, side), F32),
            pltpu.VMEM((2, count, side), F32),
            pltpu.VMEM((2, tiles, side, side), F32),
        ],
        compiler_params=pltpu.CompilerParams(vmem_limit_bytes=VMEM_BYTES),
        cost_estimate=pl.CostEstimate(flops=int(8e9), bytes_accessed=int(3e6), transcendentals=0),
        name="tile_sums",
    )(affine, target, weights, *coef, masks, blocks)


def pair_kernel(keep_ref, got_ref, after_ref, *outs):
    del after_ref
    for dz, out in enumerate(outs):
        for which in range(2):
            total = keep_ref[dz, which] + got_ref[dz, which].astype(F32)
            out[which] = total.astype(out.dtype)


def pair(keep, got, after):
    tiles, _, side, _ = keep.shape
    return pl.pallas_call(
        pair_kernel,
        out_shape=[jax.ShapeDtypeStruct((2, side, side), BF16 if dz else F32) for dz in range(tiles)],
        in_specs=[vmem(), vmem(), smem()],
        out_specs=[vmem()] * tiles,
        compiler_params=pltpu.CompilerParams(vmem_limit_bytes=TINY_BYTES),
        name="pair",
    )(keep, got, after)


def moments(product_x, product_y):
    side = product_x.shape[0]
    centre = (side - 1) / 2.0
    sum_x = product_x[side - 8 : side]
    sum_y = product_y[side - 8 : side]
    later = sum_y
    for v in range(side // 8 - 2, -1, -1):
        sum_x = sum_x + product_x[8 * v : 8 * v + 8]
        sum_y = sum_y + product_y[8 * v : 8 * v + 8]
        if v:
            later = later + sum_y
    sub = lax.broadcasted_iota(jnp.int32, (8, side), 0).astype(F32) - centre
    lane = lax.broadcasted_iota(jnp.int32, (1, side), 1).astype(F32) - centre
    tilted_y = 8.0 * later + sub * sum_y
    first = jnp.sum(sum_x, axis=0, keepdims=True)
    second = jnp.sum(sum_y, axis=0, keepdims=True)
    fourth = jnp.sum(tilted_y, axis=0, keepdims=True)
    return [first, second, first * lane * (1.0 / side), fourth * (1.0 / side)]


def slopes_kernel(step_blocks, start, affine_ref, coef_ref, rows_ref, near_ref, mask_ref, block_ref, *rest):
    slope_ref, part_ref, token_ref = rest[-3:]
    token_ref[0] = 0
    step = pl.program_id(0) + start
    side = 128

    ones = jnp.ones((side, side), BF16)

    def enter(j):
        b = step * step_blocks + j
        mask_row = mask_ref[pl.ds(b, 1), :].astype(F32)
        masked = block_ref[j] * mask_row.astype(BF16)
        taps = []
        for k in range(2):
            taps.append(taps_of(affine_ref[0, k, 0, b], affine_ref[0, k, 2, b], coef_ref, True))
            taps.append(taps_of(affine_ref[0, k, 1, b], affine_ref[0, k, 3, b], coef_ref, True))
        return masked, mask_rows(mask_row), taps

    def first(masked, extra, taps):
        x0, x1 = spread(*taps[0], rows_ref, near_ref), spread(*taps[2], rows_ref, near_ref)
        col_both = dot(jnp.concatenate([masked, extra], axis=0), jnp.concatenate([x0[0], x1[0]], axis=1))
        y0, y1 = spread(*taps[1], rows_ref, near_ref), spread(*taps[3], rows_ref, near_ref)
        with_ones = jnp.concatenate([masked, ones], axis=1)
        rights = [jnp.concatenate(x0, axis=1), jnp.concatenate(x1, axis=1)]
        return col_both, [dot_t(y0[0], with_ones), dot_t(y1[0], with_ones)], rights, [y0[1], y1[1]]

    def second(col_both, rows, rights, downs):
        found = []
        for k in range(2):
            row_pass = rows[k][:, :side].astype(BF16)
            col_pass = col_both[:side, k * side : (k + 1) * side].astype(BF16)
            cols_sum = col_both[side : side + 1, k * side : (k + 1) * side]
            found.append((dot(row_pass, rights[k]), dot_t(downs[k], col_pass), rows[k][:, side:], cols_sum))
        return found

    def leave(j, found):
        for k, (both, slope_y, rows_sum, cols_sum) in enumerate(found):
            weight_map = jnp.maximum(rows_sum * cols_sum, 0.0)
            value_x = weight_map * both[:, side:]
            value_y = weight_map * slope_y
            slope_ref[j, 2 * k] = value_x.astype(SLOPE)
            slope_ref[j, 2 * k + 1] = value_y.astype(SLOPE)
            warped = both[:, :side]
            for m, row in enumerate(moments(warped * value_x, warped * value_y)):
                part_ref[j, 4 * k + m : 4 * k + m + 1, :] = row

    staged(step_blocks, LAG2, enter, first, second, leave)


def slopes_of(affine, coef, masks, blocks, first, size):
    side = blocks.shape[1]
    step_blocks = STEP2
    start = first // step_blocks
    return pl.pallas_call(
        functools.partial(slopes_kernel, step_blocks, start),
        grid=(size // step_blocks,),
        out_shape=[
            jax.ShapeDtypeStruct((size, 4, side, side), SLOPE),
            jax.ShapeDtypeStruct((size, 8, side), F32),
            jax.ShapeDtypeStruct((1,), jnp.int32),
        ],
        in_specs=[
            scalars(affine),
            *[pl.BlockSpec(c.shape, lambda i, rank=c.ndim: (0,) * rank) for c in coef],
            pl.BlockSpec(masks.shape, lambda i: (0, 0)),
            pl.BlockSpec((step_blocks, side, side), lambda i: (i + start, 0, 0)),
        ],
        out_specs=[
            pl.BlockSpec((step_blocks, 4, side, side), lambda i: (i, 0, 0, 0)),
            pl.BlockSpec((step_blocks, 8, side), lambda i: (i, 0, 0)),
            smem(),
        ],
        compiler_params=pltpu.CompilerParams(vmem_limit_bytes=SMALL_BYTES),
        cost_estimate=pl.CostEstimate(flops=int(1.5e8) * size, bytes_accessed=int(3e5) * size, transcendentals=0),
        name="slopes",
    )(affine, *coef, masks, blocks)


def coadd_kernel(after_ref, *refs):
    del after_ref
    parts, (piece_ref, short_ref, edge_ref) = refs[:-3], refs[-3:]
    num, den = parts[0][0], parts[0][1]
    for part in parts[1:]:
        num = num + part[0].astype(F32)
        den = den + part[1].astype(F32)
    side = num.shape[1]
    left = lax.broadcasted_iota(jnp.int32, num.shape, 1) < side // 2
    first = num / (1.0 + den)
    piece = (num + jnp.where(left, 0.0, pltpu.roll(first, side // 2, 1))) / (1.0 + den)
    piece_ref[...] = piece
    short_ref[...] = piece.astype(BF16)
    flipped = jnp.transpose(piece)
    half = side // 2
    outer = jnp.concatenate([flipped[0:8], flipped[half : half + 8]], axis=0)
    inner = jnp.concatenate([flipped[half - 8 : half], flipped[side - 8 : side]], axis=0)
    edge_ref[...] = jnp.where(lax.axis_index("exp") == 0, outer, inner).astype(BF16)


def coadd_of(after, parts):
    side = parts[0].shape[2]
    return pl.pallas_call(
        coadd_kernel,
        out_shape=[
            jax.ShapeDtypeStruct((side, side), F32),
            jax.ShapeDtypeStruct((side, side), BF16),
            jax.ShapeDtypeStruct((16, side), BF16),
        ],
        in_specs=[smem()] + [vmem()] * len(parts),
        out_specs=[vmem()] * 3,
        compiler_params=pltpu.CompilerParams(vmem_limit_bytes=TINY_BYTES),
        name="coadd",
    )(after, *parts)


def band_of(values, diagonal):
    total = jnp.zeros(diagonal.shape, F32)
    for q, value in enumerate(values):
        total = jnp.where(diagonal == q, value, total)
    high = total.astype(BF16)
    return jnp.concatenate([high, (total - high.astype(F32)).astype(BF16)], axis=1)


def bands_kernel(psf_ref, after_ref, inner_ref, outer_ref, rows_ref, token_ref):
    token_ref[0] = after_ref[0]
    side = inner_ref.shape[1]
    along = lax.broadcasted_iota(jnp.int32, (side, side), 0)
    across = lax.broadcasted_iota(jnp.int32, (side, side), 1)
    edge = along[:16]
    edge = jnp.where(edge < 8, edge - 8, edge + side - 8)
    for k in range(2):
        taps = [psf_ref[k, 1, q] for q in range(TAPS)]
        inner_ref[k] = band_of(taps, along - across + RAD)
        outer_ref[k] = band_of(taps, edge - across[:16] + RAD)
        wide = (side, side + 32)
        below = lax.broadcasted_iota(jnp.int32, wide, 1) - lax.broadcasted_iota(jnp.int32, wide, 0) - 16 + RAD
        total = jnp.zeros(wide, F32)
        for q in range(TAPS):
            total = jnp.where(below == q, psf_ref[k, 0, q], total)
        high = total.astype(BF16)
        rows_ref[k, 0:side, :] = high
        rows_ref[k, side : 2 * side, :] = (total - high.astype(F32)).astype(BF16)


def bands_of(psf, after, side=128):
    return pl.pallas_call(
        bands_kernel,
        out_shape=[jax.ShapeDtypeStruct((2, rows, 2 * side), BF16) for rows in (side, 16)]
        + [jax.ShapeDtypeStruct((2, 2 * side, side + 32), BF16), jax.ShapeDtypeStruct((1,), jnp.int32)],
        in_specs=[smem(), smem()],
        out_specs=[vmem(), vmem(), vmem(), smem()],
        compiler_params=pltpu.CompilerParams(vmem_limit_bytes=TINY_BYTES),
        name="bands",
    )(psf, after)


def smoothed(tile, edges, inner, outer):
    side = tile.shape[1]
    high = tile.astype(BF16)
    low = (tile - high.astype(F32)).astype(BF16)
    both = dot(high, inner) + dot_t(edges, outer)
    return both[:, :side] + both[:, side:] + dot(low, inner[:, :side])


def join_kernel(inner_ref, outer_ref, own_ref, other_ref, edge_ref, far_ref, after_ref, sky_ref):
    del after_ref
    here = lax.axis_index("exp") == 0
    own, other = own_ref[...], other_ref[...].astype(F32)
    tiles = halves_of(jnp.where(here, own, other), jnp.where(here, other, own))
    edge, far = edge_ref[...].astype(F32), far_ref[...].astype(F32)
    left, right = jnp.where(here, far, edge), jnp.where(here, edge, far)
    column = lax.axis_index("ty")
    left = jnp.where(column > 0, left, 0.0)
    right = jnp.where(column < lax.axis_size("ty") - 1, right, 0.0)
    for k in range(2):
        at = slice(8 * k, 8 * k + 8)
        edges = jnp.concatenate([left[at], right[at]], axis=0).astype(BF16)
        sky_ref[k] = smoothed(tiles[k], edges, inner_ref[k], outer_ref[k]).astype(BF16)


def join(bands, own, other, edge, far, after):
    side = own.shape[1]
    return pl.pallas_call(
        join_kernel,
        out_shape=jax.ShapeDtypeStruct((2, side, side), BF16),
        in_specs=[vmem()] * 6 + [smem()],
        out_specs=vmem(),
        compiler_params=pltpu.CompilerParams(vmem_limit_bytes=TINY_BYTES),
        name="join",
    )(*bands, own, other, edge, far, after)


def tile_kernel(own_ref, other_ref, tile_ref):
    here = lax.axis_index("exp") == 0
    own, other = own_ref[...], other_ref[...]
    tile_ref[...] = halves_of(jnp.where(here, own, other), jnp.where(here, other, own))[1]


def tile_of(own, other):
    return pl.pallas_call(
        tile_kernel,
        out_shape=jax.ShapeDtypeStruct(own.shape, F32),
        in_specs=[vmem(), vmem()],
        out_specs=vmem(),
        compiler_params=pltpu.CompilerParams(vmem_limit_bytes=TINY_BYTES),
        name="tile",
    )(own, other)


def whole_kernel(inner_ref, outer_ref, tile_ref, edge_ref, sky_ref):
    for k in range(2):
        sky_ref[k] = smoothed(tile_ref[k], edge_ref[k], inner_ref[k], outer_ref[k]).astype(BF16)


def whole_sky(bands, tiles, edges):
    return pl.pallas_call(
        whole_kernel,
        out_shape=jax.ShapeDtypeStruct(tiles.shape, BF16),
        in_specs=[vmem()] * 4,
        out_specs=vmem(),
        compiler_params=pltpu.CompilerParams(vmem_limit_bytes=TINY_BYTES),
        name="whole_sky",
    )(*bands, tiles, edges)


def gradient_kernel(tiles, target_ref, band_ref, *rest):
    skies = rest[:tiles]
    chunk_refs, (out_ref, smooth, model) = rest[tiles:-3], rest[-3:]
    side = 128
    for k in range(2):
        smooth[k, 0:16, :] = jnp.zeros((16, side), BF16)
        smooth[k, 16 + tiles * side : 32 + tiles * side, :] = jnp.zeros((16, side), BF16)
        for turn in range(tiles):
            tile = lax.rem(lax.axis_index("tx") + tiles - turn, tiles)
            smooth[k, pl.ds(pl.multiple_of(16 + tile * side, 16), side), :] = skies[turn][k]
        for tile in range(tiles):
            both = dot(band_ref[k], smooth[k, tile * side : (tile + 1) * side + 32, :])
            total = both[:side] + both[side:]
            model[k, tile * side : (tile + 1) * side, :] = total.astype(BF16).astype(F32)

    count = out_ref.shape[3]
    lane = lax.broadcasted_iota(jnp.int32, (8, count), 1)
    gathered = jnp.zeros((8, count), F32)
    first = 0
    for slope_ref, part_ref in zip(chunk_refs[::2], chunk_refs[1::2]):

        def body(group, gathered, first=first, slope_ref=slope_ref, part_ref=part_ref):
            found = []
            for u in range(GROUP3):
                j = group * GROUP3 + u
                start = pl.multiple_of(target_ref[0, 0, first + j] * side, side)
                rows = []
                for k in range(2):
                    cutout = model[k, pl.ds(start, side), :]
                    slope_x, slope_y = slope_ref[j, 2 * k].astype(F32), slope_ref[j, 2 * k + 1].astype(F32)
                    rows += moments(cutout * slope_x, cutout * slope_y)
                found.append((j, rows))
            for j, rows in found:
                total = jnp.sum(part_ref[j] - jnp.concatenate(rows, axis=0), axis=1, keepdims=True) * (1.0 / side)
                gathered = jnp.where(lane == first + j, total, gathered)
            return gathered

        gathered = lax.fori_loop(0, slope_ref.shape[0] // GROUP3, body, gathered, unroll=True)
        first += slope_ref.shape[0]
    out_ref[0, 0] = gathered[0:4]
    out_ref[0, 1] = gathered[4:8]


def gradients_of(target, row_bands, skies, chunks):
    side = skies[0].shape[1]
    tiles, count = len(skies), target.shape[2]
    arrays = [array for pair_of in chunks for array in pair_of]
    return pl.pallas_call(
        functools.partial(gradient_kernel, tiles),
        out_shape=jax.ShapeDtypeStruct((1, 2, 4, count), F32),
        in_specs=[smem()] + [vmem()] * (1 + tiles + len(arrays)),
        out_specs=vmem(),
        scratch_shapes=[
            pltpu.VMEM((2, tiles * side + 32, side), BF16),
            pltpu.VMEM((2, tiles * side, side), F32),
        ],
        compiler_params=pltpu.CompilerParams(vmem_limit_bytes=SMALL_BYTES),
        cost_estimate=pl.CostEstimate(flops=int(4e9), bytes_accessed=int(20e6), transcendentals=0),
        name="gradients",
    )(target, row_bands, *skies, *arrays)


def swap(cells):
    return lax.ppermute(cells, "exp", [(0, 1), (1, 0)])


def turned(cells, dz, tiles):
    return lax.ppermute(cells, "tx", [(z, (z + dz) % tiles) for z in range(tiles)])


def to_sides(edge, columns, flip):
    perm = [(y, flip * columns + (y - 1) % columns) for y in range(columns)]
    perm += [(columns + y, (1 - flip) * columns + (y + 1) % columns) for y in range(columns)]
    return lax.ppermute(edge, ("exp", "ty"), perm)


def local(exposures, block_tile, affine, col_mask, block_weight, psf):
    blocks = exposures[0]
    count, side = blocks.shape[0], blocks.shape[1]
    tiles, halves, columns = lax.axis_size("tx"), lax.axis_size("exp"), lax.axis_size("ty")
    rows, near = windows()
    coef = (jnp.asarray(series()), jnp.asarray(rows), jnp.asarray(near, BF16))
    affine = affine.transpose(0, 2, 3, 1)
    block_tile = block_tile.transpose(0, 2, 1)
    masks = col_mask[0]
    small = halves == 2 and tiles <= 4
    sums = tile_sums(affine, block_tile, block_weight, coef, masks, blocks, tiles, small)
    chunks, tokens, first = [], [], 0
    scale = count // sum(CHUNKS)
    for size in CHUNKS:
        *found, token = slopes_of(affine, coef, masks, blocks, first, size * scale)
        chunks.append(found)
        tokens.append(token)
        first += size * scale
    if small:
        keep, send = sums
        *bands, row_bands, token = bands_of(psf, tokens[0])
        totals = pair(keep, swap(send), token)
        got = [totals[0]] + [turned(totals[dz], dz, tiles) for dz in range(1, tiles)]
        piece, short, edge = coadd_of(tokens[1], got)
        other = swap(short)
        near, far = to_sides(edge, columns, 0), to_sides(edge, columns, 1)
        coadd_tile = tile_of(piece, swap(piece))
        sky = join(bands, piece, other, near, far, tokens[-2])
        skies = [sky] + [turned(sky, dz, tiles) for dz in range(1, tiles)]
    else:
        me = lax.axis_index("tx")
        summed = lax.psum_scatter(sums[0], "tx", scatter_dimension=0, tiled=True)
        (num, den) = lax.psum(summed[0], "exp")
        one = num[0] / (1.0 + den[0])
        coadd_tile = (num[1] + one) / (1.0 + den[1])
        both = jnp.stack([one, coadd_tile])
        flipped = jnp.swapaxes(both, 1, 2).astype(BF16)
        left = lax.ppermute(flipped[:, side - 8 :], "ty", [(y, y + 1) for y in range(columns - 1)])
        right = lax.ppermute(flipped[:, :8], "ty", [(y + 1, y) for y in range(columns - 1)])
        *bands, row_bands, _ = bands_of(psf, tokens[0])
        sky = whole_sky(bands, both, jnp.concatenate([left, right], axis=1))
        gathered = lax.all_gather(sky, "tx", axis=0)
        skies = [lax.dynamic_index_in_dim(gathered, (me + tiles - turn) % tiles, 0, False) for turn in range(tiles)]
    gradients = gradients_of(block_tile, row_bands, skies, chunks)
    return gradients.transpose(0, 3, 1, 2), coadd_tile


def solution(mesh):
    placed = (
        P("ty", ("exp", "tx"), None, None),
        P("ty", ("exp", "tx"), None),
        P("ty", ("exp", "tx"), None, None),
        P("ty", ("exp", "tx"), None),
        P("ty", ("exp", "tx")),
        P(),
    )
    return jax.shard_map(
        local,
        mesh=mesh,
        in_specs=placed,
        out_specs=(P("ty", ("exp", "tx"), None, None), P("tx", "ty")),
        check_vma=False,
    )
```
